32 devices in a mesh: seq: 8 (over y, x, core), dp: 4 (over z).
Axes of the slice: x: 2, y: 2, z: 4, core: 2. Of those that a mesh axis runs over, the one named last changes fastest.
Arguments:
- bases: int32 [4, 1024], P('dp', 'seq'), may hold values from 0 to 3
- lengths: int32 [4, 8], P('dp', 'seq'), may hold values from 64 to 128, as said below
- cotangent: bfloat16 [4, 1024, 768], P('dp', 'seq'), may hold values from -6 to 6
- first_conv_taps: bfloat16 [3, 768, 384], P(None, 'seq'), may hold values from -0.125 to 0.125
- first_projection: bfloat16 [384, 768], P('seq'), may hold values from -0.3125 to 0.3125
- second_conv_taps: bfloat16 [3, 768, 384], P(None, 'seq'), may hold values from -0.125 to 0.125
- second_projection: bfloat16 [384, 768], P('seq'), may hold values from -0.3125 to 0.3125
- embed: float32 [4, 768], replicated, may hold values from -6 to 6
Outputs:
- saliency: float32 [4, 4, 1024], P('dp', None, 'seq')
- grad_proj: float32 [589824], P(('seq', 'dp'))
The draws below stay inside these ranges and needn't reach their ends.
Inputs may be any that keep to these rules, and one draw needn't show every extreme that they name: `lengths`: every block holds between 64 and 128 live rows; in each window one block holds exactly 128 and another exactly 64.
All inputs are finite; a program needn't handle non-finite values.
Results may differ from the reference program's by a relative error of at most 0.0042.
Values may be sent and summed in bfloat16 or wider, within the bound.
No kernel may reach another device: no remote copies, remote signals or barrier semaphores. Data moves between devices by JAX's collectives and lax.ppermute only.
A program may use at most 64 MiB of HBM per device.

```python
import math
import jax
import jax.numpy as jnp
from jax import lax

C = 768
B = 384
CAP = 128
FIRST_DILATION = 16
SECOND_DILATION = 64
WINDOW = 1024
N_SEQ = 8
N_DP = 4


def draw_lengths(key, part):
    key_vals, key_top, key_shift = jax.random.split(key, 3)
    values = jax.random.randint(key_vals, (N_DP, N_SEQ), CAP // 2, CAP + 1)
    top_idx = jax.random.randint(key_top, (N_DP,), 0, N_SEQ)
    shift_by = jax.random.randint(key_shift, (N_DP,), 1, N_SEQ)
    low_idx = (top_idx + shift_by) % N_SEQ
    columns = jnp.arange(N_SEQ)[None, :]
    values = jnp.where(columns == top_idx[:, None], CAP, values)
    values = jnp.where(columns == low_idx[:, None], CAP // 2, values)
    return values.astype(jnp.int32)


def set_ends(result, stream_key, low, top_value):
    longest = result.shape.index(max(result.shape))
    spots = []
    for shift in (0, 1):
        where = [jax.random.randint(jax.random.fold_in(stream_key, axis), (), 0, length) for axis, length in enumerate(result.shape)]
        where[longest] = (where[longest] + shift) % result.shape[longest]
        spots.append(tuple(where))
    return result.at[spots[0]].set(low).at[spots[1]].set(top_value)


def levels(stream_key, shape, pieces, smallest, top_value):
    level = 1.0
    for dim, parts in pieces:
        steps = jax.random.uniform(jax.random.fold_in(jax.random.fold_in(stream_key, 6), dim), (parts,), jnp.float32, smallest / len(pieces), top_value / len(pieces))
        level = level * jnp.repeat(jnp.exp(steps), shape[dim] // parts).reshape((-1,) + (1,) * (len(shape) - 1 - dim))
    return level


def scatter_about(stream_key, dims, width, bound, cuts=(), kind=jnp.bfloat16):
    entries = width * jax.random.normal(stream_key, dims, jnp.float32)
    if cuts:
        entries = entries * levels(stream_key, dims, cuts, -0.22, 0.18)
    return jnp.clip(entries, -bound, bound).astype(kind)


def setup_inputs(seed: int = 0) -> dict:
    arg_keys = jax.random.split(jax.random.key(seed), 9)
    bases = set_ends(jax.random.randint(arg_keys[0], (N_DP, WINDOW), 0, 4), jax.random.fold_in(arg_keys[0], 1), 0, 3).astype(jnp.int32)
    lengths = draw_lengths(jax.random.fold_in(arg_keys[8], 71), 0)
    cotangent = scatter_about(arg_keys[2], (N_DP, WINDOW, C), 1.0, 6.0, ((0, 4), (1, 8)))
    first_conv_taps = scatter_about(arg_keys[3], (3, C, B), (3 * C) ** -0.5, 0.125, ((1, 8),))
    first_projection = scatter_about(arg_keys[4], (B, C), B ** -0.5, 0.3125, ((0, 8),))
    second_conv_taps = scatter_about(arg_keys[5], (3, C, B), (3 * C) ** -0.5, 0.125, ((1, 8),))
    second_projection = scatter_about(arg_keys[6], (B, C), B ** -0.5, 0.3125, ((0, 8),))
    embed = scatter_about(arg_keys[7], (4, C), 1.0, 6.0, (), jnp.float32)
    return dict(bases=bases, lengths=lengths, cotangent=cotangent, first_conv_taps=first_conv_taps, first_projection=first_projection, second_conv_taps=second_conv_taps, second_projection=second_projection, embed=embed)


SQRT_HALF = 0.7071067811865476
INV_SQRT_TWO_PI = 0.3989422804014327

def gelu_value(values):
    return 0.5 * values * (1.0 + lax.erf(values * SQRT_HALF))

def gelu_slope(values):
    return 0.5 * (1.0 + lax.erf(values * SQRT_HALF)) + values * jnp.exp(-0.5 * values * values) * INV_SQRT_TWO_PI

def tap_sum(values, taps, dilation):
    total_rows = values.shape[0]
    padded = jnp.pad(values, ((dilation, dilation), (0, 0)))
    summed = jnp.dot(padded[:total_rows], taps[0], preferred_element_type=jnp.float32)
    summed = summed + jnp.dot(padded[dilation:dilation + total_rows], taps[1], preferred_element_type=jnp.float32)
    summed = summed + jnp.dot(padded[2 * dilation:2 * dilation + total_rows], taps[2], preferred_element_type=jnp.float32)
    return summed

def reverse_live(values, live_count):
    return jnp.roll(jnp.flip(values, 0), live_count - values.shape[0], axis=0)

def run_pass(start_rows, cot_half, live, residual_blocks):
    stream = start_rows
    saved = []
    for conv_taps, proj_matrix, dilation in residual_blocks:
        active = gelu_value(stream).astype(jnp.bfloat16)
        before = tap_sum(active, conv_taps, dilation) * live
        middle = gelu_value(before).astype(jnp.bfloat16)
        saved.append((stream, before, middle))
        stream = stream + jnp.dot(middle, proj_matrix, preferred_element_type=jnp.float32)
    grad_rows = cot_half
    proj_grads = [None, None]
    for block_idx in (1, 0):
        conv_taps, proj_matrix, dilation = residual_blocks[block_idx]
        stream_in, before, middle = saved[block_idx]
        grad_low = grad_rows.astype(jnp.bfloat16)
        proj_grads[block_idx] = jnp.dot(middle.T, grad_low, preferred_element_type=jnp.float32)
        back_mid = jnp.dot(grad_low, proj_matrix.T, preferred_element_type=jnp.float32)
        grad_before = (back_mid * gelu_slope(before) * live).astype(jnp.bfloat16)
        back_taps = jnp.stack([conv_taps[2].T, conv_taps[1].T, conv_taps[0].T])
        grad_active = tap_sum(grad_before, back_taps, dilation)
        grad_rows = grad_rows + grad_active * gelu_slope(stream_in) * live
    return (grad_rows, proj_grads)

def reference(bases, lengths, cotangent, first_conv_taps, first_projection, second_conv_taps, second_projection, embed):
    residual_blocks = [(first_conv_taps, first_projection, FIRST_DILATION), (second_conv_taps, second_projection, SECOND_DILATION)]
    slot_ids = jnp.arange(WINDOW, dtype=jnp.int32)
    device_of = slot_ids // CAP
    row_of = slot_ids % CAP
    grad_first = jnp.zeros((B, C), jnp.float32)
    grad_second = jnp.zeros((B, C), jnp.float32)
    saliency_list = []
    for window_idx in range(N_DP):
        counts = lengths[window_idx]
        starts = (jnp.cumsum(counts) - counts).astype(jnp.int32)
        live_slot = row_of < counts[device_of]
        target = jnp.where(live_slot, starts[device_of] + row_of, WINDOW).astype(jnp.int32)
        live_count = jnp.sum(counts).astype(jnp.int32)
        packed_base = jnp.zeros((WINDOW,), jnp.int32).at[target].set(bases[window_idx], mode='drop')
        packed_cot = jnp.zeros((WINDOW, C), jnp.float32).at[target].set(cotangent[window_idx].astype(jnp.float32), mode='drop')
        live = (slot_ids < live_count).astype(jnp.float32)[:, None]
        comp_base = (3 - reverse_live(packed_base, live_count)) * (slot_ids < live_count).astype(jnp.int32)
        comp_cot = reverse_live(packed_cot, live_count) * live
        grad_fwd, grads_fwd = run_pass(embed[packed_base] * live, 0.5 * packed_cot * live, live, residual_blocks)
        grad_rev, grads_rev = run_pass(embed[comp_base] * live, 0.5 * comp_cot, live, residual_blocks)
        sal_fwd = jnp.dot(grad_fwd, embed.T, precision=lax.Precision.HIGHEST)
        sal_rev = jnp.dot(grad_rev, embed.T, precision=lax.Precision.HIGHEST)
        combined = (sal_fwd + reverse_live(sal_rev, live_count)[:, ::-1]) * live / math.sqrt(C)
        back_idx = jnp.where(live_slot, target, 0).astype(jnp.int32)
        padded_sal = combined[back_idx] * live_slot.astype(jnp.float32)[:, None]
        saliency_list.append(padded_sal.T)
        grad_first = grad_first + grads_fwd[0] + grads_rev[0]
        grad_second = grad_second + grads_fwd[1] + grads_rev[1]
    grad_proj = jnp.concatenate([grad_first.reshape(-1), grad_second.reshape(-1)]) / math.sqrt(N_DP * WINDOW)
    return (jnp.stack(saliency_list), grad_proj)
```

```python
import functools
import math

import jax
import jax.numpy as jnp
from jax import lax
from jax.experimental import pallas as pl
from jax.experimental.pallas import tpu as pltpu
from jax.sharding import PartitionSpec as P

FIRST_DILATION = 16
SECOND_DILATION = 64
HALO = FIRST_DILATION + SECOND_DILATION
SPILL = 16
REACH = 3
TABLE = 128
SQRT_HALF = 0.7071067811865476
INV_SQRT_TWO_PI = 0.3989422804014327
F32 = jnp.float32
BF16 = jnp.bfloat16
FAR = -100000.0


def gelu_pair(v):
    half = 0.5 * (1.0 + lax.erf(v * SQRT_HALF))
    return v * half, half + v * jnp.exp(-0.5 * v * v) * INV_SQRT_TWO_PI


def split(v):
    high = v.astype(BF16)
    return high, (v - high.astype(F32)).astype(BF16)


def mm(a, b):
    return lax.dot_general(a, b, (((1,), (0,)), ((), ())), preferred_element_type=F32)


def mm_nt(a, b):
    return lax.dot_general(a, b, (((1,), (1,)), ((), ())), preferred_element_type=F32)


def mm_tn(a, b):
    return lax.dot_general(a, b, (((0,), (0,)), ((), ())), preferred_element_type=F32)


def iota(shape, dim):
    return lax.broadcasted_iota(jnp.int32, shape, dim)


def spread(rows, index):
    out = jnp.broadcast_to(rows[0:1], (index.shape[0], rows.shape[1]))
    for q in range(1, 4):
        out = jnp.where(index == q, rows[q : q + 1], out)
    return out


def call(body, out_shapes, args, scratch=(), limit=24, cost=None):
    in_specs = [
        pl.BlockSpec(memory_space=pltpu.SMEM if a.dtype == jnp.int32 and a.ndim == 1 else pltpu.VMEM)
        for a in args
    ]
    return pl.pallas_call(
        body,
        out_shape=[jax.ShapeDtypeStruct(s, d) for s, d in out_shapes],
        in_specs=in_specs,
        out_specs=[pl.BlockSpec(memory_space=pltpu.VMEM)] * len(out_shapes),
        scratch_shapes=list(scratch),
        compiler_params=pltpu.CompilerParams(vmem_limit_bytes=limit * 1024 * 1024),
        cost_estimate=cost,
    )(*args)


def base_tables(embed_ref, pick, conv, shard):
    row = iota((16, 1), 0)
    low, high = row & 3, row >> 2
    emb = embed_ref[...]
    by_low = spread(emb, low)
    by_high = spread(emb, high)
    act = gelu_pair(by_low)[0].astype(BF16)
    prod_high, prod_low = split(gelu_pair(by_high)[1] * by_low)
    own = mm(jnp.concatenate([act, prod_high, prod_low], axis=0), pick).astype(BF16)
    first = jnp.zeros((16, conv.shape[2]), F32)
    second = []
    for k in range(3):
        res = mm(own, conv[k])
        first = jnp.where(high == k, res[0:16], first)
        second.append(res[16:32] + res[32:48])
    return first, jnp.concatenate(second, axis=0)


def prep_kernel(
    where_ref, bases_ref, cot_ref, c1_ref, p1_ref, c2_ref, p2_ref, embed_ref,
    m1_ref, m2_ref, r1_ref, r2_ref, l1_ref, l2_ref,
):
    me, count = where_ref[0], where_ref[2]
    shard = c1_ref.shape[1]
    chans = embed_ref.shape[1]
    width = c1_ref.shape[2]
    pick = (iota((chans, shard), 0) == iota((chans, shard), 1) + me * shard).astype(BF16)
    first, second = base_tables(embed_ref, pick, c1_ref, shard)
    prows = p1_ref.shape[0]
    m1_ref[0:prows] = p1_ref[...]
    f_high, f_low = split(first)
    cap = bases_ref.shape[1]
    info = jnp.concatenate(
        [
            bases_ref[...].astype(F32),
            jnp.full((1, 128), count, jnp.int32).astype(F32),
            jnp.zeros((1, chans - cap - 128), F32),
        ],
        axis=1,
    )
    tail = jnp.concatenate([f_high.astype(F32), f_low.astype(F32)], axis=1)
    tail = jnp.where(iota((16, 1), 0) == 12, info, tail)
    m1_ref[prows : prows + 16] = tail.astype(BF16)
    half = 3 * shard // 2
    flat = c2_ref[...].reshape(3 * shard, width)
    m2_ref[0:half, 0:width] = flat[0:half]
    m2_ref[0:half, width : 2 * width] = flat[half : 2 * half]
    m2_ref[half : half + prows] = p2_ref[...]
    s_high, s_low = split(second)
    m2_ref[half + prows : half + prows + 48, 0:width] = s_high
    m2_ref[half + prows : half + prows + 48, width : 2 * width] = s_low
    cot = cot_ref[...]
    take = (iota((HALO, cap), 1) == iota((HALO, cap), 0) + (count - HALO)).astype(BF16)
    last = mm(take, cot).astype(BF16)
    r1_ref[...] = last
    r2_ref[...] = last[HALO - SPILL :]
    l1_ref[...] = cot[0:HALO]
    l2_ref[...] = cot[0:SPILL]


def table_body(
    first, project, info_at, cot_ref, r1_ref, r2_ref, l1_ref, l2_ref, embed_ref,
    b1_ref, s1_ref, a2_ref, s2_ref, hot_f_ref, hot_r_ref, cx_ref,
):
    cap = cot_ref.shape[0]
    outer = HALO + SECOND_DILATION + FIRST_DILATION
    span = cap + 2 * outer
    counts = [info_at(o)[0:1, cap : cap + 128] for o in range(-REACH, REACH + 1)]
    begin = [None] * (2 * REACH + 1)
    begin[REACH] = jnp.zeros((1, 128), F32)
    for o in range(1, REACH + 1):
        begin[REACH + o] = begin[REACH + o - 1] + counts[REACH + o - 1]
        begin[REACH - o] = begin[REACH - o + 1] - counts[REACH - o]
    lane = iota((1, 128), 1).astype(F32)
    rowpos = (iota((span, 128), 0) - outer).astype(F32)
    total = jnp.zeros((span, 128), F32)
    for o in range(-REACH, REACH + 1):
        code = info_at(o)[0:1, 0:cap] + 1.0
        pos = jnp.where(lane < counts[REACH + o], begin[REACH + o] + lane, FAR)
        total = total + jnp.where(rowpos == pos, code, 0.0)
    codes = jnp.sum(total, axis=1, keepdims=True)
    d = FIRST_DILATION
    left, mid, right = codes[0 : span - 2 * d], codes[d : span - d], codes[2 * d : span]
    rows = span - 2 * d
    lanes = iota((rows, TABLE), 1).astype(F32)
    flip = lambda c: jnp.where(c == 0.0, 0.0, 5.0 - c)
    idx = jnp.where(mid == 0.0, -1.0, (mid - 1.0) * 25.0 + left * 5.0 + right)
    hot_f_ref[...] = (lanes == idx).astype(BF16)
    idx = jnp.where(mid == 0.0, -1.0, (4.0 - mid) * 25.0 + flip(right) * 5.0 + flip(left))
    hot_r_ref[...] = (lanes == idx).astype(BF16)

    entry = iota((TABLE, 1), 0)
    by25 = (entry * 1311) >> 15
    by5 = (entry * 6554) >> 15
    in_left = by5 - 5 * by25
    in_right = entry - 5 * by5
    sums = jnp.zeros((TABLE, first.shape[1]), F32)
    for q in range(4):
        sums = jnp.where(in_left == q + 1, first[q : q + 1], sums)
    sums = sums + spread(first[4:8], by25)
    after = jnp.zeros((TABLE, first.shape[1]), F32)
    for q in range(4):
        after = jnp.where(in_right == q + 1, first[8 + q : 9 + q], after)
    value, slope = gelu_pair(sums + after)
    b1 = value.astype(BF16)
    b1_ref[...] = b1
    high, low = split(slope)
    s1_ref[0:TABLE] = high
    s1_ref[TABLE : 2 * TABLE] = low
    stream = spread(embed_ref[...], by25) + mm(b1, project)
    value, slope = gelu_pair(stream)
    a2_ref[...] = value.astype(BF16)
    high, low = split(slope)
    s2_ref[0:TABLE] = high
    s2_ref[TABLE : 2 * TABLE] = low

    own_n = counts[REACH]
    before_n, after_n = counts[REACH - 1], counts[REACH + 1]
    grow = cap + 2 * HALO
    lane_h = iota((1, HALO), 1).astype(F32)
    lane_s = iota((1, SPILL), 1).astype(F32)
    row_h = (iota((grow, HALO), 0) - HALO).astype(F32)
    row_s = (iota((grow, SPILL), 0) - HALO).astype(F32)
    row_o = (iota((grow, cap), 0) - HALO).astype(F32)
    own_pos = jnp.where(lane < own_n, lane, FAR)
    acc = mm((row_o == own_pos).astype(BF16), cot_ref[...])
    pos = jnp.where(lane_h >= HALO - before_n[:, 0:HALO], lane_h - HALO, FAR)
    acc = acc + mm((row_h == pos).astype(BF16), r1_ref[...])
    pos = jnp.where(
        counts[REACH - 2][:, 0:SPILL] > 0.0, lane_s - SPILL - before_n[:, 0:SPILL], FAR
    )
    acc = acc + mm((row_s == pos).astype(BF16), r2_ref[...])
    pos = jnp.where(lane_h < after_n[:, 0:HALO], lane_h + own_n[:, 0:HALO], FAR)
    acc = acc + mm((row_h == pos).astype(BF16), l1_ref[...])
    pos = jnp.where(
        (counts[REACH + 2][:, 0:SPILL] > 0.0) & (after_n[:, 0:SPILL] < HALO),
        lane_s + own_n[:, 0:SPILL] + after_n[:, 0:SPILL],
        FAR,
    )
    acc = acc + mm((row_s == pos).astype(BF16), l2_ref[...])
    cx_ref[...] = (0.5 * acc).astype(BF16)


def table_kernel_packed(rels, where_ref, *refs):
    parts = refs[: len(rels)]
    rest = refs[len(rels) : len(rels) + 6]
    outs = refs[len(rels) + 6 :]
    p1_ref = outs[7]
    info_ref = outs[8]
    me = where_ref[0]
    shard = parts[0].shape[0] - 16
    width = parts[0].shape[1] // 2
    info_ref[...] = jnp.zeros(info_ref.shape, F32)
    first = jnp.zeros((16, width), F32)
    for rel, part in zip(rels, parts):
        peer = me ^ rel
        p1_ref[pl.ds(pl.multiple_of(peer * shard, 16), shard), :] = part[0:shard]
        tail = part[shard : shard + 16].astype(F32)
        first = first + tail[:, 0:width] + tail[:, width : 2 * width]
        info_ref[REACH + peer] = jnp.broadcast_to(tail[12:13, 0:256], (8, 256))
    table_body(
        first, p1_ref[...], lambda o: info_ref[me + (REACH + o)], *rest, *outs[:7]
    )


def table_kernel_plain(first_ref, project_ref, info_ref, *refs):
    table_body(first_ref[...], project_ref[...], lambda o: info_ref[REACH + o], *refs)


def tower_body(
    conv, p2, second, p1, count, bases_ref, cx_ref, b1_ref, s1_ref, a2_ref, s2_ref,
    hot_f_ref, hot_r_ref, embed_ref, sal_ref, put,
):
    cap = bases_ref.shape[1]
    grow = cap + 2 * HALO
    inner = cap + 2 * FIRST_DILATION
    d, D = FIRST_DILATION, SECOND_DILATION
    cx = cx_ref[...]
    a2 = a2_ref[...]
    taps = []
    for k in range(3):
        high, low = split(mm(a2, conv(k)))
        taps.append(jnp.concatenate([high, low], axis=0))
    back_mid = mm_nt(cx, p2)
    own_col = (iota((cap, 1), 0) < count).astype(F32)
    own_cx = cx[HALO : HALO + cap]
    own_gb = (own_cx.astype(F32) * own_col).astype(BF16)
    grads = []
    mids = []
    for hot_ref, order in ((hot_f_ref, (0, 1, 2)), (hot_r_ref, (2, 1, 0))):
        before = jnp.zeros((grow, a2_ref.shape[1] // 2), F32)
        for place in range(3):
            hot = hot_ref[place * D : place * D + grow]
            before = before + mm(jnp.concatenate([hot, hot], axis=1), taps[order[place]])
        value, slope = gelu_pair(before)
        mids.append(value[HALO : HALO + cap].astype(BF16))
        grads.append((back_mid * slope).astype(BF16))
    dproj2 = mm_tn(mids[0], own_gb) + mm_tn(mids[1], own_gb)
    put(1, dproj2)
    base_g = cx[D : D + inner].astype(F32)
    b1 = b1_ref[...]
    s1 = s1_ref[...]
    s2 = s2_ref[...]
    sal = jnp.zeros((8, cap), F32)
    emb = embed_ref[...]
    emb8 = jnp.concatenate([emb, emb], axis=0)
    flipped = jnp.concatenate(
        [emb[3 - c : 4 - c] for c in range(4)] * 2, axis=0
    )
    sec_high, sec_low = split(second)
    bases = bases_ref[...]
    dproj1 = None
    for pass_idx, (hot_ref, order) in enumerate(((hot_f_ref, (0, 1, 2)), (hot_r_ref, (2, 1, 0)))):
        grad = grads[pass_idx]
        ga = jnp.zeros((inner, cx.shape[1]), F32)
        for place in range(3):
            ga = ga + mm_nt(grad[place * D : place * D + inner], conv(order[2 - place]))
        hot = hot_ref[2 * D : 2 * D + inner]
        hot2 = jnp.concatenate([hot, hot], axis=1)
        g = base_g + ga * mm(hot2, s2)
        gb = g.astype(BF16)
        own_hot = (hot[d : d + cap].astype(F32) * own_col).astype(BF16)
        own_b1 = mm(own_hot, b1).astype(BF16)
        piece = mm_tn(own_b1, gb[d : d + cap])
        dproj1 = piece if dproj1 is None else dproj1 + piece
        gh = (mm_nt(gb, p1) * mm(hot2, s1)).astype(BF16)
        g_high, g_low = split(g[d : d + cap])
        e_high, e_low = split(emb8 if pass_idx == 0 else flipped)
        sal = sal + mm_nt(e_high, g_high) + mm_nt(e_high, g_low) + mm_nt(e_low, g_high)
        table = jnp.zeros((16, cap), F32)
        for place in range(3):
            k = order[2 - place]
            rows = gh[place * d : place * d + cap]
            table = table + mm_nt(sec_high[16 * k : 16 * k + 16], rows)
            table = table + mm_nt(sec_low[16 * k : 16 * k + 16], rows)
        got = jnp.zeros((4, cap), F32)
        for q in range(4):
            match = bases == (q if pass_idx == 0 else 3 - q)
            got = got + jnp.where(match, table[4 * q : 4 * q + 4], 0.0)
        if pass_idx == 1:
            got = jnp.concatenate([got[3 - c : 4 - c] for c in range(4)], axis=0)
        sal = sal + jnp.concatenate([got, got], axis=0)
    put(0, dproj1)
    live = iota((1, cap), 1) < count
    sal_ref[...] = jnp.where(live, sal[0:4] * (1.0 / math.sqrt(cx.shape[1])), 0.0)


def tower_kernel_packed(rels, where_ref, *refs):
    parts = refs[: len(rels)]
    bases_ref, cx_ref, b1_ref, s1_ref, a2_ref, s2_ref, hf, hr, p1_ref, emb = refs[len(rels) : len(rels) + 10]
    sal_ref, keep_ref, send_ref, conv_ref, p2_ref, all_ref = refs[len(rels) + 10 :]
    me, count = where_ref[0], where_ref[2]
    chans = cx_ref.shape[1]
    width = chans // 2
    shard = chans // 8
    prow = width // 8
    half = 3 * shard // 2
    second = jnp.zeros((48, width), F32)
    for rel, part in zip(rels, parts):
        peer = me ^ rel
        at = pl.multiple_of(peer * shard, 16)
        conv_ref[0, pl.ds(at, shard), :] = part[0:shard, 0:width]
        conv_ref[1, pl.ds(at, half - shard), :] = part[shard:half, 0:width]
        at_half = pl.multiple_of(peer * shard + (half - shard), 16)
        conv_ref[1, pl.ds(at_half, half - shard), :] = part[0 : half - shard, width : 2 * width]
        conv_ref[2, pl.ds(at, shard), :] = part[half - shard : half, width : 2 * width]
        p2_ref[pl.ds(pl.multiple_of(peer * prow, 16), prow), :] = part[half : half + prow]
        tail = part[half + prow : half + prow + 48].astype(F32)
        second = second + tail[:, 0:width] + tail[:, width : 2 * width]

    def put(block, value):
        rows = value.shape[0] // 4
        for c in range(4):
            all_ref[(4 * block + c) ^ me] = value[c * rows : (c + 1) * rows]

    tower_body(
        lambda k: conv_ref[k], p2_ref[...], second, p1_ref[...], count, bases_ref, cx_ref,
        b1_ref, s1_ref, a2_ref, s2_ref, hf, hr, emb, sal_ref, put,
    )
    for rel in range(4):
        keep_ref[rel] = all_ref[2 * rel]
        send_ref[rel] = all_ref[2 * rel + 1].astype(BF16)


def tower_kernel_plain(
    where_ref, conv_ref, p2_ref, second_ref, p1_ref, bases_ref, cx_ref, b1_ref, s1_ref,
    a2_ref, s2_ref, hf, hr, emb, sal_ref, grad_ref,
):
    def put(block, value):
        rows = value.shape[0]
        grad_ref[block * rows : (block + 1) * rows] = value

    tower_body(
        lambda k: conv_ref[k], p2_ref[...], second_ref[...], p1_ref[...], where_ref[2],
        bases_ref, cx_ref, b1_ref, s1_ref, a2_ref, s2_ref, hf, hr, emb, sal_ref, put,
    )


def core_sum_kernel(keep_ref, recv_ref, own_ref, x_ref, y_ref, d_ref):
    own_ref[...] = keep_ref[0] + recv_ref[0].astype(F32)
    for rel, out in ((1, x_ref), (2, y_ref), (3, d_ref)):
        out[...] = (keep_ref[rel] + recv_ref[rel].astype(F32)).astype(BF16)


def plane_sum_kernel(where_ref, own_ref, x_ref, y_ref, d_ref, *refs):
    outs, sum_ref = refs[:-1], refs[-1]
    sum_ref[...] = (
        own_ref[...] + x_ref[...].astype(F32) + y_ref[...].astype(F32) + d_ref[...].astype(F32)
    )
    z = where_ref[1]
    rows = own_ref.shape[0] // len(outs)
    width = own_ref.shape[1] // 2
    for rel, out in enumerate(outs):
        value = sum_ref[pl.ds(pl.multiple_of((z ^ rel) * rows, 8), rows), :]
        if rel == 0:
            out[...] = value
        else:
            out[...] = jnp.concatenate(
                [value[:, 0:width], value[:, width : 2 * width]], axis=0
            ).astype(BF16)


def last_sum_kernel(scale, own_ref, *refs):
    out_ref = refs[-1]
    total = own_ref[...]
    rows = total.shape[0]
    for ref in refs[:-1]:
        value = ref[...].astype(F32)
        total = total + jnp.concatenate([value[0:rows], value[rows : 2 * rows]], axis=1)
    out_ref[...] = total * scale


def xor_move(array, axis, bits):
    return lax.ppermute(array, axis, [(i, i ^ bits) for i in range(lax.axis_size(axis))])


def shift_move(array, axis, by):
    size = lax.axis_size(axis)
    return lax.ppermute(array, axis, [(i, i + by) for i in range(size) if 0 <= i + by < size])


def table_shapes(cap, chans, width):
    rows = cap + 2 * (HALO + SECOND_DILATION)
    return [
        ((TABLE, width), BF16),
        ((2 * TABLE, width), BF16),
        ((TABLE, chans), BF16),
        ((2 * TABLE, chans), BF16),
        ((rows, TABLE), BF16),
        ((rows, TABLE), BF16),
        ((cap + 2 * HALO, chans), BF16),
    ]


def fast_shards(bases, where, cot, c1, p1, c2, p2, embed):
    cap, chans = cot.shape
    width = c1.shape[2]
    n_dp = lax.axis_size("dp")
    m1, m2, r1, r2, l1, l2 = call(
        prep_kernel,
        [
            ((p1.shape[0] + 16, chans), BF16),
            ((3 * c2.shape[1] // 2 + p2.shape[0] + 48, chans), BF16),
            ((HALO, chans), BF16),
            ((SPILL, chans), BF16),
            ((HALO, chans), BF16),
            ((SPILL, chans), BF16),
        ],
        [where, bases, cot, c1, p1, c2, p2, embed],
    )

    def gather(m):
        near = [m] + [xor_move(m, "seq", bits) for bits in (2, 4, 6)]
        return near + [xor_move(a, "seq", 1) for a in near]

    rels = (0, 2, 4, 6, 1, 3, 5, 7)
    g1 = gather(m1)
    halos = [
        shift_move(r1, "seq", 1),
        shift_move(r2, "seq", 2),
        shift_move(l1, "seq", -1),
        shift_move(l2, "seq", -2),
    ]
    g2 = gather(m2)
    tables = call(
        functools.partial(table_kernel_packed, rels),
        table_shapes(cap, chans, width) + [((width, chans), BF16)],
        [where, *g1, cot, *halos, embed],
        scratch=[pltpu.VMEM((8 + 2 * REACH, 8, 256), F32)],
        cost=pl.CostEstimate(flops=3 * 10**8, bytes_accessed=4 * 10**6, transcendentals=0),
    )
    b1, s1, a2, s2, hf, hr, cx, p1_full = tables
    rows = chans // 8
    sal, keep, send = call(
        functools.partial(tower_kernel_packed, rels),
        [((4, cap), F32), ((4, rows, chans), F32), ((4, rows, chans), BF16)],
        [where, *g2, bases, cx, b1, s1, a2, s2, hf, hr, p1_full, embed],
        scratch=[
            pltpu.VMEM((3, chans, width), BF16),
            pltpu.VMEM((width, chans), BF16),
            pltpu.VMEM((8, rows, chans), F32),
        ],
        limit=40,
    )
    recv = xor_move(send, "seq", 1)
    own, sx, sy, sd = call(
        core_sum_kernel,
        [((rows, chans), F32)] + [((rows, chans), BF16)] * 3,
        [keep, recv],
    )
    got = [xor_move(a, "seq", bits) for a, bits in ((sx, 2), (sy, 4), (sd, 6))]
    part = rows // n_dp
    outs = call(
        plane_sum_kernel,
        [((part, chans), F32)] + [((2 * part, width), BF16)] * (n_dp - 1),
        [where, own, *got],
        scratch=[pltpu.VMEM((rows, chans), F32)],
    )
    far = [xor_move(a, "dp", rel + 1) for rel, a in enumerate(outs[1:])]
    scale = 1.0 / math.sqrt(8 * n_dp * cap)
    (grad,) = call(
        functools.partial(last_sum_kernel, scale), [((part, chans), F32)], [outs[0], *far]
    )
    return sal[None], grad.reshape(-1)


def plain_shards(bases, where, cot, c1, p1, c2, p2, embed):
    cap, chans = cot.shape
    width = c1.shape[2]
    me, count = where[0], where[2]
    shard = c1.shape[1]
    own = lax.dynamic_slice_in_dim(embed, me * shard, shard, 1)
    act, slope = gelu_pair(own)
    taps = c1.astype(F32)
    high = lax.Precision.HIGHEST
    first = jnp.einsum("qc,kcb->kqb", act.astype(BF16).astype(F32), taps, precision=high)
    second = jnp.einsum("qc,dc,kcb->kqdb", slope, own, taps, precision=high)
    first = lax.psum(first.reshape(12, width), "seq")
    second = lax.psum(second.reshape(48, width), "seq")
    first = jnp.concatenate([first, jnp.zeros((4, width), F32)], axis=0)
    p1_full = lax.all_gather(p1, "seq", axis=0, tiled=True)
    p2_full = lax.all_gather(p2, "seq", axis=0, tiled=True)
    conv = lax.all_gather(c2, "seq", axis=1, tiled=True)
    info = jnp.concatenate(
        [bases.astype(F32), jnp.broadcast_to(count.astype(F32), (1, 128))], axis=1
    )
    info = lax.all_gather(info, "seq", axis=0, tiled=True)
    info = jnp.pad(info, ((REACH, REACH), (0, 0)))
    info = lax.dynamic_slice_in_dim(info, me, 2 * REACH + 1, 0)
    info = jnp.broadcast_to(info[:, None, :], (2 * REACH + 1, 8, cap + 128))
    padded = jnp.pad(cot, ((HALO, 0), (0, 0)))
    last = lax.dynamic_slice_in_dim(padded, count, HALO, 0)
    halos = [
        shift_move(last, "seq", 1),
        shift_move(last[HALO - SPILL :], "seq", 2),
        shift_move(cot[:HALO], "seq", -1),
        shift_move(cot[:SPILL], "seq", -2),
    ]
    b1, s1, a2, s2, hf, hr, cx = call(
        table_kernel_plain,
        table_shapes(cap, chans, width),
        [first, p1_full, info, cot, *halos, embed],
    )
    sal, grad = call(
        tower_kernel_plain,
        [((4, cap), F32), ((2 * width, chans), F32)],
        [where, conv, p2_full, second, p1_full, bases, cx, b1, s1, a2, s2, hf, hr, embed],
        limit=40,
    )
    scale = 1.0 / math.sqrt(lax.axis_size("seq") * lax.axis_size("dp") * cap)
    grad = lax.psum_scatter(
        grad.reshape(-1) * scale, ("seq", "dp"), scatter_dimension=0, tiled=True
    )
    return sal[None], grad


def shards(
    bases,
    lengths,
    cotangent,
    first_conv_taps,
    first_projection,
    second_conv_taps,
    second_projection,
    embed,
):
    where = jnp.stack(
        [
            lax.axis_index("seq").astype(jnp.int32),
            lax.axis_index("dp").astype(jnp.int32),
            lengths[0, 0],
        ]
    )
    run = fast_shards if lax.axis_size("seq") == 8 and lax.axis_size("dp") == 4 else plain_shards
    return run(
        bases, where, cotangent[0], first_conv_taps, first_projection, second_conv_taps,
        second_projection, embed,
    )


def solution(mesh):
    in_specs = (
        P("dp", "seq"),
        P("dp", "seq"),
        P("dp", "seq", None),
        P(None, "seq", None),
        P("seq", None),
        P(None, "seq", None),
        P("seq", None),
        P(),
    )
    out_specs = (P("dp", None, "seq"), P(("seq", "dp")))
    return jax.shard_map(shards, mesh=mesh, in_specs=in_specs, out_specs=out_specs, check_vma=False)
```

```python
import functools
import math

import jax
import jax.numpy as jnp
from jax import lax
from jax.experimental import pallas as pl
from jax.experimental.pallas import tpu as pltpu
from jax.sharding import PartitionSpec as P

FIRST_DILATION = 16
SECOND_DILATION = 64
HALO = FIRST_DILATION + SECOND_DILATION
SPILL = 16
REACH = 3
TABLE = 128
SQRT_HALF = 0.7071067811865476
INV_SQRT_TWO_PI = 0.3989422804014327
F32 = jnp.float32
BF16 = jnp.bfloat16
FAR = -100000.0


def gelu_pair(v):
    half = 0.5 * (1.0 + lax.erf(v * SQRT_HALF))
    return v * half, half + v * jnp.exp(-0.5 * v * v) * INV_SQRT_TWO_PI


def split(v):
    high = v.astype(BF16)
    return high, (v - high.astype(F32)).astype(BF16)


def mm(a, b):
    return lax.dot_general(a, b, (((1,), (0,)), ((), ())), preferred_element_type=F32)


def mm_nt(a, b):
    return lax.dot_general(a, b, (((1,), (1,)), ((), ())), preferred_element_type=F32)


def mm_tn(a, b):
    return lax.dot_general(a, b, (((0,), (0,)), ((), ())), preferred_element_type=F32)


def iota(shape, dim):
    return lax.broadcasted_iota(jnp.int32, shape, dim)


def spread(rows, index):
    out = jnp.broadcast_to(rows[0:1], (index.shape[0], rows.shape[1]))
    for q in range(1, 4):
        out = jnp.where(index == q, rows[q : q + 1], out)
    return out


def call(body, out_shapes, args, scratch=(), limit=24, cost=None, space=pltpu.VMEM):
    in_specs = [
        pl.BlockSpec(memory_space=pltpu.SMEM if a.dtype == jnp.int32 and a.ndim == 1 else space)
        for a in args
    ]
    return pl.pallas_call(
        body,
        out_shape=[jax.ShapeDtypeStruct(s, d) for s, d in out_shapes],
        in_specs=in_specs,
        out_specs=[pl.BlockSpec(memory_space=pltpu.VMEM)] * len(out_shapes),
        scratch_shapes=list(scratch),
        compiler_params=pltpu.CompilerParams(vmem_limit_bytes=limit * 1024 * 1024),
        cost_estimate=cost,
    )(*args)


def base_tables(embed_ref, pick, conv, shard):
    row = iota((16, 1), 0)
    low, high = row & 3, row >> 2
    emb = embed_ref[...]
    by_low = spread(emb, low)
    by_high = spread(emb, high)
    act = gelu_pair(by_low)[0].astype(BF16)
    prod_high, prod_low = split(gelu_pair(by_high)[1] * by_low)
    own = mm(jnp.concatenate([act, prod_high, prod_low], axis=0), pick).astype(BF16)
    first = jnp.zeros((16, conv.shape[2]), F32)
    second = []
    for k in range(3):
        res = mm(own, conv[k])
        first = jnp.where(high == k, res[0:16], first)
        second.append(res[16:32] + res[32:48])
    return first, jnp.concatenate(second, axis=0)


def prep_kernel(where_ref, *refs):
    sources = refs[:7]
    own_ref, x_ref, y_ref, d_ref, cot_out, embed_out, bases_out = refs[7:14]
    held = refs[14:21]
    sems = refs[21]
    moves = [
        pltpu.make_async_copy(src, dst, sems.at[n])
        for n, (src, dst) in enumerate(zip(sources, held))
    ]
    for move in moves:
        move.start()
    for move in moves:
        move.wait()
    embed_ref, c1_ref, cot_ref, bases_ref, c2_ref, p2_ref, p1_ref = held
    me, count = where_ref[0], where_ref[2]
    shard = c1_ref.shape[1]
    chans = embed_ref.shape[1]
    width = c1_ref.shape[2]
    cap = bases_ref.shape[1]
    prows = p1_ref.shape[0]
    pick = (iota((chans, shard), 0) == iota((chans, shard), 1) + me * shard).astype(BF16)
    first, second = base_tables(embed_ref, pick, c1_ref, shard)
    f_high, f_low = split(first)
    info = jnp.concatenate(
        [
            bases_ref[...].astype(F32),
            jnp.full((1, 128), count, jnp.int32).astype(F32),
            jnp.zeros((1, chans - cap - 128), F32),
        ],
        axis=1,
    )
    tail = jnp.concatenate([f_high.astype(F32), f_low.astype(F32)], axis=1)
    tail = jnp.where(iota((16, 1), 0) == 12, info, tail)
    wide = jnp.concatenate([second[0:24], second[24:48]], axis=1)
    tail = jnp.concatenate([wide, tail, jnp.zeros((8, chans), F32)], axis=0).astype(BF16)
    half = 3 * shard // 2
    flat = c2_ref[...].reshape(3 * shard, width)
    cot = cot_ref[...]
    take = (iota((HALO, cap), 1) == iota((HALO, cap), 0) + (count - HALO)).astype(BF16)
    last = mm(take, cot).astype(BF16)
    chip = me >> 1
    for rel, out in enumerate((own_ref, x_ref, y_ref, d_ref)):
        out[0:half, 0:width] = flat[0:half]
        out[0:half, width : 2 * width] = flat[half : 2 * half]
        out[half : half + prows] = p2_ref[...]
        out[half + prows : half + 2 * prows] = p1_ref[...]
        out[half + 2 * prows : half + 2 * prows + 48] = tail
        upward = (me & 1) == 0 if rel == 0 else (chip ^ rel) > chip
        out[half + 2 * prows + 48 :] = jnp.where(upward, last, cot[0:HALO])
    cot_out[...] = cot
    embed_out[...] = embed_ref[...]
    bases_out[...] = bases_ref[...]


def table_body(
    first, project, info_at, cot_ref, r1, r2, l1, l2, embed_ref,
    b1_ref, s1_ref, a2_ref, s2_ref, hot_f_ref, hot_r_ref, cx_ref,
):
    cap = cot_ref.shape[0]
    outer = HALO + SECOND_DILATION + FIRST_DILATION
    span = cap + 2 * outer
    counts = [info_at(o)[0:1, cap : cap + 128] for o in range(-REACH, REACH + 1)]
    begin = [None] * (2 * REACH + 1)
    begin[REACH] = jnp.zeros((1, 128), F32)
    for o in range(1, REACH + 1):
        begin[REACH + o] = begin[REACH + o - 1] + counts[REACH + o - 1]
        begin[REACH - o] = begin[REACH - o + 1] - counts[REACH - o]
    lane = iota((1, 128), 1).astype(F32)
    rowpos = (iota((span, 128), 0) - outer).astype(F32)
    total = jnp.zeros((span, 128), F32)
    for o in range(-REACH, REACH + 1):
        code = info_at(o)[0:1, 0:cap] + 1.0
        pos = jnp.where(lane < counts[REACH + o], begin[REACH + o] + lane, FAR)
        total = total + jnp.where(rowpos == pos, code, 0.0)
    codes = jnp.sum(total, axis=1, keepdims=True)
    d = FIRST_DILATION
    left, mid, right = codes[0 : span - 2 * d], codes[d : span - d], codes[2 * d : span]
    rows = span - 2 * d
    lanes = iota((rows, TABLE), 1).astype(F32)
    flip = lambda c: jnp.where(c == 0.0, 0.0, 5.0 - c)
    idx = jnp.where(mid == 0.0, -1.0, (mid - 1.0) * 25.0 + left * 5.0 + right)
    hot_f_ref[...] = (lanes == idx).astype(BF16)
    idx = jnp.where(mid == 0.0, -1.0, (4.0 - mid) * 25.0 + flip(right) * 5.0 + flip(left))
    hot_r_ref[...] = (lanes == idx).astype(BF16)

    entry = iota((TABLE, 1), 0)
    by25 = (entry * 1311) >> 15
    by5 = (entry * 6554) >> 15
    in_left = by5 - 5 * by25
    in_right = entry - 5 * by5
    sums = jnp.zeros((TABLE, first.shape[1]), F32)
    for q in range(4):
        sums = jnp.where(in_left == q + 1, first[q : q + 1], sums)
    sums = sums + spread(first[4:8], by25)
    after = jnp.zeros((TABLE, first.shape[1]), F32)
    for q in range(4):
        after = jnp.where(in_right == q + 1, first[8 + q : 9 + q], after)
    value, slope = gelu_pair(sums + after)
    b1 = value.astype(BF16)
    b1_ref[...] = b1
    high, low = split(slope)
    s1_ref[0:TABLE] = high
    s1_ref[TABLE : 2 * TABLE] = low
    stream = spread(embed_ref[...], by25) + mm(b1, project)
    value, slope = gelu_pair(stream)
    a2_ref[...] = value.astype(BF16)
    high, low = split(slope)
    s2_ref[0:TABLE] = high
    s2_ref[TABLE : 2 * TABLE] = low

    own_n = counts[REACH]
    before_n, after_n = counts[REACH - 1], counts[REACH + 1]
    grow = cap + 2 * HALO
    lane_h = iota((1, HALO), 1).astype(F32)
    lane_s = iota((1, SPILL), 1).astype(F32)
    row_h = (iota((grow, HALO), 0) - HALO).astype(F32)
    row_s = (iota((grow, SPILL), 0) - HALO).astype(F32)
    row_o = (iota((grow, cap), 0) - HALO).astype(F32)
    own_pos = jnp.where(lane < own_n, lane, FAR)
    acc = mm((row_o == own_pos).astype(BF16), cot_ref[...])
    pos = jnp.where(lane_h >= HALO - before_n[:, 0:HALO], lane_h - HALO, FAR)
    acc = acc + mm((row_h == pos).astype(BF16), r1)
    pos = jnp.where(
        counts[REACH - 2][:, 0:SPILL] > 0.0, lane_s - SPILL - before_n[:, 0:SPILL], FAR
    )
    acc = acc + mm((row_s == pos).astype(BF16), r2)
    pos = jnp.where(lane_h < after_n[:, 0:HALO], lane_h + own_n[:, 0:HALO], FAR)
    acc = acc + mm((row_h == pos).astype(BF16), l1)
    pos = jnp.where(
        (counts[REACH + 2][:, 0:SPILL] > 0.0) & (after_n[:, 0:SPILL] < HALO),
        lane_s + own_n[:, 0:SPILL] + after_n[:, 0:SPILL],
        FAR,
    )
    acc = acc + mm((row_s == pos).astype(BF16), l2)
    cx_ref[...] = (0.5 * acc).astype(BF16)


def table_kernel_plain(
    first_ref, project_ref, info_ref, cot_ref, r1_ref, r2_ref, l1_ref, l2_ref, embed_ref, *outs
):
    table_body(
        first_ref[...], project_ref[...], lambda o: info_ref[REACH + o], cot_ref, r1_ref[...],
        r2_ref[...], l1_ref[...], l2_ref[...], embed_ref, *outs
    )


def tower_body(
    conv, p2, second, p1, count, bases_ref, cx_ref, b1_ref, s1_ref, a2_ref, s2_ref,
    hot_f_ref, hot_r_ref, embed_ref, sal_ref, put,
):
    cap = bases_ref.shape[1]
    grow = cap + 2 * HALO
    inner = cap + 2 * FIRST_DILATION
    d, D = FIRST_DILATION, SECOND_DILATION
    cx = cx_ref[...]
    a2 = a2_ref[...]
    taps = []
    for k in range(3):
        high, low = split(mm(a2, conv(k)))
        taps.append(jnp.concatenate([high, low], axis=0))
    back_mid = mm_nt(cx, p2)
    own_col = (iota((cap, 1), 0) < count).astype(F32)
    own_cx = cx[HALO : HALO + cap]
    own_gb = (own_cx.astype(F32) * own_col).astype(BF16)
    grads = []
    mids = []
    for hot_ref, order in ((hot_f_ref, (0, 1, 2)), (hot_r_ref, (2, 1, 0))):
        before = jnp.zeros((grow, a2_ref.shape[1] // 2), F32)
        for place in range(3):
            hot = hot_ref[place * D : place * D + grow]
            before = before + mm(jnp.concatenate([hot, hot], axis=1), taps[order[place]])
        value, slope = gelu_pair(before)
        mids.append(value[HALO : HALO + cap].astype(BF16))
        grads.append((back_mid * slope).astype(BF16))
    dproj2 = mm_tn(mids[0], own_gb) + mm_tn(mids[1], own_gb)
    put(1, dproj2)
    base_g = cx[D : D + inner].astype(F32)
    b1 = b1_ref[...]
    s1 = s1_ref[...]
    s2 = s2_ref[...]
    sal = jnp.zeros((8, cap), F32)
    emb = embed_ref[...]
    emb8 = jnp.concatenate([emb, emb], axis=0)
    flipped = jnp.concatenate(
        [emb[3 - c : 4 - c] for c in range(4)] * 2, axis=0
    )
    sec_high, sec_low = split(second)
    bases = bases_ref[...]
    dproj1 = None
    for pass_idx, (hot_ref, order) in enumerate(((hot_f_ref, (0, 1, 2)), (hot_r_ref, (2, 1, 0)))):
        grad = grads[pass_idx]
        ga = jnp.zeros((inner, cx.shape[1]), F32)
        for place in range(3):
            ga = ga + mm_nt(grad[place * D : place * D + inner], conv(order[2 - place]))
        hot = hot_ref[2 * D : 2 * D + inner]
        hot2 = jnp.concatenate([hot, hot], axis=1)
        g = base_g + ga * mm(hot2, s2)
        gb = g.astype(BF16)
        own_hot = (hot[d : d + cap].astype(F32) * own_col).astype(BF16)
        own_b1 = mm(own_hot, b1).astype(BF16)
        piece = mm_tn(own_b1, gb[d : d + cap])
        dproj1 = piece if dproj1 is None else dproj1 + piece
        gh = (mm_nt(gb, p1) * mm(hot2, s1)).astype(BF16)
        g_high, g_low = split(g[d : d + cap])
        e_high, e_low = split(emb8 if pass_idx == 0 else flipped)
        sal = sal + mm_nt(e_high, g_high) + mm_nt(e_high, g_low) + mm_nt(e_low, g_high)
        table = jnp.zeros((16, cap), F32)
        for place in range(3):
            k = order[2 - place]
            rows = gh[place * d : place * d + cap]
            table = table + mm_nt(sec_high[16 * k : 16 * k + 16], rows)
            table = table + mm_nt(sec_low[16 * k : 16 * k + 16], rows)
        got = jnp.zeros((4, cap), F32)
        for q in range(4):
            match = bases == (q if pass_idx == 0 else 3 - q)
            got = got + jnp.where(match, table[4 * q : 4 * q + 4], 0.0)
        if pass_idx == 1:
            got = jnp.concatenate([got[3 - c : 4 - c] for c in range(4)], axis=0)
        sal = sal + jnp.concatenate([got, got], axis=0)
    put(0, dproj1)
    live = iota((1, cap), 1) < count
    sal_ref[...] = jnp.where(live, sal[0:4] * (1.0 / math.sqrt(cx.shape[1])), 0.0)


def tower_kernel_packed(where_ref, *refs):
    parts = refs[:8]
    cot_ref, embed_ref, bases_ref, sal_ref, keep_ref, send_ref = refs[8:14]
    tables = refs[14:21]
    conv_ref, p1_ref, p2_ref, info_ref, halo_ref, all_ref = refs[21:]
    me, count = where_ref[0], where_ref[2]
    chip, core = me >> 1, me & 1
    chans = cot_ref.shape[1]
    width = chans // 2
    shard = chans // 8
    prow = width // 8
    half = 3 * shard // 2
    info_ref[0:REACH] = jnp.zeros((REACH, 8, 256), F32)
    info_ref[REACH + 8 :] = jnp.zeros((REACH, 8, 256), F32)
    first = jnp.zeros((16, width), F32)
    wide = jnp.zeros((24, chans), F32)
    for n, part in enumerate(parts):
        rel = 2 * (n & 3) + (n >> 2)
        peer = me ^ rel
        at = pl.multiple_of(peer * shard, 16)
        conv_ref[0, pl.ds(at, shard), :] = part[0:shard, 0:width]
        conv_ref[1, pl.ds(at, half - shard), :] = part[shard:half, 0:width]
        at_half = pl.multiple_of(peer * shard + (half - shard), 16)
        conv_ref[1, pl.ds(at_half, half - shard), :] = part[0 : half - shard, width : 2 * width]
        conv_ref[2, pl.ds(at, shard), :] = part[half - shard : half, width : 2 * width]
        at = pl.multiple_of(peer * prow, 16)
        p2_ref[pl.ds(at, prow), :] = part[half : half + prow]
        p1_ref[pl.ds(at, prow), :] = part[half + prow : half + 2 * prow]
        tail = part[half + 2 * prow : half + 2 * prow + 48].astype(F32)
        wide = wide + tail[0:24]
        first = first + tail[24:40, 0:width] + tail[24:40, width : 2 * width]
        info_ref[REACH + peer] = jnp.broadcast_to(tail[36:37, 0:256], (8, 256))
        halo_ref[(n >> 2) * 4 + (peer >> 1)] = part[half + 2 * prow + 48 :]
    r1 = halo_ref[4 + jnp.maximum(chip + core - 1, 0)]
    l1 = halo_ref[4 + jnp.minimum(chip + core, 3)]
    r2 = halo_ref[jnp.maximum(chip - 1, 0)]
    l2 = halo_ref[jnp.minimum(chip + 1, 3)]
    table_body(
        first, p1_ref[...], lambda o: info_ref[me + (REACH + o)], cot_ref, r1,
        r2[HALO - SPILL :], l1, l2[0:SPILL], embed_ref, *tables,
    )
    second = jnp.concatenate([wide[:, 0:width], wide[:, width : 2 * width]], axis=0)

    def put(block, value):
        rows = value.shape[0] // 4
        for c in range(4):
            peer = 4 * block + c
            all_ref[((core ^ (peer & 1)) << 2) + (peer >> 1)] = value[c * rows : (c + 1) * rows]

    b1, s1, a2, s2, hf, hr, cx = tables
    tower_body(
        lambda k: conv_ref[k], p2_ref[...], second, p1_ref[...], count, bases_ref, cx,
        b1, s1, a2, s2, hf, hr, embed_ref, sal_ref, put,
    )
    keep_ref[...] = all_ref[0:4]
    send_ref[...] = all_ref[4:8].astype(BF16)


def tower_kernel_plain(
    where_ref, conv_ref, p2_ref, second_ref, p1_ref, bases_ref, cx_ref, b1_ref, s1_ref,
    a2_ref, s2_ref, hf, hr, emb, sal_ref, grad_ref,
):
    def put(block, value):
        rows = value.shape[0]
        grad_ref[block * rows : (block + 1) * rows] = value

    tower_body(
        lambda k: conv_ref[k], p2_ref[...], second_ref[...], p1_ref[...], where_ref[2],
        bases_ref, cx_ref, b1_ref, s1_ref, a2_ref, s2_ref, hf, hr, emb, sal_ref, put,
    )


def core_sum_kernel(where_ref, keep_ref, recv_ref, own_ref, out_ref):
    out_ref[...] = (keep_ref[...] + recv_ref[...].astype(F32)).astype(BF16)
    chip = where_ref[0] >> 1
    own_ref[...] = keep_ref[chip] + recv_ref[chip].astype(F32)


def plane_sum_kernel(where_ref, own_ref, got_ref, mine_ref, out_ref, sum_ref):
    chip, z = where_ref[0] >> 1, where_ref[1]
    total = own_ref[...]
    for c in range(got_ref.shape[0]):
        total = total + jnp.where(chip == c, 0.0, got_ref[c].astype(F32))
    sum_ref[...] = total
    count, rows = out_ref.shape[0], mine_ref.shape[0]
    width = own_ref.shape[1] // 2
    for c in range(count):
        value = total[c * rows : (c + 1) * rows]
        out_ref[c] = jnp.concatenate([value[:, 0:width], value[:, width:]], axis=0).astype(BF16)
    mine_ref[...] = sum_ref[pl.ds(pl.multiple_of(z * rows, 8), rows), :]


def last_sum_kernel(scale, where_ref, mine_ref, got_ref, out_ref):
    total = mine_ref[...]
    rows, chans = total.shape
    for c in range(got_ref.shape[0]):
        value = got_ref[c].astype(F32)
        value = jnp.concatenate([value[0:rows], value[rows : 2 * rows]], axis=1)
        total = total + jnp.where(where_ref[1] == c, 0.0, value)
    total = total * scale
    parts = chans // 128
    for n in range(parts):
        out_ref[pl.ds(n, rows, stride=parts), :] = total[:, 128 * n : 128 * n + 128]


def flip_move(array, *axes):
    sizes = [lax.axis_size(a) for a in axes]
    size = math.prod(sizes)
    return lax.ppermute(array, axes, [(i, size - 1 - i) for i in range(size)])


def shift_move(array, axis, by):
    size = lax.axis_size(axis)
    return lax.ppermute(array, axis, [(i, i + by) for i in range(size) if 0 <= i + by < size])


def table_shapes(cap, chans, width):
    rows = cap + 2 * (HALO + SECOND_DILATION)
    return [
        ((TABLE, width), BF16),
        ((2 * TABLE, width), BF16),
        ((TABLE, chans), BF16),
        ((2 * TABLE, chans), BF16),
        ((rows, TABLE), BF16),
        ((rows, TABLE), BF16),
        ((cap + 2 * HALO, chans), BF16),
    ]


def fast_shards(
    bases, lengths, cotangent, c1, p1, c2, p2, embed
):
    cot = cotangent[0]
    me = (lax.axis_index("y") * 2 + lax.axis_index("x")) * 2 + lax.axis_index("core")
    where = jnp.stack([me.astype(jnp.int32), lax.axis_index("dp").astype(jnp.int32), lengths[0, 0]])
    cap, chans = cot.shape
    width = c1.shape[2]
    n_dp = lax.axis_size("dp")
    height = 3 * c2.shape[1] // 2 + 2 * p1.shape[0] + 48 + HALO
    sources = [embed, c1, cot, bases, c2, p2, p1]
    outs = call(
        prep_kernel,
        [((height, chans), BF16)] * 4
        + [(cot.shape, BF16), (embed.shape, F32), (bases.shape, jnp.int32)],
        [where, *sources],
        scratch=[pltpu.VMEM(a.shape, a.dtype) for a in sources]
        + [pltpu.SemaphoreType.DMA((len(sources),))],
        space=pl.ANY,
    )
    near = list(outs[:4])
    for n, axes in ((1, ("x",)), (2, ("y",)), (3, ("y", "x"))):
        near[n] = flip_move(near[n], *axes)
    across = [flip_move(a, "core") for a in near]
    rows = chans // 8
    sal, keep, send = call(
        tower_kernel_packed,
        [((4, cap), F32), ((4, rows, chans), F32), ((4, rows, chans), BF16)],
        [where, outs[0], *near[1:], *across, *outs[4:]],
        scratch=[pltpu.VMEM(s, d) for s, d in table_shapes(cap, chans, width)]
        + [
            pltpu.VMEM((3, chans, width), BF16),
            pltpu.VMEM((width, chans), BF16),
            pltpu.VMEM((width, chans), BF16),
            pltpu.VMEM((8 + 2 * REACH, 8, 256), F32),
            pltpu.VMEM((8, HALO, chans), BF16),
            pltpu.VMEM((8, rows, chans), F32),
        ],
        limit=40,
    )
    recv = flip_move(send, "core")
    own, out = call(
        core_sum_kernel,
        [((rows, chans), F32), ((4, rows, chans), BF16)],
        [where, keep, recv],
    )
    got = lax.all_to_all(out, ("y", "x"), 0, 0)
    part = rows // n_dp
    mine, out = call(
        plane_sum_kernel,
        [((part, chans), F32), ((n_dp, 2 * part, width), BF16)],
        [where, own, got],
        scratch=[pltpu.VMEM((rows, chans), F32)],
    )
    got = lax.all_to_all(out, "dp", 0, 0)
    scale = 1.0 / math.sqrt(8 * n_dp * cap)
    (grad,) = call(
        functools.partial(last_sum_kernel, scale),
        [((part * chans // 128, 128), F32)],
        [where, mine, got],
    )
    return sal[None], grad.reshape(-1)


def plain_shards(bases, lengths, cotangent, c1, p1, c2, p2, embed):
    cot = cotangent[0]
    where = jnp.stack(
        [
            lax.axis_index("seq").astype(jnp.int32),
            lax.axis_index("dp").astype(jnp.int32),
            lengths[0, 0],
        ]
    )
    cap, chans = cot.shape
    width = c1.shape[2]
    me, count = where[0], where[2]
    shard = c1.shape[1]
    own = lax.dynamic_slice_in_dim(embed, me * shard, shard, 1)
    act, slope = gelu_pair(own)
    taps = c1.astype(F32)
    high = lax.Precision.HIGHEST
    first = jnp.einsum("qc,kcb->kqb", act.astype(BF16).astype(F32), taps, precision=high)
    second = jnp.einsum("qc,dc,kcb->kqdb", slope, own, taps, precision=high)
    first = lax.psum(first.reshape(12, width), "seq")
    second = lax.psum(second.reshape(48, width), "seq")
    first = jnp.concatenate([first, jnp.zeros((4, width), F32)], axis=0)
    p1_full = lax.all_gather(p1, "seq", axis=0, tiled=True)
    p2_full = lax.all_gather(p2, "seq", axis=0, tiled=True)
    conv = lax.all_gather(c2, "seq", axis=1, tiled=True)
    info = jnp.concatenate(
        [bases.astype(F32), jnp.broadcast_to(count.astype(F32), (1, 128))], axis=1
    )
    info = lax.all_gather(info, "seq", axis=0, tiled=True)
    info = jnp.pad(info, ((REACH, REACH), (0, 0)))
    info = lax.dynamic_slice_in_dim(info, me, 2 * REACH + 1, 0)
    info = jnp.broadcast_to(info[:, None, :], (2 * REACH + 1, 8, cap + 128))
    padded = jnp.pad(cot, ((HALO, 0), (0, 0)))
    last = lax.dynamic_slice_in_dim(padded, count, HALO, 0)
    halos = [
        shift_move(last, "seq", 1),
        shift_move(last[HALO - SPILL :], "seq", 2),
        shift_move(cot[:HALO], "seq", -1),
        shift_move(cot[:SPILL], "seq", -2),
    ]
    b1, s1, a2, s2, hf, hr, cx = call(
        table_kernel_plain,
        table_shapes(cap, chans, width),
        [first, p1_full, info, cot, *halos, embed],
    )
    sal, grad = call(
        tower_kernel_plain,
        [((4, cap), F32), ((2 * width, chans), F32)],
        [where, conv, p2_full, second, p1_full, bases, cx, b1, s1, a2, s2, hf, hr, embed],
        limit=40,
    )
    scale = 1.0 / math.sqrt(lax.axis_size("seq") * lax.axis_size("dp") * cap)
    grad = lax.psum_scatter(
        grad.reshape(-1) * scale, ("seq", "dp"), scatter_dimension=0, tiled=True
    )
    return sal[None], grad


def solution(mesh):
    run, seq = plain_shards, "seq"
    if mesh.shape["seq"] == 8:
        run, seq = fast_shards, ("y", "x", "core")
        count = mesh.shape["dp"]
        mesh = jax.sharding.Mesh(mesh.devices.reshape(2, 2, 2, count), (*seq, "dp"))
    every = seq if isinstance(seq, tuple) else (seq,)
    in_specs = (
        P("dp", seq),
        P("dp", seq),
        P("dp", seq, None),
        P(None, seq, None),
        P(seq, None),
        P(None, seq, None),
        P(seq, None),
        P(),
    )
    out_specs = (P("dp", None, seq), P((*every, "dp")))
    return jax.shard_map(run, mesh=mesh, in_specs=in_specs, out_specs=out_specs, check_vma=False)
```

```python
import functools
import math

import jax
import jax.numpy as jnp
from jax import lax
from jax.experimental import pallas as pl
from jax.experimental.pallas import tpu as pltpu
from jax.sharding import PartitionSpec as P

FIRST_DILATION = 16
SECOND_DILATION = 64
HALO = FIRST_DILATION + SECOND_DILATION
SPILL = 16
REACH = 3
TABLE = 128
SQRT_HALF = 0.7071067811865476
INV_SQRT_TWO_PI = 0.3989422804014327
F32 = jnp.float32
BF16 = jnp.bfloat16
FAR = -100000.0


def gelu_pair(v):
    half = 0.5 * (1.0 + lax.erf(v * SQRT_HALF))
    return v * half, half + v * jnp.exp(-0.5 * v * v) * INV_SQRT_TWO_PI


def split(v):
    high = v.astype(BF16)
    return high, (v - high.astype(F32)).astype(BF16)


def mm(a, b):
    return lax.dot_general(a, b, (((1,), (0,)), ((), ())), preferred_element_type=F32)


def mm_nt(a, b):
    return lax.dot_general(a, b, (((1,), (1,)), ((), ())), preferred_element_type=F32)


def mm_tn(a, b):
    return lax.dot_general(a, b, (((0,), (0,)), ((), ())), preferred_element_type=F32)


def iota(shape, dim):
    return lax.broadcasted_iota(jnp.int32, shape, dim)


def spread(rows, index):
    out = jnp.broadcast_to(rows[0:1], (index.shape[0], rows.shape[1]))
    for q in range(1, 4):
        out = jnp.where(index == q, rows[q : q + 1], out)
    return out


def call(body, out_shapes, args, scratch=(), limit=24, cost=None, space=pltpu.VMEM):
    in_specs = [
        pl.BlockSpec(memory_space=pltpu.SMEM if a.dtype == jnp.int32 and a.ndim == 1 else space)
        for a in args
    ]
    return pl.pallas_call(
        body,
        out_shape=[jax.ShapeDtypeStruct(s, d) for s, d in out_shapes],
        in_specs=in_specs,
        out_specs=[pl.BlockSpec(memory_space=pltpu.VMEM)] * len(out_shapes),
        scratch_shapes=list(scratch),
        compiler_params=pltpu.CompilerParams(vmem_limit_bytes=limit * 1024 * 1024),
        cost_estimate=cost,
    )(*args)


def base_tables(emb, pick, conv):
    row = iota((16, 1), 0)
    low, high = row & 3, row >> 2
    by_low = spread(emb, low)
    by_high = spread(emb, high)
    act = gelu_pair(by_low)[0].astype(BF16)
    prod_high, prod_low = split(gelu_pair(by_high)[1] * by_low)
    own = mm(jnp.concatenate([act, prod_high, prod_low], axis=0), pick).astype(BF16)
    first = jnp.zeros((16, conv[0].shape[1]), F32)
    second = []
    for k in range(3):
        res = mm(own, conv[k])
        first = jnp.where(high == k, res[0:16], first)
        second.append(res[16:32] + res[32:48])
    return first, jnp.concatenate(second, axis=0)


def prep_kernel(
    where_ref, narrow_ref, broad_ref, small_ref,
    own_ref, half_ref, r1_ref, r2_ref, l1_ref, l2_ref,
):
    me, count = where_ref[0], where_ref[2]
    width = narrow_ref.shape[1]
    chans = 2 * width
    shard = narrow_ref.shape[0] // 6
    prows = width // 8
    cap = broad_ref.shape[0] - 2 * prows
    half = 3 * shard // 2
    cut = half - 16
    flat = narrow_ref.at[3 * shard : 6 * shard]
    cot = broad_ref[2 * prows :]
    pick = (iota((chans, shard), 0) == iota((chans, shard), 1) + me * shard).astype(BF16)
    taps = [narrow_ref[k * shard : (k + 1) * shard] for k in range(3)]
    first, second = base_tables(small_ref[0:4], pick, taps)
    f_high, f_low = split(first)
    info = jnp.concatenate(
        [
            small_ref[4:5, 0:cap],
            jnp.full((1, 128), count, jnp.int32).astype(F32),
            jnp.zeros((1, chans - cap - 128), F32),
        ],
        axis=1,
    )
    tail = jnp.concatenate([f_high.astype(F32), f_low.astype(F32)], axis=1)
    tail = jnp.where(iota((16, 1), 0) == 12, info, tail)
    wide = jnp.concatenate([second[0:24], second[24:48]], axis=1)
    extra = jnp.concatenate([info, jnp.zeros((7, chans), F32)], axis=0)
    own_ref[0:cut, 0:width] = flat[0:cut]
    own_ref[0:cut, width:chans] = flat[half : half + cut]
    own_ref[cut:half] = tail.astype(BF16)
    own_ref[half : half + 16, 0:width] = flat[cut:half]
    own_ref[half : half + 16, width:chans] = flat[half + cut : 2 * half]
    own_ref[half + 16 : half + 16 + 2 * prows] = broad_ref[0 : 2 * prows]
    own_ref[2 * half - 32 :] = jnp.concatenate([wide, extra], axis=0).astype(BF16)
    half_ref[...] = own_ref[pl.ds(pl.multiple_of((where_ref[1] & 1) * half, 16), half), :]
    take = (iota((HALO, cap), 1) == iota((HALO, cap), 0) + (count - HALO)).astype(BF16)
    last = mm(take, cot).astype(BF16)
    r1_ref[...] = last
    r2_ref[...] = last[HALO - SPILL :]
    l1_ref[...] = cot[0:HALO]
    l2_ref[...] = cot[0:SPILL]


def table_body(
    first, project, info_at, cot, r1, r2, l1, l2, emb,
    b1_ref, s1_ref, a2_ref, s2_ref, hot_f_ref, hot_r_ref, cx_ref,
):
    cap = cot.shape[0]
    outer = HALO + SECOND_DILATION + FIRST_DILATION
    span = cap + 2 * outer
    counts = [info_at(o)[0:1, cap : cap + 128] for o in range(-REACH, REACH + 1)]
    begin = [None] * (2 * REACH + 1)
    begin[REACH] = jnp.zeros((1, 128), F32)
    for o in range(1, REACH + 1):
        begin[REACH + o] = begin[REACH + o - 1] + counts[REACH + o - 1]
        begin[REACH - o] = begin[REACH - o + 1] - counts[REACH - o]
    lane = iota((1, 128), 1).astype(F32)
    rowpos = (iota((span, 128), 0) - outer).astype(F32)
    total = jnp.zeros((span, 128), F32)
    for o in range(-REACH, REACH + 1):
        code = info_at(o)[0:1, 0:cap] + 1.0
        pos = jnp.where(lane < counts[REACH + o], begin[REACH + o] + lane, FAR)
        total = total + jnp.where(rowpos == pos, code, 0.0)
    codes = jnp.sum(total, axis=1, keepdims=True)
    d = FIRST_DILATION
    left, mid, right = codes[0 : span - 2 * d], codes[d : span - d], codes[2 * d : span]
    rows = span - 2 * d
    lanes = iota((rows, TABLE), 1).astype(F32)
    flip = lambda c: jnp.where(c == 0.0, 0.0, 5.0 - c)
    idx = jnp.where(mid == 0.0, -1.0, (mid - 1.0) * 25.0 + left * 5.0 + right)
    hot_f_ref[...] = (lanes == idx).astype(BF16)
    idx = jnp.where(mid == 0.0, -1.0, (4.0 - mid) * 25.0 + flip(right) * 5.0 + flip(left))
    hot_r_ref[...] = (lanes == idx).astype(BF16)

    entry = iota((TABLE, 1), 0)
    by25 = (entry * 1311) >> 15
    by5 = (entry * 6554) >> 15
    in_left = by5 - 5 * by25
    in_right = entry - 5 * by5
    sums = jnp.zeros((TABLE, first.shape[1]), F32)
    for q in range(4):
        sums = jnp.where(in_left == q + 1, first[q : q + 1], sums)
    sums = sums + spread(first[4:8], by25)
    after = jnp.zeros((TABLE, first.shape[1]), F32)
    for q in range(4):
        after = jnp.where(in_right == q + 1, first[8 + q : 9 + q], after)
    value, slope = gelu_pair(sums + after)
    b1 = value.astype(BF16)
    b1_ref[...] = b1
    high, low = split(slope)
    s1_ref[0:TABLE] = high
    s1_ref[TABLE : 2 * TABLE] = low
    stream = spread(emb, by25) + mm(b1, project)
    value, slope = gelu_pair(stream)
    a2_ref[...] = value.astype(BF16)
    high, low = split(slope)
    s2_ref[0:TABLE] = high
    s2_ref[TABLE : 2 * TABLE] = low

    own_n = counts[REACH]
    before_n, after_n = counts[REACH - 1], counts[REACH + 1]
    grow = cap + 2 * HALO
    lane_h = iota((1, HALO), 1).astype(F32)
    lane_s = iota((1, SPILL), 1).astype(F32)
    row_h = (iota((grow, HALO), 0) - HALO).astype(F32)
    row_s = (iota((grow, SPILL), 0) - HALO).astype(F32)
    row_o = (iota((grow, cap), 0) - HALO).astype(F32)
    own_pos = jnp.where(lane < own_n, lane, FAR)
    acc = mm((row_o == own_pos).astype(BF16), cot)
    pos = jnp.where(lane_h >= HALO - before_n[:, 0:HALO], lane_h - HALO, FAR)
    acc = acc + mm((row_h == pos).astype(BF16), r1)
    pos = jnp.where(
        counts[REACH - 2][:, 0:SPILL] > 0.0, lane_s - SPILL - before_n[:, 0:SPILL], FAR
    )
    acc = acc + mm((row_s == pos).astype(BF16), r2)
    pos = jnp.where(lane_h < after_n[:, 0:HALO], lane_h + own_n[:, 0:HALO], FAR)
    acc = acc + mm((row_h == pos).astype(BF16), l1)
    pos = jnp.where(
        (counts[REACH + 2][:, 0:SPILL] > 0.0) & (after_n[:, 0:SPILL] < HALO),
        lane_s + own_n[:, 0:SPILL] + after_n[:, 0:SPILL],
        FAR,
    )
    acc = acc + mm((row_s == pos).astype(BF16), l2)
    cx_ref[...] = (0.5 * acc).astype(BF16)


def table_kernel_plain(
    first_ref, project_ref, info_ref, cot_ref, r1_ref, r2_ref, l1_ref, l2_ref, embed_ref, *outs
):
    table_body(
        first_ref[...], project_ref[...], lambda o: info_ref[REACH + o], cot_ref[...], r1_ref[...],
        r2_ref[...], l1_ref[...], l2_ref[...], embed_ref[...], *outs
    )


def tower_body(
    conv, p2, second, p1, count, bases, cx_ref, b1_ref, s1_ref, a2_ref, s2_ref,
    hot_f_ref, hot_r_ref, emb, sal_ref, put,
):
    cap = bases.shape[1]
    grow = cap + 2 * HALO
    inner = cap + 2 * FIRST_DILATION
    d, D = FIRST_DILATION, SECOND_DILATION
    cx = cx_ref[...]
    a2 = a2_ref[...]
    taps = []
    for k in range(3):
        high, low = split(mm(a2, conv(k)))
        taps.append(jnp.concatenate([high, low], axis=0))
    back_mid = mm_nt(cx, p2)
    own_col = (iota((cap, 1), 0) < count).astype(F32)
    own_cx = cx[HALO : HALO + cap]
    own_gb = (own_cx.astype(F32) * own_col).astype(BF16)
    grads = []
    mids = []
    for hot_ref, order in ((hot_f_ref, (0, 1, 2)), (hot_r_ref, (2, 1, 0))):
        before = jnp.zeros((grow, a2_ref.shape[1] // 2), F32)
        for place in range(3):
            hot = hot_ref[place * D : place * D + grow]
            before = before + mm(jnp.concatenate([hot, hot], axis=1), taps[order[place]])
        value, slope = gelu_pair(before)
        mids.append(value[HALO : HALO + cap].astype(BF16))
        grads.append((back_mid * slope).astype(BF16))
    dproj2 = mm_tn(mids[0], own_gb) + mm_tn(mids[1], own_gb)
    put(1, dproj2)
    base_g = cx[D : D + inner].astype(F32)
    b1 = b1_ref[...]
    s1 = s1_ref[...]
    s2 = s2_ref[...]
    sal = jnp.zeros((8, cap), F32)
    emb8 = jnp.concatenate([emb, emb], axis=0)
    flipped = jnp.concatenate(
        [emb[3 - c : 4 - c] for c in range(4)] * 2, axis=0
    )
    sec_high, sec_low = split(second)
    dproj1 = None
    for pass_idx, (hot_ref, order) in enumerate(((hot_f_ref, (0, 1, 2)), (hot_r_ref, (2, 1, 0)))):
        grad = grads[pass_idx]
        ga = jnp.zeros((inner, cx.shape[1]), F32)
        for place in range(3):
            ga = ga + mm_nt(grad[place * D : place * D + inner], conv(order[2 - place]))
        hot = hot_ref[2 * D : 2 * D + inner]
        hot2 = jnp.concatenate([hot, hot], axis=1)
        g = base_g + ga * mm(hot2, s2)
        gb = g.astype(BF16)
        own_hot = (hot[d : d + cap].astype(F32) * own_col).astype(BF16)
        own_b1 = mm(own_hot, b1).astype(BF16)
        piece = mm_tn(own_b1, gb[d : d + cap])
        dproj1 = piece if dproj1 is None else dproj1 + piece
        gh = (mm_nt(gb, p1) * mm(hot2, s1)).astype(BF16)
        g_high, g_low = split(g[d : d + cap])
        e_high, e_low = split(emb8 if pass_idx == 0 else flipped)
        sal = sal + mm_nt(e_high, g_high) + mm_nt(e_high, g_low) + mm_nt(e_low, g_high)
        table = jnp.zeros((16, cap), F32)
        for place in range(3):
            k = order[2 - place]
            rows = gh[place * d : place * d + cap]
            table = table + mm_nt(sec_high[16 * k : 16 * k + 16], rows)
            table = table + mm_nt(sec_low[16 * k : 16 * k + 16], rows)
        got = jnp.zeros((4, cap), F32)
        for q in range(4):
            match = bases == (q if pass_idx == 0 else 3 - q)
            got = got + jnp.where(match, table[4 * q : 4 * q + 4], 0.0)
        if pass_idx == 1:
            got = jnp.concatenate([got[3 - c : 4 - c] for c in range(4)], axis=0)
        sal = sal + jnp.concatenate([got, got], axis=0)
    put(0, dproj1)
    live = iota((1, cap), 1) < count
    sal_ref[...] = jnp.where(live, sal[0:4] * (1.0 / math.sqrt(cx.shape[1])), 0.0)


def tower_kernel_packed(where_ref, *refs):
    own_parts, plane_parts, dp_parts = refs[0:2], refs[2:8], refs[8:14]
    broad_ref, small_ref, r1_ref, r2_ref, l1_ref, l2_ref = refs[14:20]
    sal_ref, keep_ref, send_ref = refs[20:23]
    tables = refs[23:30]
    conv_ref, p1_ref, p2_ref, info_ref, first_ref, second_ref, all_ref = refs[30:]
    me, count = where_ref[0], where_ref[2]
    core, odd = me & 1, where_ref[1] & 1
    chans = broad_ref.shape[1]
    width = chans // 2
    shard = chans // 8
    prow = width // 8
    cap = broad_ref.shape[0] - 2 * prow
    half = 3 * shard // 2
    cut = half - 16
    info_ref[0:REACH] = jnp.zeros((REACH, 8, 256), F32)
    info_ref[REACH + 8 :] = jnp.zeros((REACH, 8, 256), F32)

    def place(side, rows, peer, told):
        at = peer * shard

        def lay(k, start, size, source, lane):
            conv_ref[k, pl.ds(pl.multiple_of(at + start, 16), size), :] = rows(
                source, size
            )[:, lane : lane + width]

        if side == 0:
            lay(0, 0, shard, 0, 0)
            lay(1, 0, cut - shard, shard, 0)
            lay(1, shard // 2, shard // 2, 0, width)
            lay(2, 0, cut - shard // 2, shard // 2, width)
            tail = rows(cut, 16).astype(F32)
            first_ref[peer] = tail[:, 0:width] + tail[:, width:]
            line = tail[12:13, 0:256]
        else:
            lay(1, cut - shard, 16, 0, 0)
            lay(2, shard - 16, 16, 0, width)
            to = pl.ds(pl.multiple_of(peer * prow, 16), prow)
            p2_ref[to, :] = rows(16, prow)
            p1_ref[to, :] = rows(16 + prow, prow)
            tail = rows(half - 32, 32).astype(F32)
            second_ref[peer] = tail[0:24]
            line = tail[24:25, 0:256]
        if told:
            info_ref[REACH + peer] = jnp.broadcast_to(line, (8, 256))

    for n in range(2):
        for side in range(2):
            rows = lambda a, size, n=n, side=side: own_parts[n][
                side * half + a : side * half + a + size
            ]
            place(side, rows, me ^ n, side == 0)
    for parity in range(2):

        @pl.when(odd == parity)
        def _():
            for n in range(6):
                peer = me ^ (2 * (n % 3 + 1) + n // 3)
                for side, part in ((parity, plane_parts[n]), (1 - parity, dp_parts[n])):
                    rows = lambda a, size, part=part: part[a : a + size]
                    place(side, rows, peer, side == parity)

    first = first_ref[0]
    wide = second_ref[0]
    for peer in range(1, 8):
        first = first + first_ref[peer]
        wide = wide + second_ref[peer]
    emb = small_ref[0:4]
    table_body(
        first, p1_ref[...], lambda o: info_ref[me + (REACH + o)], broad_ref[2 * prow :],
        r1_ref[...], r2_ref[...], l1_ref[...], l2_ref[...], emb, *tables,
    )
    second = jnp.concatenate([wide[:, 0:width], wide[:, width : 2 * width]], axis=0)

    def put(block, value):
        rows = value.shape[0] // 4
        for c in range(4):
            peer = 4 * block + c
            all_ref[((core ^ (peer & 1)) << 2) + (peer >> 1)] = value[c * rows : (c + 1) * rows]

    b1, s1, a2, s2, hf, hr, cx = tables
    tower_body(
        lambda k: conv_ref[k], p2_ref[...], second, p1_ref[...], count, small_ref[4:5, 0:cap],
        cx, b1, s1, a2, s2, hf, hr, emb, sal_ref, put,
    )
    keep_ref[...] = all_ref[0:4]
    send_ref[...] = all_ref[4:8].astype(BF16)


def tower_kernel_plain(
    where_ref, conv_ref, p2_ref, second_ref, p1_ref, bases_ref, cx_ref, b1_ref, s1_ref,
    a2_ref, s2_ref, hf, hr, emb, sal_ref, grad_ref,
):
    def put(block, value):
        rows = value.shape[0]
        grad_ref[block * rows : (block + 1) * rows] = value

    tower_body(
        lambda k: conv_ref[k], p2_ref[...], second_ref[...], p1_ref[...], where_ref[2],
        bases_ref[...], cx_ref, b1_ref, s1_ref, a2_ref, s2_ref, hf, hr, emb[...], sal_ref, put,
    )


def fold(value):
    width = value.shape[1] // 2
    return jnp.concatenate([value[:, 0:width], value[:, width:]], axis=0)


def core_sum_kernel(where_ref, keep_ref, recv_ref, mine_ref, out_ref, sum_ref):
    rows = mine_ref.shape[0] // 2
    per = keep_ref.shape[1] // rows
    for c in range(keep_ref.shape[0]):
        total = keep_ref[c] + recv_ref[c].astype(F32)
        sum_ref[c] = total
        for n in range(per):
            out_ref[per * c + n] = fold(total[n * rows : (n + 1) * rows]).astype(BF16)
    chip = where_ref[0] >> 1
    at = pl.ds(pl.multiple_of(where_ref[1] * rows, 8), rows)
    mine_ref[...] = fold(sum_ref[chip, at, :])


def last_sum_kernel(scale, where_ref, mine_ref, got_ref, out_ref):
    total = mine_ref[...]
    me = (where_ref[0] >> 1) * (got_ref.shape[0] // 4) + where_ref[1]
    for c in range(got_ref.shape[0]):
        total = total + jnp.where(me == c, 0.0, got_ref[c].astype(F32))
    total = total * scale
    rows, half = total.shape[0] // 2, total.shape[1] // 128
    for n in range(2 * half):
        at = rows * (n // half)
        lane = 128 * (n % half)
        out_ref[pl.ds(n, rows, stride=2 * half), :] = total[at : at + rows, lane : lane + 128]


def flip_move(array, *axes):
    sizes = [lax.axis_size(a) for a in axes]
    size = math.prod(sizes)
    return lax.ppermute(array, axes, [(i, size - 1 - i) for i in range(size)])


def shift_move(array, by, axes=("y", "x", "core")):
    size = math.prod(lax.axis_size(a) for a in axes)
    return lax.ppermute(array, axes, [(i, i + by) for i in range(size) if 0 <= i + by < size])


def table_shapes(cap, chans, width):
    rows = cap + 2 * (HALO + SECOND_DILATION)
    return [
        ((TABLE, width), BF16),
        ((2 * TABLE, width), BF16),
        ((TABLE, chans), BF16),
        ((2 * TABLE, chans), BF16),
        ((rows, TABLE), BF16),
        ((rows, TABLE), BF16),
        ((cap + 2 * HALO, chans), BF16),
    ]


def fast_shards(
    bases, lengths, cotangent, c1, p1, c2, p2, embed
):
    cot = cotangent[0]
    me = (lax.axis_index("y") * 2 + lax.axis_index("x")) * 2 + lax.axis_index("core")
    where = jnp.stack([me.astype(jnp.int32), lax.axis_index("dp").astype(jnp.int32), lengths[0, 0]])
    cap, chans = cot.shape
    width = c1.shape[2]
    n_dp = lax.axis_size("dp")
    half = 3 * c2.shape[1] // 2
    narrow = jnp.concatenate([c1.reshape(-1, width), c2.reshape(-1, width)], axis=0)
    broad = jnp.concatenate([p2, p1, cot], axis=0)
    small = jnp.concatenate(
        [embed, jnp.pad(bases.astype(F32), ((0, 3), (0, chans - cap)))], axis=0
    )
    own, part, r1, r2, l1, l2 = call(
        prep_kernel,
        [((r, chans), BF16) for r in (2 * half, half, HALO, SPILL, HALO, SPILL)],
        [where, narrow, broad, small],
    )
    plane = [flip_move(part, *axes) for axes in (("x",), ("y",), ("y", "x"))]
    pairs = [(i, i ^ 1) for i in range(n_dp)]
    other = [lax.ppermute(a, "dp", pairs) for a in plane]
    halos = [shift_move(r1, 1), shift_move(r2, 2), shift_move(l1, -1), shift_move(l2, -2)]
    across = lambda arrays: [flip_move(a, "core") for a in arrays]
    rows = chans // 8
    sal, keep, send = call(
        tower_kernel_packed,
        [((4, cap), F32), ((4, rows, chans), F32), ((4, rows, chans), BF16)],
        [
            where, own, *across([own]), *plane, *across(plane), *other, *across(other),
            broad, small, *halos,
        ],
        scratch=[pltpu.VMEM(s, d) for s, d in table_shapes(cap, chans, width)]
        + [
            pltpu.VMEM((3, chans, width), BF16),
            pltpu.VMEM((width, chans), BF16),
            pltpu.VMEM((width, chans), BF16),
            pltpu.VMEM((8 + 2 * REACH, 8, 256), F32),
            pltpu.VMEM((8, 16, width), F32),
            pltpu.VMEM((8, 24, chans), F32),
            pltpu.VMEM((8, rows, chans), F32),
        ],
        limit=40,
    )
    recv = flip_move(send, "core")
    part = rows // n_dp
    mine, out = call(
        core_sum_kernel,
        [((2 * part, width), F32), ((4 * n_dp, 2 * part, width), BF16)],
        [where, keep, recv],
        scratch=[pltpu.VMEM((4, rows, chans), F32)],
    )
    got = lax.all_to_all(out, ("y", "x", "dp"), 0, 0)
    scale = 1.0 / math.sqrt(8 * n_dp * cap)
    (grad,) = call(
        functools.partial(last_sum_kernel, scale),
        [((part * chans // 128, 128), F32)],
        [where, mine, got],
    )
    return sal[None], grad.reshape(-1)


def plain_shards(bases, lengths, cotangent, c1, p1, c2, p2, embed):
    cot = cotangent[0]
    where = jnp.stack(
        [
            lax.axis_index("seq").astype(jnp.int32),
            lax.axis_index("dp").astype(jnp.int32),
            lengths[0, 0],
        ]
    )
    cap, chans = cot.shape
    width = c1.shape[2]
    me, count = where[0], where[2]
    shard = c1.shape[1]
    own = lax.dynamic_slice_in_dim(embed, me * shard, shard, 1)
    act, slope = gelu_pair(own)
    taps = c1.astype(F32)
    high = lax.Precision.HIGHEST
    first = jnp.einsum("qc,kcb->kqb", act.astype(BF16).astype(F32), taps, precision=high)
    second = jnp.einsum("qc,dc,kcb->kqdb", slope, own, taps, precision=high)
    first = lax.psum(first.reshape(12, width), "seq")
    second = lax.psum(second.reshape(48, width), "seq")
    first = jnp.concatenate([first, jnp.zeros((4, width), F32)], axis=0)
    p1_full = lax.all_gather(p1, "seq", axis=0, tiled=True)
    p2_full = lax.all_gather(p2, "seq", axis=0, tiled=True)
    conv = lax.all_gather(c2, "seq", axis=1, tiled=True)
    info = jnp.concatenate(
        [bases.astype(F32), jnp.broadcast_to(count.astype(F32), (1, 128))], axis=1
    )
    info = lax.all_gather(info, "seq", axis=0, tiled=True)
    info = jnp.pad(info, ((REACH, REACH), (0, 0)))
    info = lax.dynamic_slice_in_dim(info, me, 2 * REACH + 1, 0)
    info = jnp.broadcast_to(info[:, None, :], (2 * REACH + 1, 8, cap + 128))
    padded = jnp.pad(cot, ((HALO, 0), (0, 0)))
    last = lax.dynamic_slice_in_dim(padded, count, HALO, 0)
    halos = [
        shift_move(last, 1, ("seq",)),
        shift_move(last[HALO - SPILL :], 2, ("seq",)),
        shift_move(cot[:HALO], -1, ("seq",)),
        shift_move(cot[:SPILL], -2, ("seq",)),
    ]
    b1, s1, a2, s2, hf, hr, cx = call(
        table_kernel_plain,
        table_shapes(cap, chans, width),
        [first, p1_full, info, cot, *halos, embed],
    )
    sal, grad = call(
        tower_kernel_plain,
        [((4, cap), F32), ((2 * width, chans), F32)],
        [where, conv, p2_full, second, p1_full, bases, cx, b1, s1, a2, s2, hf, hr, embed],
        limit=40,
    )
    scale = 1.0 / math.sqrt(lax.axis_size("seq") * lax.axis_size("dp") * cap)
    grad = lax.psum_scatter(
        grad.reshape(-1) * scale, ("seq", "dp"), scatter_dimension=0, tiled=True
    )
    return sal[None], grad


def solution(mesh):
    run, seq = plain_shards, "seq"
    if mesh.shape["seq"] == 8 and mesh.shape["dp"] == 4:
        run, seq = fast_shards, ("y", "x", "core")
        count = mesh.shape["dp"]
        mesh = jax.sharding.Mesh(mesh.devices.reshape(2, 2, 2, count), (*seq, "dp"))
    every = seq if isinstance(seq, tuple) else (seq,)
    in_specs = (
        P("dp", seq),
        P("dp", seq),
        P("dp", seq, None),
        P(None, seq, None),
        P(seq, None),
        P(None, seq, None),
        P(seq, None),
        P(),
    )
    out_specs = (P("dp", None, seq), P((*every, "dp")))
    return jax.shard_map(run, mesh=mesh, in_specs=in_specs, out_specs=out_specs, check_vma=False)
```

```python
import functools
import math

import jax
import jax.numpy as jnp
from jax import lax
from jax.experimental import pallas as pl
from jax.experimental.pallas import tpu as pltpu
from jax.sharding import PartitionSpec as P

FIRST_DILATION = 16
SECOND_DILATION = 64
HALO = FIRST_DILATION + SECOND_DILATION
SPILL = 16
REACH = 3
TABLE = 128
SQRT_HALF = 0.7071067811865476
INV_SQRT_TWO_PI = 0.3989422804014327
F32 = jnp.float32
BF16 = jnp.bfloat16
FAR = -100000.0


def gelu_pair(v):
    half = 0.5 * (1.0 + lax.erf(v * SQRT_HALF))
    return v * half, half + v * jnp.exp(-0.5 * v * v) * INV_SQRT_TWO_PI


def split(v):
    high = v.astype(BF16)
    return high, (v - high.astype(F32)).astype(BF16)


def mm(a, b):
    return lax.dot_general(a, b, (((1,), (0,)), ((), ())), preferred_element_type=F32)


def mm_nt(a, b):
    return lax.dot_general(a, b, (((1,), (1,)), ((), ())), preferred_element_type=F32)


def mm_tn(a, b):
    return lax.dot_general(a, b, (((0,), (0,)), ((), ())), preferred_element_type=F32)


def iota(shape, dim):
    return lax.broadcasted_iota(jnp.int32, shape, dim)


def spread(rows, index):
    out = jnp.broadcast_to(rows[0:1], (index.shape[0], rows.shape[1]))
    for q in range(1, 4):
        out = jnp.where(index == q, rows[q : q + 1], out)
    return out


def call(body, out_shapes, args, scratch=(), limit=24, cost=None, space=pltpu.VMEM):
    in_specs = [
        pl.BlockSpec(memory_space=pltpu.SMEM if a.dtype == jnp.int32 and a.ndim == 1 else space)
        for a in args
    ]
    return pl.pallas_call(
        body,
        out_shape=[jax.ShapeDtypeStruct(s, d) for s, d in out_shapes],
        in_specs=in_specs,
        out_specs=[pl.BlockSpec(memory_space=pltpu.VMEM)] * len(out_shapes),
        scratch_shapes=list(scratch),
        compiler_params=pltpu.CompilerParams(vmem_limit_bytes=limit * 1024 * 1024),
        cost_estimate=cost,
    )(*args)


def base_tables(emb, pick, conv):
    row = iota((16, 1), 0)
    low, high = row & 3, row >> 2
    by_low = spread(emb, low)
    by_high = spread(emb, high)
    act = gelu_pair(by_low)[0].astype(BF16)
    prod_high, prod_low = split(gelu_pair(by_high)[1] * by_low)
    own = mm(jnp.concatenate([act, prod_high, prod_low], axis=0), pick).astype(BF16)
    first = jnp.zeros((16, conv[0].shape[1]), F32)
    second = []
    for k in range(3):
        res = mm(own, conv[k])
        first = jnp.where(high == k, res[0:16], first)
        second.append(res[16:32] + res[32:48])
    return first, jnp.concatenate(second, axis=0)


def prep_kernel(
    where_ref, narrow_ref, broad_ref, small_ref,
    own_ref, x_ref, y_ref, d_ref,
):
    me, count = where_ref[0], where_ref[2]
    width = narrow_ref.shape[1]
    chans = 2 * width
    shard = narrow_ref.shape[0] // 6
    prows = width // 8
    cap = broad_ref.shape[0] - 2 * prows
    half = 3 * shard // 2
    cut = half - 16
    flat = narrow_ref.at[3 * shard : 6 * shard]
    cot = broad_ref[2 * prows :]
    pick = (iota((chans, shard), 0) == iota((chans, shard), 1) + me * shard).astype(BF16)
    taps = [narrow_ref[k * shard : (k + 1) * shard] for k in range(3)]
    first, second = base_tables(small_ref[0:4], pick, taps)
    f_high, f_low = split(first)
    info = jnp.concatenate(
        [
            small_ref[4:5, 0:cap],
            jnp.full((1, 128), count, jnp.int32).astype(F32),
            jnp.zeros((1, chans - cap - 128), F32),
        ],
        axis=1,
    )
    tail = jnp.concatenate([f_high.astype(F32), f_low.astype(F32)], axis=1)
    tail = jnp.where(iota((16, 1), 0) == 12, info, tail)
    wide = jnp.concatenate([second[0:24], second[24:48]], axis=1)
    extra = jnp.concatenate([info, jnp.zeros((7, chans), F32)], axis=0)
    own_ref[0:cut, 0:width] = flat[0:cut]
    own_ref[0:cut, width:chans] = flat[half : half + cut]
    own_ref[cut:half] = tail.astype(BF16)
    own_ref[half : half + 16, 0:width] = flat[cut:half]
    own_ref[half : half + 16, width:chans] = flat[half + cut : 2 * half]
    own_ref[half + 16 : half + 16 + 2 * prows] = broad_ref[0 : 2 * prows]
    own_ref[2 * half - 32 : 2 * half] = jnp.concatenate([wide, extra], axis=0).astype(BF16)
    part = own_ref[pl.ds(pl.multiple_of((where_ref[1] & 1) * half, 16), half), :]
    for out in (x_ref, y_ref, d_ref):
        out[0:half] = part
    take = (iota((HALO, cap), 1) == iota((HALO, cap), 0) + (count - HALO)).astype(BF16)
    last = mm(take, cot).astype(BF16)
    chip = me >> 1
    own_ref[2 * half :] = jnp.where((me & 1) == 0, last, cot[0:HALO])
    x_ref[half:] = jnp.where((chip ^ 1) > chip, last, cot[0:HALO])
    d_ref[half:] = jnp.where((chip ^ 3) > chip, last, cot[0:HALO])


def table_body(
    first, project, info_at, cot, r1, r2, l1, l2, emb,
    b1_ref, s1_ref, a2_ref, s2_ref, hot_f_ref, hot_r_ref, cx_ref,
):
    cap = cot.shape[0]
    outer = HALO + SECOND_DILATION + FIRST_DILATION
    span = cap + 2 * outer
    counts = [info_at(o)[0:1, cap : cap + 128] for o in range(-REACH, REACH + 1)]
    begin = [None] * (2 * REACH + 1)
    begin[REACH] = jnp.zeros((1, 128), F32)
    for o in range(1, REACH + 1):
        begin[REACH + o] = begin[REACH + o - 1] + counts[REACH + o - 1]
        begin[REACH - o] = begin[REACH - o + 1] - counts[REACH - o]
    lane = iota((1, 128), 1).astype(F32)
    rowpos = (iota((span, 128), 0) - outer).astype(F32)
    total = jnp.zeros((span, 128), F32)
    for o in range(-REACH, REACH + 1):
        code = info_at(o)[0:1, 0:cap] + 1.0
        pos = jnp.where(lane < counts[REACH + o], begin[REACH + o] + lane, FAR)
        total = total + jnp.where(rowpos == pos, code, 0.0)
    codes = jnp.sum(total, axis=1, keepdims=True)
    d = FIRST_DILATION
    left, mid, right = codes[0 : span - 2 * d], codes[d : span - d], codes[2 * d : span]
    rows = span - 2 * d
    lanes = iota((rows, TABLE), 1).astype(F32)
    flip = lambda c: jnp.where(c == 0.0, 0.0, 5.0 - c)
    idx = jnp.where(mid == 0.0, -1.0, (mid - 1.0) * 25.0 + left * 5.0 + right)
    hot_f_ref[...] = (lanes == idx).astype(BF16)
    idx = jnp.where(mid == 0.0, -1.0, (4.0 - mid) * 25.0 + flip(right) * 5.0 + flip(left))
    hot_r_ref[...] = (lanes == idx).astype(BF16)

    entry = iota((TABLE, 1), 0)
    by25 = (entry * 1311) >> 15
    by5 = (entry * 6554) >> 15
    in_left = by5 - 5 * by25
    in_right = entry - 5 * by5
    sums = jnp.zeros((TABLE, first.shape[1]), F32)
    for q in range(4):
        sums = jnp.where(in_left == q + 1, first[q : q + 1], sums)
    sums = sums + spread(first[4:8], by25)
    after = jnp.zeros((TABLE, first.shape[1]), F32)
    for q in range(4):
        after = jnp.where(in_right == q + 1, first[8 + q : 9 + q], after)
    value, slope = gelu_pair(sums + after)
    b1 = value.astype(BF16)
    b1_ref[...] = b1
    high, low = split(slope)
    s1_ref[0:TABLE] = high
    s1_ref[TABLE : 2 * TABLE] = low
    stream = spread(emb, by25) + mm(b1, project)
    value, slope = gelu_pair(stream)
    a2_ref[...] = value.astype(BF16)
    high, low = split(slope)
    s2_ref[0:TABLE] = high
    s2_ref[TABLE : 2 * TABLE] = low

    own_n = counts[REACH]
    before_n, after_n = counts[REACH - 1], counts[REACH + 1]
    grow = cap + 2 * HALO
    lane_h = iota((1, HALO), 1).astype(F32)
    lane_s = iota((1, SPILL), 1).astype(F32)
    row_h = (iota((grow, HALO), 0) - HALO).astype(F32)
    row_s = (iota((grow, SPILL), 0) - HALO).astype(F32)
    row_o = (iota((grow, cap), 0) - HALO).astype(F32)
    own_pos = jnp.where(lane < own_n, lane, FAR)
    acc = mm((row_o == own_pos).astype(BF16), cot)
    pos = jnp.where(lane_h >= HALO - before_n[:, 0:HALO], lane_h - HALO, FAR)
    acc = acc + mm((row_h == pos).astype(BF16), r1)
    pos = jnp.where(
        counts[REACH - 2][:, 0:SPILL] > 0.0, lane_s - SPILL - before_n[:, 0:SPILL], FAR
    )
    acc = acc + mm((row_s == pos).astype(BF16), r2)
    pos = jnp.where(lane_h < after_n[:, 0:HALO], lane_h + own_n[:, 0:HALO], FAR)
    acc = acc + mm((row_h == pos).astype(BF16), l1)
    pos = jnp.where(
        (counts[REACH + 2][:, 0:SPILL] > 0.0) & (after_n[:, 0:SPILL] < HALO),
        lane_s + own_n[:, 0:SPILL] + after_n[:, 0:SPILL],
        FAR,
    )
    acc = acc + mm((row_s == pos).astype(BF16), l2)
    cx_ref[...] = (0.5 * acc).astype(BF16)


def table_kernel_plain(
    first_ref, project_ref, info_ref, cot_ref, r1_ref, r2_ref, l1_ref, l2_ref, embed_ref, *outs
):
    table_body(
        first_ref[...], project_ref[...], lambda o: info_ref[REACH + o], cot_ref[...], r1_ref[...],
        r2_ref[...], l1_ref[...], l2_ref[...], embed_ref[...], *outs
    )


def tower_body(
    conv, p2, second, p1, count, bases, cx_ref, b1_ref, s1_ref, a2_ref, s2_ref,
    hot_f_ref, hot_r_ref, emb, sal_ref, put,
):
    cap = bases.shape[1]
    grow = cap + 2 * HALO
    inner = cap + 2 * FIRST_DILATION
    d, D = FIRST_DILATION, SECOND_DILATION
    cx = cx_ref[...]
    a2 = a2_ref[...]
    taps = []
    for k in range(3):
        high, low = split(mm(a2, conv(k)))
        taps.append(jnp.concatenate([high, low], axis=0))
    back_mid = mm_nt(cx, p2)
    own_col = (iota((cap, 1), 0) < count).astype(F32)
    own_cx = cx[HALO : HALO + cap]
    own_gb = (own_cx.astype(F32) * own_col).astype(BF16)
    grads = []
    mids = []
    for hot_ref, order in ((hot_f_ref, (0, 1, 2)), (hot_r_ref, (2, 1, 0))):
        before = jnp.zeros((grow, a2_ref.shape[1] // 2), F32)
        for place in range(3):
            hot = hot_ref[place * D : place * D + grow]
            before = before + mm(jnp.concatenate([hot, hot], axis=1), taps[order[place]])
        value, slope = gelu_pair(before)
        mids.append(value[HALO : HALO + cap].astype(BF16))
        grads.append((back_mid * slope).astype(BF16))
    dproj2 = mm_tn(mids[0], own_gb) + mm_tn(mids[1], own_gb)
    put(1, dproj2)
    base_g = cx[D : D + inner].astype(F32)
    b1 = b1_ref[...]
    s1 = s1_ref[...]
    s2 = s2_ref[...]
    sal = jnp.zeros((8, cap), F32)
    emb8 = jnp.concatenate([emb, emb], axis=0)
    flipped = jnp.concatenate(
        [emb[3 - c : 4 - c] for c in range(4)] * 2, axis=0
    )
    sec_high, sec_low = split(second)
    dproj1 = None
    for pass_idx, (hot_ref, order) in enumerate(((hot_f_ref, (0, 1, 2)), (hot_r_ref, (2, 1, 0)))):
        grad = grads[pass_idx]
        ga = jnp.zeros((inner, cx.shape[1]), F32)
        for place in range(3):
            ga = ga + mm_nt(grad[place * D : place * D + inner], conv(order[2 - place]))
        hot = hot_ref[2 * D : 2 * D + inner]
        hot2 = jnp.concatenate([hot, hot], axis=1)
        g = base_g + ga * mm(hot2, s2)
        gb = g.astype(BF16)
        own_hot = (hot[d : d + cap].astype(F32) * own_col).astype(BF16)
        own_b1 = mm(own_hot, b1).astype(BF16)
        piece = mm_tn(own_b1, gb[d : d + cap])
        dproj1 = piece if dproj1 is None else dproj1 + piece
        gh = (mm_nt(gb, p1) * mm(hot2, s1)).astype(BF16)
        g_high, g_low = split(g[d : d + cap])
        e_high, e_low = split(emb8 if pass_idx == 0 else flipped)
        sal = sal + mm_nt(e_high, g_high) + mm_nt(e_high, g_low) + mm_nt(e_low, g_high)
        table = jnp.zeros((16, cap), F32)
        for place in range(3):
            k = order[2 - place]
            rows = gh[place * d : place * d + cap]
            table = table + mm_nt(sec_high[16 * k : 16 * k + 16], rows)
            table = table + mm_nt(sec_low[16 * k : 16 * k + 16], rows)
        got = jnp.zeros((4, cap), F32)
        for q in range(4):
            match = bases == (q if pass_idx == 0 else 3 - q)
            got = got + jnp.where(match, table[4 * q : 4 * q + 4], 0.0)
        if pass_idx == 1:
            got = jnp.concatenate([got[3 - c : 4 - c] for c in range(4)], axis=0)
        sal = sal + jnp.concatenate([got, got], axis=0)
    put(0, dproj1)
    live = iota((1, cap), 1) < count
    sal_ref[...] = jnp.where(live, sal[0:4] * (1.0 / math.sqrt(cx.shape[1])), 0.0)


def tower_kernel_packed(where_ref, *refs):
    own_parts, plane_parts, dp_parts = refs[0:2], refs[2:8], refs[8:14]
    broad_ref, small_ref, sal_ref, keep_ref, send_ref = refs[14:19]
    tables = refs[19:26]
    conv_ref, p1_ref, p2_ref, info_ref, first_ref, second_ref, halo_ref, all_ref = refs[26:]
    me, count = where_ref[0], where_ref[2]
    chip, core, odd = me >> 1, me & 1, where_ref[1] & 1
    chans = broad_ref.shape[1]
    width = chans // 2
    shard = chans // 8
    prow = width // 8
    cap = broad_ref.shape[0] - 2 * prow
    half = 3 * shard // 2
    cut = half - 16
    info_ref[0:REACH] = jnp.zeros((REACH, 8, 256), F32)
    info_ref[REACH + 8 :] = jnp.zeros((REACH, 8, 256), F32)

    def place(side, rows, peer, told):
        at = peer * shard

        def lay(k, start, size, source, lane):
            conv_ref[k, pl.ds(pl.multiple_of(at + start, 16), size), :] = rows(
                source, size
            )[:, lane : lane + width]

        if side == 0:
            lay(0, 0, shard, 0, 0)
            lay(1, 0, cut - shard, shard, 0)
            lay(1, shard // 2, shard // 2, 0, width)
            lay(2, 0, cut - shard // 2, shard // 2, width)
            tail = rows(cut, 16).astype(F32)
            first_ref[peer] = tail[:, 0:width] + tail[:, width:]
            line = tail[12:13, 0:256]
        else:
            lay(1, cut - shard, 16, 0, 0)
            lay(2, shard - 16, 16, 0, width)
            to = pl.ds(pl.multiple_of(peer * prow, 16), prow)
            p2_ref[to, :] = rows(16, prow)
            p1_ref[to, :] = rows(16 + prow, prow)
            tail = rows(half - 32, 32).astype(F32)
            second_ref[peer] = tail[0:24]
            line = tail[24:25, 0:256]
        if told:
            info_ref[REACH + peer] = jnp.broadcast_to(line, (8, 256))

    for n in range(2):
        for side in range(2):
            rows = lambda a, size, n=n, side=side: own_parts[n][
                side * half + a : side * half + a + size
            ]
            place(side, rows, me ^ n, side == 0)
    for parity in range(2):

        @pl.when(odd == parity)
        def _():
            for n in range(6):
                peer = me ^ (2 * (n % 3 + 1) + n // 3)
                for side, part in ((parity, plane_parts[n]), (1 - parity, dp_parts[n])):
                    rows = lambda a, size, part=part: part[a : a + size]
                    place(side, rows, peer, side == parity)

    for n in range(2):
        halo_ref[4 * n + chip] = own_parts[n][2 * half :]
        halo_ref[4 * n + (chip ^ 1)] = plane_parts[3 * n][half:]
        halo_ref[4 * n + (chip ^ 3)] = plane_parts[3 * n + 2][half:]
    r1 = halo_ref[4 + jnp.maximum(chip + core - 1, 0)]
    l1 = halo_ref[4 + jnp.minimum(chip + core, 3)]
    r2 = halo_ref[jnp.maximum(chip - 1, 0)]
    l2 = halo_ref[jnp.minimum(chip + 1, 3)]
    first = first_ref[0]
    wide = second_ref[0]
    for peer in range(1, 8):
        first = first + first_ref[peer]
        wide = wide + second_ref[peer]
    emb = small_ref[0:4]
    table_body(
        first, p1_ref[...], lambda o: info_ref[me + (REACH + o)], broad_ref[2 * prow :],
        r1, r2[HALO - SPILL :], l1, l2[0:SPILL], emb, *tables,
    )
    second = jnp.concatenate([wide[:, 0:width], wide[:, width : 2 * width]], axis=0)

    def put(block, value):
        rows = value.shape[0] // 4
        for c in range(4):
            peer = 4 * block + c
            all_ref[((core ^ (peer & 1)) << 2) + (peer >> 1)] = value[c * rows : (c + 1) * rows]

    b1, s1, a2, s2, hf, hr, cx = tables
    tower_body(
        lambda k: conv_ref[k], p2_ref[...], second, p1_ref[...], count, small_ref[4:5, 0:cap],
        cx, b1, s1, a2, s2, hf, hr, emb, sal_ref, put,
    )
    keep_ref[...] = all_ref[0:4]
    send_ref[...] = all_ref[4:8].astype(BF16)


def tower_kernel_plain(
    where_ref, conv_ref, p2_ref, second_ref, p1_ref, bases_ref, cx_ref, b1_ref, s1_ref,
    a2_ref, s2_ref, hf, hr, emb, sal_ref, grad_ref,
):
    def put(block, value):
        rows = value.shape[0]
        grad_ref[block * rows : (block + 1) * rows] = value

    tower_body(
        lambda k: conv_ref[k], p2_ref[...], second_ref[...], p1_ref[...], where_ref[2],
        bases_ref[...], cx_ref, b1_ref, s1_ref, a2_ref, s2_ref, hf, hr, emb[...], sal_ref, put,
    )


def fold(value):
    width = value.shape[1] // 2
    return jnp.concatenate([value[:, 0:width], value[:, width:]], axis=0)


def core_sum_kernel(where_ref, keep_ref, recv_ref, own_ref, *outs):
    chip = where_ref[0] >> 1
    own_ref[...] = keep_ref[chip] + recv_ref[chip].astype(F32)
    for n, out in enumerate(outs):
        at = chip ^ (n + 1)
        out[...] = (keep_ref[at] + recv_ref[at].astype(F32)).astype(BF16)


def plane_sum_kernel(where_ref, own_ref, x_ref, y_ref, d_ref, mine_ref, *refs):
    outs, sum_ref = refs[:-1], refs[-1]
    sum_ref[...] = (
        own_ref[...] + x_ref[...].astype(F32) + y_ref[...].astype(F32) + d_ref[...].astype(F32)
    )
    z = where_ref[1]
    rows = mine_ref.shape[0] // 2
    mine_ref[...] = fold(sum_ref[pl.ds(pl.multiple_of(z * rows, 8), rows), :])
    for n, out in enumerate(outs):
        at = pl.multiple_of((z ^ (n + 1)) * rows, 8)
        out[...] = fold(sum_ref[pl.ds(at, rows), :]).astype(BF16)


def last_sum_kernel(scale, mine_ref, *refs):
    out_ref = refs[-1]
    total = mine_ref[...]
    for ref in refs[:-1]:
        total = total + ref[...].astype(F32)
    total = total * scale
    rows, half = total.shape[0] // 2, total.shape[1] // 128
    for n in range(2 * half):
        at = rows * (n // half)
        lane = 128 * (n % half)
        out_ref[pl.ds(n, rows, stride=2 * half), :] = total[at : at + rows, lane : lane + 128]


def flip_move(array, *axes):
    sizes = [lax.axis_size(a) for a in axes]
    size = math.prod(sizes)
    return lax.ppermute(array, axes, [(i, size - 1 - i) for i in range(size)])


def xor_move(array, axis, bits):
    return lax.ppermute(array, axis, [(i, i ^ bits) for i in range(lax.axis_size(axis))])


def shift_move(array, by, axes):
    size = math.prod(lax.axis_size(a) for a in axes)
    return lax.ppermute(array, axes, [(i, i + by) for i in range(size) if 0 <= i + by < size])


def table_shapes(cap, chans, width):
    rows = cap + 2 * (HALO + SECOND_DILATION)
    return [
        ((TABLE, width), BF16),
        ((2 * TABLE, width), BF16),
        ((TABLE, chans), BF16),
        ((2 * TABLE, chans), BF16),
        ((rows, TABLE), BF16),
        ((rows, TABLE), BF16),
        ((cap + 2 * HALO, chans), BF16),
    ]


def fast_shards(
    bases, lengths, cotangent, c1, p1, c2, p2, embed
):
    cot = cotangent[0]
    me = (lax.axis_index("y") * 2 + lax.axis_index("x")) * 2 + lax.axis_index("core")
    where = jnp.stack([me.astype(jnp.int32), lax.axis_index("dp").astype(jnp.int32), lengths[0, 0]])
    cap, chans = cot.shape
    width = c1.shape[2]
    n_dp = lax.axis_size("dp")
    half = 3 * c2.shape[1] // 2
    narrow = jnp.concatenate([c1.reshape(-1, width), c2.reshape(-1, width)], axis=0)
    broad = jnp.concatenate([p2, p1, cot], axis=0)
    small = jnp.concatenate(
        [embed, jnp.pad(bases.astype(F32), ((0, 3), (0, chans - cap)))], axis=0
    )
    own, to_x, to_y, to_d = call(
        prep_kernel,
        [
            ((2 * half + HALO, chans), BF16),
            ((half + HALO, chans), BF16),
            ((half, chans), BF16),
            ((half + HALO, chans), BF16),
        ],
        [where, narrow, broad, small],
    )
    plane = [flip_move(to_x, "x"), flip_move(to_y, "y"), flip_move(to_d, "y", "x")]
    other = [xor_move(a[:half], "dp", 1) for a in plane]
    across = lambda arrays: [flip_move(a, "core") for a in arrays]
    rows = chans // 8
    sal, keep, send = call(
        tower_kernel_packed,
        [((4, cap), F32), ((4, rows, chans), F32), ((4, rows, chans), BF16)],
        [
            where, own, *across([own]), *plane, *across(plane), *other, *across(other),
            broad, small,
        ],
        scratch=[pltpu.VMEM(s, d) for s, d in table_shapes(cap, chans, width)]
        + [
            pltpu.VMEM((3, chans, width), BF16),
            pltpu.VMEM((width, chans), BF16),
            pltpu.VMEM((width, chans), BF16),
            pltpu.VMEM((8 + 2 * REACH, 8, 256), F32),
            pltpu.VMEM((8, 16, width), F32),
            pltpu.VMEM((8, 24, chans), F32),
            pltpu.VMEM((8, HALO, chans), BF16),
            pltpu.VMEM((8, rows, chans), F32),
        ],
        limit=40,
    )
    recv = flip_move(send, "core")
    own, *outs = call(
        core_sum_kernel,
        [((rows, chans), F32)] + [((rows, chans), BF16)] * 3,
        [where, keep, recv],
    )
    got = [flip_move(a, *axes) for a, axes in zip(outs, (("x",), ("y",), ("y", "x")))]
    part = rows // n_dp
    mine, *outs = call(
        plane_sum_kernel,
        [((2 * part, width), F32)] + [((2 * part, width), BF16)] * (n_dp - 1),
        [where, own, *got],
        scratch=[pltpu.VMEM((rows, chans), F32)],
    )
    got = [xor_move(a, "dp", n + 1) for n, a in enumerate(outs)]
    scale = 1.0 / math.sqrt(8 * n_dp * cap)
    (grad,) = call(
        functools.partial(last_sum_kernel, scale),
        [((part * chans // 128, 128), F32)],
        [mine, *got],
    )
    return sal[None], grad.reshape(-1)


def plain_shards(bases, lengths, cotangent, c1, p1, c2, p2, embed):
    cot = cotangent[0]
    where = jnp.stack(
        [
            lax.axis_index("seq").astype(jnp.int32),
            lax.axis_index("dp").astype(jnp.int32),
            lengths[0, 0],
        ]
    )
    cap, chans = cot.shape
    width = c1.shape[2]
    me, count = where[0], where[2]
    shard = c1.shape[1]
    own = lax.dynamic_slice_in_dim(embed, me * shard, shard, 1)
    act, slope = gelu_pair(own)
    taps = c1.astype(F32)
    high = lax.Precision.HIGHEST
    first = jnp.einsum("qc,kcb->kqb", act.astype(BF16).astype(F32), taps, precision=high)
    second = jnp.einsum("qc,dc,kcb->kqdb", slope, own, taps, precision=high)
    first = lax.psum(first.reshape(12, width), "seq")
    second = lax.psum(second.reshape(48, width), "seq")
    first = jnp.concatenate([first, jnp.zeros((4, width), F32)], axis=0)
    p1_full = lax.all_gather(p1, "seq", axis=0, tiled=True)
    p2_full = lax.all_gather(p2, "seq", axis=0, tiled=True)
    conv = lax.all_gather(c2, "seq", axis=1, tiled=True)
    info = jnp.concatenate(
        [bases.astype(F32), jnp.broadcast_to(count.astype(F32), (1, 128))], axis=1
    )
    info = lax.all_gather(info, "seq", axis=0, tiled=True)
    info = jnp.pad(info, ((REACH, REACH), (0, 0)))
    info = lax.dynamic_slice_in_dim(info, me, 2 * REACH + 1, 0)
    info = jnp.broadcast_to(info[:, None, :], (2 * REACH + 1, 8, cap + 128))
    padded = jnp.pad(cot, ((HALO, 0), (0, 0)))
    last = lax.dynamic_slice_in_dim(padded, count, HALO, 0)
    halos = [
        shift_move(last, 1, ("seq",)),
        shift_move(last[HALO - SPILL :], 2, ("seq",)),
        shift_move(cot[:HALO], -1, ("seq",)),
        shift_move(cot[:SPILL], -2, ("seq",)),
    ]
    b1, s1, a2, s2, hf, hr, cx = call(
        table_kernel_plain,
        table_shapes(cap, chans, width),
        [first, p1_full, info, cot, *halos, embed],
    )
    sal, grad = call(
        tower_kernel_plain,
        [((4, cap), F32), ((2 * width, chans), F32)],
        [where, conv, p2_full, second, p1_full, bases, cx, b1, s1, a2, s2, hf, hr, embed],
        limit=40,
    )
    scale = 1.0 / math.sqrt(lax.axis_size("seq") * lax.axis_size("dp") * cap)
    grad = lax.psum_scatter(
        grad.reshape(-1) * scale, ("seq", "dp"), scatter_dimension=0, tiled=True
    )
    return sal[None], grad


def solution(mesh):
    run, seq = plain_shards, "seq"
    if mesh.shape["seq"] == 8 and mesh.shape["dp"] == 4:
        run, seq = fast_shards, ("y", "x", "core")
        count = mesh.shape["dp"]
        mesh = jax.sharding.Mesh(mesh.devices.reshape(2, 2, 2, count), (*seq, "dp"))
    every = seq if isinstance(seq, tuple) else (seq,)
    in_specs = (
        P("dp", seq),
        P("dp", seq),
        P("dp", seq, None),
        P(None, seq, None),
        P(seq, None),
        P(None, seq, None),
        P(seq, None),
        P(),
    )
    out_specs = (P("dp", None, seq), P((*every, "dp")))
    return jax.shard_map(run, mesh=mesh, in_specs=in_specs, out_specs=out_specs, check_vma=False)
```

```python
import functools
import math

import jax
import jax.numpy as jnp
from jax import lax
from jax.experimental import pallas as pl
from jax.experimental.pallas import tpu as pltpu
from jax.sharding import PartitionSpec as P

FIRST_DILATION = 16
SECOND_DILATION = 64
HALO = FIRST_DILATION + SECOND_DILATION
SPILL = 16
REACH = 3
TABLE = 128
SQRT_HALF = 0.7071067811865476
INV_SQRT_TWO_PI = 0.3989422804014327
F32 = jnp.float32
BF16 = jnp.bfloat16
FAR = -100000.0


def gelu_pair(v):
    half = 0.5 * (1.0 + lax.erf(v * SQRT_HALF))
    return v * half, half + v * jnp.exp(-0.5 * v * v) * INV_SQRT_TWO_PI


def split(v):
    high = v.astype(BF16)
    return high, (v - high.astype(F32)).astype(BF16)


def mm(a, b):
    return lax.dot_general(a, b, (((1,), (0,)), ((), ())), preferred_element_type=F32)


def mm_nt(a, b):
    return lax.dot_general(a, b, (((1,), (1,)), ((), ())), preferred_element_type=F32)


def mm_tn(a, b):
    return lax.dot_general(a, b, (((0,), (0,)), ((), ())), preferred_element_type=F32)


def iota(shape, dim):
    return lax.broadcasted_iota(jnp.int32, shape, dim)


def spread(rows, index):
    out = jnp.broadcast_to(rows[0:1], (index.shape[0], rows.shape[1]))
    for q in range(1, 4):
        out = jnp.where(index == q, rows[q : q + 1], out)
    return out


def call(body, out_shapes, args, scratch=(), limit=24, cost=None, space=pltpu.VMEM):
    in_specs = [
        pl.BlockSpec(memory_space=pltpu.SMEM if a.dtype == jnp.int32 and a.ndim == 1 else space)
        for a in args
    ]
    return pl.pallas_call(
        body,
        out_shape=[jax.ShapeDtypeStruct(s, d) for s, d in out_shapes],
        in_specs=in_specs,
        out_specs=[pl.BlockSpec(memory_space=pltpu.VMEM)] * len(out_shapes),
        scratch_shapes=list(scratch),
        compiler_params=pltpu.CompilerParams(vmem_limit_bytes=limit * 1024 * 1024),
        cost_estimate=cost,
    )(*args)


def base_tables(emb, pick, conv):
    row = iota((16, 1), 0)
    low, high = row & 3, row >> 2
    by_low = spread(emb, low)
    by_high = spread(emb, high)
    act = gelu_pair(by_low)[0].astype(BF16)
    prod_high, prod_low = split(gelu_pair(by_high)[1] * by_low)
    own = mm(jnp.concatenate([act, prod_high, prod_low], axis=0), pick).astype(BF16)
    first = jnp.zeros((16, conv[0].shape[1]), F32)
    second = []
    for k in range(3):
        res = mm(own, conv[k])
        first = jnp.where(high == k, res[0:16], first)
        second.append(res[16:32] + res[32:48])
    return first, jnp.concatenate(second, axis=0)


def prep_kernel(
    where_ref, narrow_ref, broad_ref, small_ref,
    own_ref, x_ref, y_ref, d_ref,
):
    me, count = where_ref[0], where_ref[2]
    width = narrow_ref.shape[1]
    chans = 2 * width
    shard = narrow_ref.shape[0] // 6
    prows = width // 8
    cap = broad_ref.shape[0] - 2 * prows
    half = 3 * shard // 2
    cut = half - 16
    flat = narrow_ref.at[3 * shard : 6 * shard]
    cot = broad_ref[2 * prows :]
    pick = (iota((chans, shard), 0) == iota((chans, shard), 1) + me * shard).astype(BF16)
    taps = [narrow_ref[k * shard : (k + 1) * shard] for k in range(3)]
    first, second = base_tables(small_ref[0:4], pick, taps)
    f_high, f_low = split(first)
    info = jnp.concatenate(
        [
            small_ref[4:5, 0:cap],
            jnp.full((1, 128), count, jnp.int32).astype(F32),
            jnp.zeros((1, chans - cap - 128), F32),
        ],
        axis=1,
    )
    tail = jnp.concatenate([f_high.astype(F32), f_low.astype(F32)], axis=1)
    tail = jnp.where(iota((16, 1), 0) == 12, info, tail)
    wide = jnp.concatenate([second[0:24], second[24:48]], axis=1)
    extra = jnp.concatenate([info, jnp.zeros((7, chans), F32)], axis=0)
    own_ref[0:cut, 0:width] = flat[0:cut]
    own_ref[0:cut, width:chans] = flat[half : half + cut]
    own_ref[cut:half] = tail.astype(BF16)
    own_ref[half : half + 16, 0:width] = flat[cut:half]
    own_ref[half : half + 16, width:chans] = flat[half + cut : 2 * half]
    own_ref[half + 16 : half + 16 + 2 * prows] = broad_ref[0 : 2 * prows]
    own_ref[2 * half - 32 : 2 * half] = jnp.concatenate([wide, extra], axis=0).astype(BF16)
    part = own_ref[pl.ds(pl.multiple_of((where_ref[1] & 1) * half, 16), half), :]
    for out in (x_ref, y_ref, d_ref):
        out[0:half] = part
    take = (iota((HALO, cap), 1) == iota((HALO, cap), 0) + (count - HALO)).astype(BF16)
    last = mm(take, cot).astype(BF16)
    chip = me >> 1
    own_ref[2 * half :] = jnp.where((me & 1) == 0, last, cot[0:HALO])
    x_ref[half:] = jnp.where((chip ^ 1) > chip, last, cot[0:HALO])
    d_ref[half:] = jnp.where((chip ^ 3) > chip, last, cot[0:HALO])


def context_body(info_at, cot, r1, r2, l1, l2, hot_f_ref, hot_r_ref, cx_ref):
    cap = cot.shape[0]
    outer = HALO + SECOND_DILATION + FIRST_DILATION
    span = cap + 2 * outer
    counts = [info_at(o)[0:1, cap : cap + 128] for o in range(-REACH, REACH + 1)]
    begin = [None] * (2 * REACH + 1)
    begin[REACH] = jnp.zeros((1, 128), F32)
    for o in range(1, REACH + 1):
        begin[REACH + o] = begin[REACH + o - 1] + counts[REACH + o - 1]
        begin[REACH - o] = begin[REACH - o + 1] - counts[REACH - o]
    lane = iota((1, 128), 1).astype(F32)
    rowpos = (iota((span, 128), 0) - outer).astype(F32)
    total = jnp.zeros((span, 128), F32)
    for o in range(-REACH, REACH + 1):
        code = info_at(o)[0:1, 0:cap] + 1.0
        pos = jnp.where(lane < counts[REACH + o], begin[REACH + o] + lane, FAR)
        total = total + jnp.where(rowpos == pos, code, 0.0)
    codes = jnp.sum(total, axis=1, keepdims=True)
    d = FIRST_DILATION
    left, mid, right = codes[0 : span - 2 * d], codes[d : span - d], codes[2 * d : span]
    rows = span - 2 * d
    lanes = iota((rows, TABLE), 1).astype(F32)
    flip = lambda c: jnp.where(c == 0.0, 0.0, 5.0 - c)
    idx = jnp.where(mid == 0.0, -1.0, (mid - 1.0) * 25.0 + left * 5.0 + right)
    hot_f_ref[...] = (lanes == idx).astype(BF16)
    idx = jnp.where(mid == 0.0, -1.0, (4.0 - mid) * 25.0 + flip(right) * 5.0 + flip(left))
    hot_r_ref[...] = (lanes == idx).astype(BF16)

    own_n = counts[REACH]
    before_n, after_n = counts[REACH - 1], counts[REACH + 1]
    grow = cap + 2 * HALO
    lane_h = iota((1, HALO), 1).astype(F32)
    lane_s = iota((1, SPILL), 1).astype(F32)
    row_h = (iota((grow, HALO), 0) - HALO).astype(F32)
    row_s = (iota((grow, SPILL), 0) - HALO).astype(F32)
    row_o = (iota((grow, cap), 0) - HALO).astype(F32)
    own_pos = jnp.where(lane < own_n, lane, FAR)
    acc = mm((row_o == own_pos).astype(BF16), cot)
    pos = jnp.where(lane_h >= HALO - before_n[:, 0:HALO], lane_h - HALO, FAR)
    acc = acc + mm((row_h == pos).astype(BF16), r1)
    pos = jnp.where(
        counts[REACH - 2][:, 0:SPILL] > 0.0, lane_s - SPILL - before_n[:, 0:SPILL], FAR
    )
    acc = acc + mm((row_s == pos).astype(BF16), r2)
    pos = jnp.where(lane_h < after_n[:, 0:HALO], lane_h + own_n[:, 0:HALO], FAR)
    acc = acc + mm((row_h == pos).astype(BF16), l1)
    pos = jnp.where(
        (counts[REACH + 2][:, 0:SPILL] > 0.0) & (after_n[:, 0:SPILL] < HALO),
        lane_s + own_n[:, 0:SPILL] + after_n[:, 0:SPILL],
        FAR,
    )
    acc = acc + mm((row_s == pos).astype(BF16), l2)
    cx_ref[...] = (0.5 * acc).astype(BF16)


def context_kernel_plain(info_ref, cot_ref, r1_ref, r2_ref, l1_ref, l2_ref, *outs):
    context_body(
        lambda o: info_ref[REACH + o], cot_ref[...], r1_ref[...], r2_ref[...], l1_ref[...],
        l2_ref[...], *outs,
    )


def context_kernel_packed(where_ref, *refs):
    parts, broad_ref, outs = refs[0:8], refs[8], refs[9:12]
    info_ref, halo_ref = refs[12:]
    me, odd = where_ref[0], where_ref[1] & 1
    chip, core = me >> 1, me & 1
    chans = broad_ref.shape[1]
    prow = chans // 16
    half = 3 * chans // 16
    info_ref[0:REACH] = jnp.zeros((REACH, 8, 256), F32)
    info_ref[REACH + 8 :] = jnp.zeros((REACH, 8, 256), F32)
    for n, part in enumerate(parts):
        peer = me ^ (2 * (n % 4) + n // 4)
        low = part[half - 16 : half].astype(F32)[12:13, 0:256]
        if n % 4 > 0:
            high = part[half - 16 : half].astype(F32)[8:9, 0:256]
            low = jnp.where(odd == 0, low, high)
        info_ref[REACH + peer] = jnp.broadcast_to(low, (8, 256))
    for n in range(2):
        halo_ref[4 * n + chip] = parts[4 * n][2 * half :]
        halo_ref[4 * n + (chip ^ 1)] = parts[4 * n + 1][half:]
        halo_ref[4 * n + (chip ^ 3)] = parts[4 * n + 3][half:]
    r1 = halo_ref[4 + jnp.maximum(chip + core - 1, 0)]
    l1 = halo_ref[4 + jnp.minimum(chip + core, 3)]
    r2 = halo_ref[jnp.maximum(chip - 1, 0)]
    l2 = halo_ref[jnp.minimum(chip + 1, 3)]
    context_body(
        lambda o: info_ref[me + (REACH + o)], broad_ref[2 * prow :], r1, r2[HALO - SPILL :], l1,
        l2[0:SPILL], *outs,
    )


def tower_body(
    first, project, conv, p2, count, emb, cap, cx_ref, hot_f_ref, hot_r_ref,
    s1_ref, gb_ref, g_ref, put,
):
    entry = iota((TABLE, 1), 0)
    by25 = (entry * 1311) >> 15
    by5 = (entry * 6554) >> 15
    in_left = by5 - 5 * by25
    in_right = entry - 5 * by5
    sums = jnp.zeros((TABLE, first.shape[1]), F32)
    for q in range(4):
        sums = jnp.where(in_left == q + 1, first[q : q + 1], sums)
    sums = sums + spread(first[4:8], by25)
    after = jnp.zeros((TABLE, first.shape[1]), F32)
    for q in range(4):
        after = jnp.where(in_right == q + 1, first[8 + q : 9 + q], after)
    value, slope = gelu_pair(sums + after)
    b1 = value.astype(BF16)
    high, low = split(slope)
    s1_ref[0:TABLE] = high
    s1_ref[TABLE : 2 * TABLE] = low
    stream = spread(emb, by25) + mm(b1, project)
    value, slope = gelu_pair(stream)
    a2 = value.astype(BF16)
    s2 = jnp.concatenate(split(slope), axis=0)

    grow = cap + 2 * HALO
    inner = cap + 2 * FIRST_DILATION
    d, D = FIRST_DILATION, SECOND_DILATION
    cx = cx_ref[...]
    back_mid = mm_nt(cx, p2)
    before = jnp.zeros((2 * grow, p2.shape[0]), F32)
    for k in range(3):
        taps = jnp.concatenate(split(mm(a2, conv(k))), axis=0)
        hot = jnp.concatenate(
            [hot_f_ref[k * D : k * D + grow], hot_r_ref[(2 - k) * D : (2 - k) * D + grow]], axis=0
        )
        before = before + mm(jnp.concatenate([hot, hot], axis=1), taps)
    value, slope = gelu_pair(before)
    own_col = (iota((cap, 1), 0) < count).astype(F32)
    own_gb = (cx[HALO : HALO + cap].astype(F32) * own_col).astype(BF16)
    mids = jnp.concatenate(
        [value[HALO : HALO + cap], value[grow + HALO : grow + HALO + cap]], axis=0
    ).astype(BF16)
    put(1, mm_tn(mids, jnp.concatenate([own_gb, own_gb], axis=0)))
    grad_f = (back_mid * slope[0:grow]).astype(BF16)
    grad_r = (back_mid * slope[grow:]).astype(BF16)
    ga = jnp.zeros((2 * inner, cx.shape[1]), F32)
    for k in range(3):
        rows = jnp.concatenate(
            [grad_f[(2 - k) * D : (2 - k) * D + inner], grad_r[k * D : k * D + inner]], axis=0
        )
        ga = ga + mm_nt(rows, conv(k))
    hot = jnp.concatenate(
        [hot_f_ref[2 * D : 2 * D + inner], hot_r_ref[2 * D : 2 * D + inner]], axis=0
    )
    base_g = cx[D : D + inner].astype(F32)
    g = jnp.concatenate([base_g, base_g], axis=0) + ga * mm(
        jnp.concatenate([hot, hot], axis=1), s2
    )
    gb = g.astype(BF16)
    gb_ref[...] = gb
    g_ref[0:cap] = g[d : d + cap]
    g_ref[cap : 2 * cap] = g[inner + d : inner + d + cap]
    col = jnp.concatenate([own_col, own_col], axis=0)
    own_hot = jnp.concatenate([hot[d : d + cap], hot[inner + d : inner + d + cap]], axis=0)
    own_b1 = mm((own_hot.astype(F32) * col).astype(BF16), b1).astype(BF16)
    own_g = jnp.concatenate([gb[d : d + cap], gb[inner + d : inner + d + cap]], axis=0)
    put(0, mm_tn(own_b1, own_g))


def saliency_kernel(
    where_ref, small_ref, hot_f_ref, hot_r_ref, s1_ref, gb_ref, g_ref, second_ref, p1_ref, sal_ref
):
    count = where_ref[2]
    cap = g_ref.shape[0] // 2
    inner = cap + 2 * FIRST_DILATION
    d, D = FIRST_DILATION, SECOND_DILATION
    hot = jnp.concatenate(
        [hot_f_ref[2 * D : 2 * D + inner], hot_r_ref[2 * D : 2 * D + inner]], axis=0
    )
    slope = mm(jnp.concatenate([hot, hot], axis=1), s1_ref[...])
    gh = (mm_nt(gb_ref[...], p1_ref[...]) * slope).astype(BF16)
    emb = small_ref[0:4]
    bases = small_ref[4:5, 0:cap]
    wide = jnp.concatenate(split(second_ref[...]), axis=0)
    total = jnp.zeros((4, cap), F32)
    e_high, e_low = split(jnp.concatenate([emb, emb], axis=0))
    for turn in range(2):
        g_high, g_low = split(g_ref[turn * cap : (turn + 1) * cap])
        got = mm_nt(e_high, g_high) + mm_nt(e_high, g_low) + mm_nt(e_low, g_high)
        got = got[0:4]
        table = jnp.zeros((16, cap), F32)
        for k in range(3):
            place = 2 - k if turn == 0 else k
            at = turn * inner + place * d
            both = mm_nt(
                jnp.concatenate(
                    [wide[16 * k : 16 * k + 16], wide[48 + 16 * k : 64 + 16 * k]], axis=0
                ),
                gh[at : at + cap],
            )
            table = table + both[0:16] + both[16:32]
        for q in range(4):
            code = float(q if turn == 0 else 3 - q)
            got = got + jnp.where(bases == code, table[4 * q : 4 * q + 4], 0.0)
        if turn == 1:
            got = jnp.concatenate([got[3 - c : 4 - c] for c in range(4)], axis=0)
        total = total + got
    live = iota((1, cap), 1) < count
    sal_ref[...] = jnp.where(live, total * (1.0 / math.sqrt(emb.shape[1])), 0.0)


def tower_kernel_packed(where_ref, *refs):
    own_parts, plane_parts, dp_parts = refs[0:2], refs[2:8], refs[8:14]
    small_ref, cx_ref, hf_ref, hr_ref = refs[14:18]
    keep_ref, send_ref, s1_ref, gb_ref, g_ref, wide_ref, p1_ref = refs[18:25]
    conv_ref, p2_ref, first_ref, second_ref = refs[25:]
    me, count = where_ref[0], where_ref[2]
    core, odd = me & 1, where_ref[1] & 1
    width, chans = p1_ref.shape
    shard = chans // 8
    prow = width // 8
    half = 3 * shard // 2
    cut = half - 16

    def place(side, rows, peer):
        at = peer * shard

        def lay(k, start, size, source, lane):
            conv_ref[k, pl.ds(pl.multiple_of(at + start, 16), size), :] = rows(
                source, size
            )[:, lane : lane + width]

        if side == 0:
            lay(0, 0, shard, 0, 0)
            lay(1, 0, cut - shard, shard, 0)
            lay(1, shard // 2, shard // 2, 0, width)
            lay(2, 0, cut - shard // 2, shard // 2, width)
            tail = rows(cut, 16).astype(F32)
            first_ref[peer] = tail[:, 0:width] + tail[:, width:]
        else:
            lay(1, cut - shard, 16, 0, 0)
            lay(2, shard - 16, 16, 0, width)
            to = pl.ds(pl.multiple_of(peer * prow, 16), prow)
            p2_ref[to, :] = rows(16, prow)
            p1_ref[to, :] = rows(16 + prow, prow)
            second_ref[peer] = rows(half - 32, 32).astype(F32)[0:24]

    for n in range(2):
        for side in range(2):
            rows = lambda a, size, n=n, side=side: own_parts[n][
                side * half + a : side * half + a + size
            ]
            place(side, rows, me ^ n)
    for parity in range(2):

        @pl.when(odd == parity)
        def _():
            for n in range(6):
                peer = me ^ (2 * (n % 3 + 1) + n // 3)
                for side, part in ((parity, plane_parts[n]), (1 - parity, dp_parts[n])):
                    rows = lambda a, size, part=part: part[a : a + size]
                    place(side, rows, peer)

    first = first_ref[0]
    wide = second_ref[0]
    for peer in range(1, 8):
        first = first + first_ref[peer]
        wide = wide + second_ref[peer]
    wide_ref[...] = jnp.concatenate([wide[:, 0:width], wide[:, width : 2 * width]], axis=0)

    def put(block, value):
        rows = value.shape[0] // 4
        for c in range(2):
            even = value[2 * c * rows : (2 * c + 1) * rows]
            uneven = value[(2 * c + 1) * rows : (2 * c + 2) * rows]
            keep_ref[2 * block + c] = jnp.where(core == 0, even, uneven)
            send_ref[2 * block + c] = jnp.where(core == 0, uneven, even).astype(BF16)

    tower_body(
        first, p1_ref[...], lambda k: conv_ref[k], p2_ref[...], count, small_ref[0:4],
        g_ref.shape[0] // 2, cx_ref, hf_ref, hr_ref, s1_ref, gb_ref, g_ref, put,
    )


def tower_kernel_plain(
    where_ref, first_ref, p1_ref, conv_ref, p2_ref, small_ref, cx_ref, hf_ref, hr_ref,
    grad_ref, s1_ref, gb_ref, g_ref,
):
    def put(block, value):
        rows = value.shape[0]
        grad_ref[block * rows : (block + 1) * rows] = value

    tower_body(
        first_ref[...], p1_ref[...], lambda k: conv_ref[k], p2_ref[...], where_ref[2],
        small_ref[0:4], g_ref.shape[0] // 2, cx_ref, hf_ref, hr_ref, s1_ref, gb_ref, g_ref, put,
    )


def fold(value):
    width = value.shape[1] // 2
    return jnp.concatenate([value[:, 0:width], value[:, width:]], axis=0)


def core_sum_kernel(where_ref, keep_ref, recv_ref, own_ref, *outs):
    chip = where_ref[0] >> 1
    own_ref[...] = keep_ref[chip] + recv_ref[chip].astype(F32)
    for n, out in enumerate(outs):
        at = chip ^ (n + 1)
        out[...] = (keep_ref[at] + recv_ref[at].astype(F32)).astype(BF16)


def plane_sum_kernel(where_ref, own_ref, x_ref, y_ref, d_ref, mine_ref, *refs):
    outs, sum_ref = refs[:-1], refs[-1]
    sum_ref[...] = (
        own_ref[...] + x_ref[...].astype(F32) + y_ref[...].astype(F32) + d_ref[...].astype(F32)
    )
    z = where_ref[1]
    rows = mine_ref.shape[0] // 2
    mine_ref[...] = fold(sum_ref[pl.ds(pl.multiple_of(z * rows, 8), rows), :])
    for n, out in enumerate(outs):
        at = pl.multiple_of((z ^ (n + 1)) * rows, 8)
        out[...] = fold(sum_ref[pl.ds(at, rows), :]).astype(BF16)


def last_sum_kernel(scale, mine_ref, *refs):
    out_ref = refs[-1]
    total = mine_ref[...]
    for ref in refs[:-1]:
        total = total + ref[...].astype(F32)
    total = total * scale
    rows, half = total.shape[0] // 2, total.shape[1] // 128
    for n in range(2 * half):
        at = rows * (n // half)
        lane = 128 * (n % half)
        out_ref[pl.ds(n, rows, stride=2 * half), :] = total[at : at + rows, lane : lane + 128]


def flip_move(array, *axes):
    sizes = [lax.axis_size(a) for a in axes]
    size = math.prod(sizes)
    return lax.ppermute(array, axes, [(i, size - 1 - i) for i in range(size)])


def xor_move(array, axis, bits):
    return lax.ppermute(array, axis, [(i, i ^ bits) for i in range(lax.axis_size(axis))])


def shift_move(array, by, axes):
    size = math.prod(lax.axis_size(a) for a in axes)
    return lax.ppermute(array, axes, [(i, i + by) for i in range(size) if 0 <= i + by < size])


def context_shapes(cap, chans):
    rows = cap + 2 * (HALO + SECOND_DILATION)
    return [((rows, TABLE), BF16), ((rows, TABLE), BF16), ((cap + 2 * HALO, chans), BF16)]


def pass_shapes(cap, chans, width):
    inner = cap + 2 * FIRST_DILATION
    return [((2 * TABLE, width), BF16), ((2 * inner, chans), BF16), ((2 * cap, chans), F32)]


def lines(embed, bases):
    cap, chans = bases.shape[1], embed.shape[1]
    extra = jnp.pad(bases.astype(F32), ((0, 3), (0, chans - cap)))
    return jnp.concatenate([embed, extra], axis=0)


def weight(flops):
    return pl.CostEstimate(flops=flops, bytes_accessed=10**6, transcendentals=0)


def fast_shards(
    bases, lengths, cotangent, c1, p1, c2, p2, embed
):
    cot = cotangent[0]
    me = (lax.axis_index("y") * 2 + lax.axis_index("x")) * 2 + lax.axis_index("core")
    where = jnp.stack([me.astype(jnp.int32), lax.axis_index("dp").astype(jnp.int32), lengths[0, 0]])
    cap, chans = cot.shape
    width = c1.shape[2]
    n_dp = lax.axis_size("dp")
    half = 3 * c2.shape[1] // 2
    narrow = jnp.concatenate([c1.reshape(-1, width), c2.reshape(-1, width)], axis=0)
    broad = jnp.concatenate([p2, p1, cot], axis=0)
    small = lines(embed, bases)
    own, to_x, to_y, to_d = call(
        prep_kernel,
        [
            ((2 * half + HALO, chans), BF16),
            ((half + HALO, chans), BF16),
            ((half, chans), BF16),
            ((half + HALO, chans), BF16),
        ],
        [where, narrow, broad, small],
    )
    plane = [flip_move(to_x, "x"), flip_move(to_y, "y"), flip_move(to_d, "y", "x")]
    other = [xor_move(a[:half], "dp", 1) for a in plane]
    across = lambda arrays: [flip_move(a, "core") for a in arrays]
    rows = chans // 8
    swapped = across([own, *plane])
    hf, hr, cx = call(
        context_kernel_packed,
        context_shapes(cap, chans),
        [where, own, *plane, *swapped, broad],
        scratch=[
            pltpu.VMEM((8 + 2 * REACH, 8, 256), F32),
            pltpu.VMEM((8, HALO, chans), BF16),
        ],
        cost=weight(10**9),
    )
    keep, send, s1, gb, g, second, p1_full = call(
        tower_kernel_packed,
        [((4, rows, chans), F32), ((4, rows, chans), BF16), *pass_shapes(cap, chans, width)]
        + [((48, width), F32), ((width, chans), BF16)],
        [
            where, own, swapped[0], *plane, *swapped[1:], *other, *across(other),
            small, cx, hf, hr,
        ],
        scratch=[
            pltpu.VMEM((3, chans, width), BF16),
            pltpu.VMEM((width, chans), BF16),
            pltpu.VMEM((8, 16, width), F32),
            pltpu.VMEM((8, 24, chans), F32),
        ],
        limit=40,
        cost=weight(4 * 10**9),
    )
    recv = flip_move(send, "core")
    (sal,) = call(
        saliency_kernel,
        [((4, cap), F32)],
        [where, small, hf, hr, s1, gb, g, second, p1_full],
        cost=weight(10**9),
    )
    own, *outs = call(
        core_sum_kernel,
        [((rows, chans), F32)] + [((rows, chans), BF16)] * 3,
        [where, keep, recv],
    )
    got = [flip_move(a, *axes) for a, axes in zip(outs, (("x",), ("y",), ("y", "x")))]
    part = rows // n_dp
    mine, *outs = call(
        plane_sum_kernel,
        [((2 * part, width), F32)] + [((2 * part, width), BF16)] * (n_dp - 1),
        [where, own, *got],
        scratch=[pltpu.VMEM((rows, chans), F32)],
    )
    got = [xor_move(a, "dp", n + 1) for n, a in enumerate(outs)]
    scale = 1.0 / math.sqrt(8 * n_dp * cap)
    (grad,) = call(
        functools.partial(last_sum_kernel, scale),
        [((part * chans // 128, 128), F32)],
        [mine, *got],
    )
    return sal[None], grad.reshape(-1)


def plain_shards(bases, lengths, cotangent, c1, p1, c2, p2, embed):
    cot = cotangent[0]
    where = jnp.stack(
        [
            lax.axis_index("seq").astype(jnp.int32),
            lax.axis_index("dp").astype(jnp.int32),
            lengths[0, 0],
        ]
    )
    cap, chans = cot.shape
    width = c1.shape[2]
    me, count = where[0], where[2]
    shard = c1.shape[1]
    own = lax.dynamic_slice_in_dim(embed, me * shard, shard, 1)
    act, slope = gelu_pair(own)
    taps = c1.astype(F32)
    high = lax.Precision.HIGHEST
    first = jnp.einsum("qc,kcb->kqb", act.astype(BF16).astype(F32), taps, precision=high)
    second = jnp.einsum("qc,dc,kcb->kqdb", slope, own, taps, precision=high)
    first = lax.psum(first.reshape(12, width), "seq")
    second = lax.psum(second.reshape(48, width), "seq")
    first = jnp.concatenate([first, jnp.zeros((4, width), F32)], axis=0)
    p1_full = lax.all_gather(p1, "seq", axis=0, tiled=True)
    p2_full = lax.all_gather(p2, "seq", axis=0, tiled=True)
    conv = lax.all_gather(c2, "seq", axis=1, tiled=True)
    info = jnp.concatenate(
        [bases.astype(F32), jnp.broadcast_to(count.astype(F32), (1, 128))], axis=1
    )
    info = lax.all_gather(info, "seq", axis=0, tiled=True)
    info = jnp.pad(info, ((REACH, REACH), (0, 0)))
    info = lax.dynamic_slice_in_dim(info, me, 2 * REACH + 1, 0)
    info = jnp.broadcast_to(info[:, None, :], (2 * REACH + 1, 8, cap + 128))
    padded = jnp.pad(cot, ((HALO, 0), (0, 0)))
    last = lax.dynamic_slice_in_dim(padded, count, HALO, 0)
    halos = [
        shift_move(last, 1, ("seq",)),
        shift_move(last[HALO - SPILL :], 2, ("seq",)),
        shift_move(cot[:HALO], -1, ("seq",)),
        shift_move(cot[:SPILL], -2, ("seq",)),
    ]
    small = lines(embed, bases)
    hf, hr, cx = call(
        context_kernel_plain, context_shapes(cap, chans), [info, cot, *halos]
    )
    grad, s1, gb, g = call(
        tower_kernel_plain,
        [((2 * width, chans), F32), *pass_shapes(cap, chans, width)],
        [where, first, p1_full, conv, p2_full, small, cx, hf, hr],
        limit=40,
    )
    (sal,) = call(
        saliency_kernel,
        [((4, cap), F32)],
        [where, small, hf, hr, s1, gb, g, second, p1_full],
    )
    scale = 1.0 / math.sqrt(lax.axis_size("seq") * lax.axis_size("dp") * cap)
    grad = lax.psum_scatter(
        grad.reshape(-1) * scale, ("seq", "dp"), scatter_dimension=0, tiled=True
    )
    return sal[None], grad


def solution(mesh):
    run, seq = plain_shards, "seq"
    if mesh.shape["seq"] == 8 and mesh.shape["dp"] == 4:
        run, seq = fast_shards, ("y", "x", "core")
        count = mesh.shape["dp"]
        mesh = jax.sharding.Mesh(mesh.devices.reshape(2, 2, 2, count), (*seq, "dp"))
    every = seq if isinstance(seq, tuple) else (seq,)
    in_specs = (
        P("dp", seq),
        P("dp", seq),
        P("dp", seq, None),
        P(None, seq, None),
        P(seq, None),
        P(None, seq, None),
        P(seq, None),
        P(),
    )
    out_specs = (P("dp", None, seq), P((*every, "dp")))
    return jax.shard_map(run, mesh=mesh, in_specs=in_specs, out_specs=out_specs, check_vma=False)
```

```python
import functools
import math

import jax
import jax.numpy as jnp
from jax import lax
from jax.experimental import pallas as pl
from jax.experimental.pallas import tpu as pltpu
from jax.sharding import PartitionSpec as P

FIRST_DILATION = 16
SECOND_DILATION = 64
HALO = FIRST_DILATION + SECOND_DILATION
SPILL = 16
REACH = 3
TABLE = 128
SQRT_HALF = 0.7071067811865476
INV_SQRT_TWO_PI = 0.3989422804014327
F32 = jnp.float32
BF16 = jnp.bfloat16
FAR = -100000.0


def gelu_pair(v):
    half = 0.5 * (1.0 + lax.erf(v * SQRT_HALF))
    return v * half, half + v * jnp.exp(-0.5 * v * v) * INV_SQRT_TWO_PI


def split(v):
    high = v.astype(BF16)
    return high, (v - high.astype(F32)).astype(BF16)


def mm(a, b):
    return lax.dot_general(a, b, (((1,), (0,)), ((), ())), preferred_element_type=F32)


def mm_nt(a, b):
    return lax.dot_general(a, b, (((1,), (1,)), ((), ())), preferred_element_type=F32)


def mm_tn(a, b):
    return lax.dot_general(a, b, (((0,), (0,)), ((), ())), preferred_element_type=F32)


def iota(shape, dim):
    return lax.broadcasted_iota(jnp.int32, shape, dim)


def spread(rows, index):
    out = jnp.broadcast_to(rows[0:1], (index.shape[0], rows.shape[1]))
    for q in range(1, 4):
        out = jnp.where(index == q, rows[q : q + 1], out)
    return out


def call(body, out_shapes, args, scratch=(), limit=24, cost=None, space=pltpu.VMEM):
    in_specs = [
        pl.BlockSpec(memory_space=pltpu.SMEM if a.dtype == jnp.int32 and a.ndim == 1 else space)
        for a in args
    ]
    return pl.pallas_call(
        body,
        out_shape=[jax.ShapeDtypeStruct(s, d) for s, d in out_shapes],
        in_specs=in_specs,
        out_specs=[pl.BlockSpec(memory_space=pltpu.VMEM)] * len(out_shapes),
        scratch_shapes=list(scratch),
        compiler_params=pltpu.CompilerParams(vmem_limit_bytes=limit * 1024 * 1024),
        cost_estimate=cost,
    )(*args)


def base_tables(emb, pick, conv):
    row = iota((16, 1), 0)
    low, high = row & 3, row >> 2
    by_low = spread(emb, low)
    by_high = spread(emb, high)
    act = gelu_pair(by_low)[0].astype(BF16)
    prod_high, prod_low = split(gelu_pair(by_high)[1] * by_low)
    own = mm(jnp.concatenate([act, prod_high, prod_low], axis=0), pick).astype(BF16)
    first = jnp.zeros((16, conv[0].shape[1]), F32)
    second = []
    for k in range(3):
        res = mm(own, conv[k])
        first = jnp.where(high == k, res[0:16], first)
        second.append(res[16:32] + res[32:48])
    return first, jnp.concatenate(second, axis=0)


def prep_kernel(
    where_ref, narrow_ref, broad_ref, small_ref,
    own_ref, half_ref,
):
    me, count = where_ref[0], where_ref[2]
    width = narrow_ref.shape[1]
    chans = 2 * width
    shard = narrow_ref.shape[0] // 6
    prows = width // 8
    cap = broad_ref.shape[0] - 2 * prows
    half = 3 * shard // 2
    cut = half - 16
    flat = narrow_ref.at[3 * shard : 6 * shard]
    cot = broad_ref[2 * prows :]
    pick = (iota((chans, shard), 0) == iota((chans, shard), 1) + me * shard).astype(BF16)
    taps = [narrow_ref[k * shard : (k + 1) * shard] for k in range(3)]
    first, second = base_tables(small_ref[0:4], pick, taps)
    f_high, f_low = split(first)
    info = jnp.concatenate(
        [
            small_ref[4:5, 0:cap],
            jnp.full((1, 128), count, jnp.int32).astype(F32),
            jnp.zeros((1, chans - cap - 128), F32),
        ],
        axis=1,
    )
    tail = jnp.concatenate([f_high.astype(F32), f_low.astype(F32)], axis=1)
    tail = jnp.where(iota((16, 1), 0) == 12, info, tail)
    wide = jnp.concatenate([second[0:24], second[24:48]], axis=1)
    extra = jnp.concatenate([info, jnp.zeros((7, chans), F32)], axis=0)
    own_ref[0:cut, 0:width] = flat[0:cut]
    own_ref[0:cut, width:chans] = flat[half : half + cut]
    own_ref[cut:half] = tail.astype(BF16)
    own_ref[half : half + 16, 0:width] = flat[cut:half]
    own_ref[half : half + 16, width:chans] = flat[half + cut : 2 * half]
    own_ref[half + 16 : half + 16 + 2 * prows] = broad_ref[0 : 2 * prows]
    own_ref[2 * half - 32 : 2 * half] = jnp.concatenate([wide, extra], axis=0).astype(BF16)
    half_ref[...] = own_ref[pl.ds(pl.multiple_of((where_ref[1] & 1) * half, 16), half), :]
    first, last = edges(cot, count)
    own_ref[2 * half :] = jnp.where((me & 1) == 0, last, first)


def edges(cot, count):
    cap = cot.shape[0]
    take = (iota((HALO, cap), 1) == iota((HALO, cap), 0) + (count - HALO)).astype(BF16)
    return cot[0:HALO], mm(take, cot).astype(BF16)


def halo_kernel(where_ref, broad_ref, after_ref, x_ref, d_ref):
    del after_ref
    chip = where_ref[0] >> 1
    first, last = edges(broad_ref[broad_ref.shape[1] // 8 :], where_ref[2])
    x_ref[...] = jnp.where((chip ^ 1) > chip, last, first)
    d_ref[...] = jnp.where((chip ^ 3) > chip, last, first)


def context_body(info_at, cot, r1, r2, l1, l2, hot_f_ref, hot_r_ref, cx_ref):
    cap = cot.shape[0]
    outer = HALO + SECOND_DILATION + FIRST_DILATION
    span = cap + 2 * outer
    counts = [info_at(o)[0:1, cap : cap + 128] for o in range(-REACH, REACH + 1)]
    begin = [None] * (2 * REACH + 1)
    begin[REACH] = jnp.zeros((1, 128), F32)
    for o in range(1, REACH + 1):
        begin[REACH + o] = begin[REACH + o - 1] + counts[REACH + o - 1]
        begin[REACH - o] = begin[REACH - o + 1] - counts[REACH - o]
    lane = iota((1, 128), 1).astype(F32)
    rowpos = (iota((span, 128), 0) - outer).astype(F32)
    total = jnp.zeros((span, 128), F32)
    for o in range(-REACH, REACH + 1):
        code = info_at(o)[0:1, 0:cap] + 1.0
        pos = jnp.where(lane < counts[REACH + o], begin[REACH + o] + lane, FAR)
        total = total + jnp.where(rowpos == pos, code, 0.0)
    codes = jnp.sum(total, axis=1, keepdims=True)
    d = FIRST_DILATION
    left, mid, right = codes[0 : span - 2 * d], codes[d : span - d], codes[2 * d : span]
    rows = span - 2 * d
    lanes = iota((rows, TABLE), 1).astype(F32)
    flip = lambda c: jnp.where(c == 0.0, 0.0, 5.0 - c)
    idx = jnp.where(mid == 0.0, -1.0, (mid - 1.0) * 25.0 + left * 5.0 + right)
    hot_f_ref[...] = (lanes == idx).astype(BF16)
    idx = jnp.where(mid == 0.0, -1.0, (4.0 - mid) * 25.0 + flip(right) * 5.0 + flip(left))
    hot_r_ref[...] = (lanes == idx).astype(BF16)

    own_n = counts[REACH]
    before_n, after_n = counts[REACH - 1], counts[REACH + 1]
    grow = cap + 2 * HALO
    lane_h = iota((1, HALO), 1).astype(F32)
    lane_s = iota((1, SPILL), 1).astype(F32)
    row_h = (iota((grow, HALO), 0) - HALO).astype(F32)
    row_s = (iota((grow, SPILL), 0) - HALO).astype(F32)
    row_o = (iota((grow, cap), 0) - HALO).astype(F32)
    own_pos = jnp.where(lane < own_n, lane, FAR)
    acc = mm((row_o == own_pos).astype(BF16), cot)
    pos = jnp.where(lane_h >= HALO - before_n[:, 0:HALO], lane_h - HALO, FAR)
    acc = acc + mm((row_h == pos).astype(BF16), r1)
    pos = jnp.where(
        counts[REACH - 2][:, 0:SPILL] > 0.0, lane_s - SPILL - before_n[:, 0:SPILL], FAR
    )
    acc = acc + mm((row_s == pos).astype(BF16), r2)
    pos = jnp.where(lane_h < after_n[:, 0:HALO], lane_h + own_n[:, 0:HALO], FAR)
    acc = acc + mm((row_h == pos).astype(BF16), l1)
    pos = jnp.where(
        (counts[REACH + 2][:, 0:SPILL] > 0.0) & (after_n[:, 0:SPILL] < HALO),
        lane_s + own_n[:, 0:SPILL] + after_n[:, 0:SPILL],
        FAR,
    )
    acc = acc + mm((row_s == pos).astype(BF16), l2)
    cx_ref[...] = (0.5 * acc).astype(BF16)


def context_kernel_plain(info_ref, cot_ref, r1_ref, r2_ref, l1_ref, l2_ref, *outs):
    context_body(
        lambda o: info_ref[REACH + o], cot_ref[...], r1_ref[...], r2_ref[...], l1_ref[...],
        l2_ref[...], *outs,
    )


def context_kernel_packed(where_ref, *refs):
    parts, far_parts, broad_ref, outs = refs[0:8], refs[8:12], refs[12], refs[13:16]
    info_ref, halo_ref = refs[16:]
    me, odd = where_ref[0], where_ref[1] & 1
    chip, core = me >> 1, me & 1
    chans = broad_ref.shape[1]
    prow = chans // 16
    half = 3 * chans // 16
    info_ref[0:REACH] = jnp.zeros((REACH, 8, 256), F32)
    info_ref[REACH + 8 :] = jnp.zeros((REACH, 8, 256), F32)
    for n, part in enumerate(parts):
        peer = me ^ (2 * (n % 4) + n // 4)
        low = part[half - 16 : half].astype(F32)[12:13, 0:256]
        if n % 4 > 0:
            high = part[half - 16 : half].astype(F32)[8:9, 0:256]
            low = jnp.where(odd == 0, low, high)
        info_ref[REACH + peer] = jnp.broadcast_to(low, (8, 256))
    for n in range(2):
        halo_ref[4 * n + chip] = parts[4 * n][2 * half :]
        halo_ref[4 * n + (chip ^ 1)] = far_parts[2 * n][...]
        halo_ref[4 * n + (chip ^ 3)] = far_parts[2 * n + 1][...]
    r1 = halo_ref[4 + jnp.maximum(chip + core - 1, 0)]
    l1 = halo_ref[4 + jnp.minimum(chip + core, 3)]
    r2 = halo_ref[jnp.maximum(chip - 1, 0)]
    l2 = halo_ref[jnp.minimum(chip + 1, 3)]
    context_body(
        lambda o: info_ref[me + (REACH + o)], broad_ref[2 * prow :], r1, r2[HALO - SPILL :], l1,
        l2[0:SPILL], *outs,
    )


def tower_body(
    first, project, conv, p2, count, emb, cap, cx_ref, hot_f_ref, hot_r_ref,
    s1_ref, gb_ref, g_ref, put,
):
    entry = iota((TABLE, 1), 0)
    by25 = (entry * 1311) >> 15
    by5 = (entry * 6554) >> 15
    in_left = by5 - 5 * by25
    in_right = entry - 5 * by5
    sums = jnp.zeros((TABLE, first.shape[1]), F32)
    for q in range(4):
        sums = jnp.where(in_left == q + 1, first[q : q + 1], sums)
    sums = sums + spread(first[4:8], by25)
    after = jnp.zeros((TABLE, first.shape[1]), F32)
    for q in range(4):
        after = jnp.where(in_right == q + 1, first[8 + q : 9 + q], after)
    value, slope = gelu_pair(sums + after)
    b1 = value.astype(BF16)
    high, low = split(slope)
    s1_ref[0:TABLE] = high
    s1_ref[TABLE : 2 * TABLE] = low
    stream = spread(emb, by25) + mm(b1, project)
    value, slope = gelu_pair(stream)
    a2 = value.astype(BF16)
    s2 = jnp.concatenate(split(slope), axis=0)

    grow = cap + 2 * HALO
    inner = cap + 2 * FIRST_DILATION
    d, D = FIRST_DILATION, SECOND_DILATION
    cx = cx_ref[...]
    back_mid = mm_nt(cx, p2)
    before = jnp.zeros((2 * grow, p2.shape[0]), F32)
    for k in range(3):
        taps = jnp.concatenate(split(mm(a2, conv(k))), axis=0)
        hot = jnp.concatenate(
            [hot_f_ref[k * D : k * D + grow], hot_r_ref[(2 - k) * D : (2 - k) * D + grow]], axis=0
        )
        before = before + mm(jnp.concatenate([hot, hot], axis=1), taps)
    value, slope = gelu_pair(before)
    own_col = (iota((cap, 1), 0) < count).astype(F32)
    own_gb = (cx[HALO : HALO + cap].astype(F32) * own_col).astype(BF16)
    mids = jnp.concatenate(
        [value[HALO : HALO + cap], value[grow + HALO : grow + HALO + cap]], axis=0
    ).astype(BF16)
    put(1, mm_tn(mids, jnp.concatenate([own_gb, own_gb], axis=0)))
    grad_f = (back_mid * slope[0:grow]).astype(BF16)
    grad_r = (back_mid * slope[grow:]).astype(BF16)
    ga = jnp.zeros((2 * inner, cx.shape[1]), F32)
    for k in range(3):
        rows = jnp.concatenate(
            [grad_f[(2 - k) * D : (2 - k) * D + inner], grad_r[k * D : k * D + inner]], axis=0
        )
        ga = ga + mm_nt(rows, conv(k))
    hot = jnp.concatenate(
        [hot_f_ref[2 * D : 2 * D + inner], hot_r_ref[2 * D : 2 * D + inner]], axis=0
    )
    base_g = cx[D : D + inner].astype(F32)
    g = jnp.concatenate([base_g, base_g], axis=0) + ga * mm(
        jnp.concatenate([hot, hot], axis=1), s2
    )
    gb = g.astype(BF16)
    gb_ref[...] = gb
    g_ref[0:cap] = g[d : d + cap]
    g_ref[cap : 2 * cap] = g[inner + d : inner + d + cap]
    col = jnp.concatenate([own_col, own_col], axis=0)
    own_hot = jnp.concatenate([hot[d : d + cap], hot[inner + d : inner + d + cap]], axis=0)
    own_b1 = mm((own_hot.astype(F32) * col).astype(BF16), b1).astype(BF16)
    own_g = jnp.concatenate([gb[d : d + cap], gb[inner + d : inner + d + cap]], axis=0)
    put(0, mm_tn(own_b1, own_g))


def saliency_kernel(
    where_ref, small_ref, hot_f_ref, hot_r_ref, s1_ref, gb_ref, g_ref, second_ref, p1_ref, sal_ref
):
    count = where_ref[2]
    cap = g_ref.shape[0] // 2
    inner = cap + 2 * FIRST_DILATION
    d, D = FIRST_DILATION, SECOND_DILATION
    hot = jnp.concatenate(
        [hot_f_ref[2 * D : 2 * D + inner], hot_r_ref[2 * D : 2 * D + inner]], axis=0
    )
    slope = mm(jnp.concatenate([hot, hot], axis=1), s1_ref[...])
    gh = (mm_nt(gb_ref[...], p1_ref[...]) * slope).astype(BF16)
    emb = small_ref[0:4]
    bases = small_ref[4:5, 0:cap]
    wide = jnp.concatenate(split(second_ref[...]), axis=0)
    total = jnp.zeros((4, cap), F32)
    e_high, e_low = split(jnp.concatenate([emb, emb], axis=0))
    for turn in range(2):
        g_high, g_low = split(g_ref[turn * cap : (turn + 1) * cap])
        got = mm_nt(e_high, g_high) + mm_nt(e_high, g_low) + mm_nt(e_low, g_high)
        got = got[0:4]
        table = jnp.zeros((16, cap), F32)
        for k in range(3):
            place = 2 - k if turn == 0 else k
            at = turn * inner + place * d
            both = mm_nt(
                jnp.concatenate(
                    [wide[16 * k : 16 * k + 16], wide[48 + 16 * k : 64 + 16 * k]], axis=0
                ),
                gh[at : at + cap],
            )
            table = table + both[0:16] + both[16:32]
        for q in range(4):
            code = float(q if turn == 0 else 3 - q)
            got = got + jnp.where(bases == code, table[4 * q : 4 * q + 4], 0.0)
        if turn == 1:
            got = jnp.concatenate([got[3 - c : 4 - c] for c in range(4)], axis=0)
        total = total + got
    live = iota((1, cap), 1) < count
    sal_ref[...] = jnp.where(live, total * (1.0 / math.sqrt(emb.shape[1])), 0.0)


def tower_kernel_packed(where_ref, *refs):
    own_parts, plane_parts, dp_parts = refs[0:2], refs[2:8], refs[8:14]
    small_ref, cx_ref, hf_ref, hr_ref = refs[14:18]
    keep_ref, send_ref, s1_ref, gb_ref, g_ref, wide_ref, p1_ref = refs[18:25]
    conv_ref, p2_ref, first_ref, second_ref = refs[25:]
    me, count = where_ref[0], where_ref[2]
    core, odd = me & 1, where_ref[1] & 1
    width, chans = p1_ref.shape
    shard = chans // 8
    prow = width // 8
    half = 3 * shard // 2
    cut = half - 16

    def place(side, rows, peer):
        at = peer * shard

        def lay(k, start, size, source, lane):
            conv_ref[k, pl.ds(pl.multiple_of(at + start, 16), size), :] = rows(
                source, size
            )[:, lane : lane + width]

        if side == 0:
            lay(0, 0, shard, 0, 0)
            lay(1, 0, cut - shard, shard, 0)
            lay(1, shard // 2, shard // 2, 0, width)
            lay(2, 0, cut - shard // 2, shard // 2, width)
            tail = rows(cut, 16).astype(F32)
            first_ref[peer] = tail[:, 0:width] + tail[:, width:]
        else:
            lay(1, cut - shard, 16, 0, 0)
            lay(2, shard - 16, 16, 0, width)
            to = pl.ds(pl.multiple_of(peer * prow, 16), prow)
            p2_ref[to, :] = rows(16, prow)
            p1_ref[to, :] = rows(16 + prow, prow)
            second_ref[peer] = rows(half - 32, 32).astype(F32)[0:24]

    for n in range(2):
        for side in range(2):
            rows = lambda a, size, n=n, side=side: own_parts[n][
                side * half + a : side * half + a + size
            ]
            place(side, rows, me ^ n)
    for parity in range(2):

        @pl.when(odd == parity)
        def _():
            for n in range(6):
                peer = me ^ (2 * (n % 3 + 1) + n // 3)
                for side, part in ((parity, plane_parts[n]), (1 - parity, dp_parts[n])):
                    rows = lambda a, size, part=part: part[a : a + size]
                    place(side, rows, peer)

    first = first_ref[0]
    wide = second_ref[0]
    for peer in range(1, 8):
        first = first + first_ref[peer]
        wide = wide + second_ref[peer]
    wide_ref[...] = jnp.concatenate([wide[:, 0:width], wide[:, width : 2 * width]], axis=0)

    def put(block, value):
        rows = value.shape[0] // 4
        for c in range(2):
            even = value[2 * c * rows : (2 * c + 1) * rows]
            uneven = value[(2 * c + 1) * rows : (2 * c + 2) * rows]
            keep_ref[2 * block + c] = jnp.where(core == 0, even, uneven)
            send_ref[2 * block + c] = jnp.where(core == 0, uneven, even).astype(BF16)

    tower_body(
        first, p1_ref[...], lambda k: conv_ref[k], p2_ref[...], count, small_ref[0:4],
        g_ref.shape[0] // 2, cx_ref, hf_ref, hr_ref, s1_ref, gb_ref, g_ref, put,
    )


def tower_kernel_plain(
    where_ref, first_ref, p1_ref, conv_ref, p2_ref, small_ref, cx_ref, hf_ref, hr_ref,
    grad_ref, s1_ref, gb_ref, g_ref,
):
    def put(block, value):
        rows = value.shape[0]
        grad_ref[block * rows : (block + 1) * rows] = value

    tower_body(
        first_ref[...], p1_ref[...], lambda k: conv_ref[k], p2_ref[...], where_ref[2],
        small_ref[0:4], g_ref.shape[0] // 2, cx_ref, hf_ref, hr_ref, s1_ref, gb_ref, g_ref, put,
    )


def fold(value):
    width = value.shape[1] // 2
    return jnp.concatenate([value[:, 0:width], value[:, width:]], axis=0)


def core_sum_kernel(keep_ref, recv_ref, own_ref, *outs):
    chip = 2 * lax.axis_index("y") + lax.axis_index("x")
    own_ref[...] = keep_ref[chip] + recv_ref[chip].astype(F32)
    for n, out in enumerate(outs):
        at = chip ^ (n + 1)
        out[...] = (keep_ref[at] + recv_ref[at].astype(F32)).astype(BF16)


def plane_sum_kernel(own_ref, d_ref, y_ref, x_ref, mine_ref, *refs):
    outs, sum_ref = refs[:-1], refs[-1]
    sum_ref[...] = (
        own_ref[...] + x_ref[...].astype(F32) + y_ref[...].astype(F32) + d_ref[...].astype(F32)
    )
    z = lax.axis_index("dp")
    rows = mine_ref.shape[0] // 2
    mine_ref[...] = fold(sum_ref[pl.ds(pl.multiple_of(z * rows, 8), rows), :])
    for n, out in enumerate(outs):
        at = pl.multiple_of((z ^ (n + 1)) * rows, 8)
        out[...] = fold(sum_ref[pl.ds(at, rows), :]).astype(BF16)


def last_sum_kernel(scale, mine_ref, *refs):
    out_ref = refs[-1]
    total = mine_ref[...]
    for ref in refs[:-1]:
        total = total + ref[...].astype(F32)
    total = total * scale
    rows, half = total.shape[0] // 2, total.shape[1] // 128
    for n in range(2 * half):
        at = rows * (n // half)
        lane = 128 * (n % half)
        out_ref[pl.ds(n, rows, stride=2 * half), :] = total[at : at + rows, lane : lane + 128]


def flip_move(array, *axes):
    sizes = [lax.axis_size(a) for a in axes]
    size = math.prod(sizes)
    return lax.ppermute(array, axes, [(i, size - 1 - i) for i in range(size)])


def xor_move(array, axis, bits):
    return lax.ppermute(array, axis, [(i, i ^ bits) for i in range(lax.axis_size(axis))])


def shift_move(array, by, axes):
    size = math.prod(lax.axis_size(a) for a in axes)
    return lax.ppermute(array, axes, [(i, i + by) for i in range(size) if 0 <= i + by < size])


def context_shapes(cap, chans):
    rows = cap + 2 * (HALO + SECOND_DILATION)
    return [((rows, TABLE), BF16), ((rows, TABLE), BF16), ((cap + 2 * HALO, chans), BF16)]


def pass_shapes(cap, chans, width):
    inner = cap + 2 * FIRST_DILATION
    return [((2 * TABLE, width), BF16), ((2 * inner, chans), BF16), ((2 * cap, chans), F32)]


def lines(embed, bases):
    cap, chans = bases.shape[1], embed.shape[1]
    row = lax.broadcasted_iota(jnp.int32, (8, chans), 0)
    line = jnp.pad(bases, ((0, 0), (0, chans - cap))).astype(F32)
    return jnp.where(row == 4, line, jnp.pad(embed, ((0, 4), (0, 0))))


def weight(flops):
    return pl.CostEstimate(flops=flops, bytes_accessed=10**6, transcendentals=0)


def fast_shards(
    bases, lengths, cotangent, c1, p1, c2, p2, embed
):
    cot = cotangent[0]
    me = (lax.axis_index("y") * 2 + lax.axis_index("x")) * 2 + lax.axis_index("core")
    where = jnp.stack([me.astype(jnp.int32), lax.axis_index("dp").astype(jnp.int32), lengths[0, 0]])
    cap, chans = cot.shape
    width = c1.shape[2]
    n_dp = lax.axis_size("dp")
    half = 3 * c2.shape[1] // 2
    narrow = jnp.concatenate([c1.reshape(-1, width), c2.reshape(-1, width)], axis=0)
    broad = jnp.concatenate([p2, p1, cot], axis=0)
    small = lines(embed, bases)
    own, part = call(
        prep_kernel,
        [((2 * half + HALO, chans), BF16), ((half, chans), BF16)],
        [where, narrow, broad, small],
    )
    from_x, from_y, from_d = [flip_move(part, *axes) for axes in (("x",), ("y",), ("y", "x"))]
    plane = [from_x, from_y, from_d]
    other = [xor_move(a, "dp", 1) for a in plane]
    edge_x, edge_d = call(
        halo_kernel, [((HALO, chans), BF16)] * 2, [where, broad, other[1]], cost=weight(10**6)
    )
    edge_d = flip_move(edge_d, "y", "x")
    edge_x = flip_move(edge_x, "x")
    across = lambda arrays: [flip_move(a, "core") for a in arrays]
    rows = chans // 8
    swapped = across([own, *plane])
    hf, hr, cx = call(
        context_kernel_packed,
        context_shapes(cap, chans),
        [where, own, *plane, *swapped, edge_x, edge_d, *across([edge_x, edge_d]), broad],
        scratch=[
            pltpu.VMEM((8 + 2 * REACH, 8, 256), F32),
            pltpu.VMEM((8, HALO, chans), BF16),
        ],
        cost=weight(10**6),
    )
    keep, send, s1, gb, g, second, p1_full = call(
        tower_kernel_packed,
        [((4, rows, chans), F32), ((4, rows, chans), BF16), *pass_shapes(cap, chans, width)]
        + [((48, width), F32), ((width, chans), BF16)],
        [
            where, own, swapped[0], *plane, *swapped[1:], *other, *across(other),
            small, cx, hf, hr,
        ],
        scratch=[
            pltpu.VMEM((3, chans, width), BF16),
            pltpu.VMEM((width, chans), BF16),
            pltpu.VMEM((8, 16, width), F32),
            pltpu.VMEM((8, 24, chans), F32),
        ],
        limit=40,
        cost=weight(4 * 10**9),
    )
    recv = flip_move(send, "core")
    (sal,) = call(
        saliency_kernel,
        [((4, cap), F32)],
        [where, small, hf, hr, s1, gb, g, second, p1_full],
        cost=weight(10**9),
    )
    own, *outs = call(
        core_sum_kernel,
        [((rows, chans), F32)] + [((rows, chans), BF16)] * 3,
        [keep, recv],
    )
    ways = (("x",), ("y",), ("y", "x"))
    got = [flip_move(outs[n], *ways[n]) for n in (2, 1, 0)]
    part = rows // n_dp
    mine, *outs = call(
        plane_sum_kernel,
        [((2 * part, width), F32)] + [((2 * part, width), BF16)] * (n_dp - 1),
        [own, *got],
        scratch=[pltpu.VMEM((rows, chans), F32)],
    )
    got = [xor_move(outs[n], "dp", n + 1) for n in reversed(range(n_dp - 1))]
    scale = 1.0 / math.sqrt(8 * n_dp * cap)
    (grad,) = call(
        functools.partial(last_sum_kernel, scale),
        [((part * chans // 128, 128), F32)],
        [mine, *got],
    )
    return sal[None], grad.reshape(-1)


def plain_shards(bases, lengths, cotangent, c1, p1, c2, p2, embed):
    cot = cotangent[0]
    where = jnp.stack(
        [
            lax.axis_index("seq").astype(jnp.int32),
            lax.axis_index("dp").astype(jnp.int32),
            lengths[0, 0],
        ]
    )
    cap, chans = cot.shape
    width = c1.shape[2]
    me, count = where[0], where[2]
    shard = c1.shape[1]
    own = lax.dynamic_slice_in_dim(embed, me * shard, shard, 1)
    act, slope = gelu_pair(own)
    taps = c1.astype(F32)
    high = lax.Precision.HIGHEST
    first = jnp.einsum("qc,kcb->kqb", act.astype(BF16).astype(F32), taps, precision=high)
    second = jnp.einsum("qc,dc,kcb->kqdb", slope, own, taps, precision=high)
    first = lax.psum(first.reshape(12, width), "seq")
    second = lax.psum(second.reshape(48, width), "seq")
    first = jnp.concatenate([first, jnp.zeros((4, width), F32)], axis=0)
    p1_full = lax.all_gather(p1, "seq", axis=0, tiled=True)
    p2_full = lax.all_gather(p2, "seq", axis=0, tiled=True)
    conv = lax.all_gather(c2, "seq", axis=1, tiled=True)
    info = jnp.concatenate(
        [bases.astype(F32), jnp.broadcast_to(count.astype(F32), (1, 128))], axis=1
    )
    info = lax.all_gather(info, "seq", axis=0, tiled=True)
    info = jnp.pad(info, ((REACH, REACH), (0, 0)))
    info = lax.dynamic_slice_in_dim(info, me, 2 * REACH + 1, 0)
    info = jnp.broadcast_to(info[:, None, :], (2 * REACH + 1, 8, cap + 128))
    padded = jnp.pad(cot, ((HALO, 0), (0, 0)))
    last = lax.dynamic_slice_in_dim(padded, count, HALO, 0)
    halos = [
        shift_move(last, 1, ("seq",)),
        shift_move(last[HALO - SPILL :], 2, ("seq",)),
        shift_move(cot[:HALO], -1, ("seq",)),
        shift_move(cot[:SPILL], -2, ("seq",)),
    ]
    small = lines(embed, bases)
    hf, hr, cx = call(
        context_kernel_plain, context_shapes(cap, chans), [info, cot, *halos]
    )
    grad, s1, gb, g = call(
        tower_kernel_plain,
        [((2 * width, chans), F32), *pass_shapes(cap, chans, width)],
        [where, first, p1_full, conv, p2_full, small, cx, hf, hr],
        limit=40,
    )
    (sal,) = call(
        saliency_kernel,
        [((4, cap), F32)],
        [where, small, hf, hr, s1, gb, g, second, p1_full],
    )
    scale = 1.0 / math.sqrt(lax.axis_size("seq") * lax.axis_size("dp") * cap)
    grad = lax.psum_scatter(
        grad.reshape(-1) * scale, ("seq", "dp"), scatter_dimension=0, tiled=True
    )
    return sal[None], grad


def solution(mesh):
    run, seq = plain_shards, "seq"
    if mesh.shape["seq"] == 8 and mesh.shape["dp"] == 4:
        run, seq = fast_shards, ("y", "x", "core")
        count = mesh.shape["dp"]
        mesh = jax.sharding.Mesh(mesh.devices.reshape(2, 2, 2, count), (*seq, "dp"))
    every = seq if isinstance(seq, tuple) else (seq,)
    in_specs = (
        P("dp", seq),
        P("dp", seq),
        P("dp", seq, None),
        P(None, seq, None),
        P(seq, None),
        P(None, seq, None),
        P(seq, None),
        P(),
    )
    out_specs = (P("dp", None, seq), P((*every, "dp")))
    return jax.shard_map(run, mesh=mesh, in_specs=in_specs, out_specs=out_specs, check_vma=False)
```

```python
import functools
import math

import jax
import jax.numpy as jnp
from jax import lax
from jax.experimental import pallas as pl
from jax.experimental.pallas import tpu as pltpu
from jax.sharding import PartitionSpec as P

FIRST_DILATION = 16
SECOND_DILATION = 64
HALO = FIRST_DILATION + SECOND_DILATION
SPILL = 16
REACH = 3
TABLE = 128
SQRT_HALF = 0.7071067811865476
INV_SQRT_TWO_PI = 0.3989422804014327
F32 = jnp.float32
BF16 = jnp.bfloat16
FAR = -100000.0


def gelu_pair(v):
    half = 0.5 * (1.0 + lax.erf(v * SQRT_HALF))
    return v * half, half + v * jnp.exp(-0.5 * v * v) * INV_SQRT_TWO_PI


def split(v):
    high = v.astype(BF16)
    return high, (v - high.astype(F32)).astype(BF16)


def mm(a, b):
    return lax.dot_general(a, b, (((1,), (0,)), ((), ())), preferred_element_type=F32)


def mm_nt(a, b):
    return lax.dot_general(a, b, (((1,), (1,)), ((), ())), preferred_element_type=F32)


def mm_tn(a, b):
    return lax.dot_general(a, b, (((0,), (0,)), ((), ())), preferred_element_type=F32)


def iota(shape, dim):
    return lax.broadcasted_iota(jnp.int32, shape, dim)


def spread(rows, index):
    out = jnp.broadcast_to(rows[0:1], (index.shape[0], rows.shape[1]))
    for q in range(1, 4):
        out = jnp.where(index == q, rows[q : q + 1], out)
    return out


def call(body, out_shapes, args, scratch=(), limit=24, cost=None):
    in_specs = [
        pl.BlockSpec(memory_space=pltpu.VMEM) for _ in args
    ]
    return pl.pallas_call(
        body,
        out_shape=[jax.ShapeDtypeStruct(s, d) for s, d in out_shapes],
        in_specs=in_specs,
        out_specs=[pl.BlockSpec(memory_space=pltpu.VMEM)] * len(out_shapes),
        scratch_shapes=list(scratch),
        compiler_params=pltpu.CompilerParams(vmem_limit_bytes=limit * 1024 * 1024),
        cost_estimate=cost,
    )(*args)


def base_tables(emb, pick, conv):
    row = iota((16, 1), 0)
    low, high = row & 3, row >> 2
    by_low = spread(emb, low)
    by_high = spread(emb, high)
    act = gelu_pair(by_low)[0].astype(BF16)
    prod_high, prod_low = split(gelu_pair(by_high)[1] * by_low)
    own = mm(jnp.concatenate([act, prod_high, prod_low], axis=0), pick).astype(BF16)
    first = jnp.zeros((16, conv[0].shape[1]), F32)
    second = []
    for k in range(3):
        res = mm(own, conv[k])
        first = jnp.where(high == k, res[0:16], first)
        second.append(res[16:32] + res[32:48])
    return first, jnp.concatenate(second, axis=0)


def position():
    return (2 * lax.axis_index("y") + lax.axis_index("x")) * 2 + lax.axis_index("core")


def prep_kernel(
    narrow_ref, broad_ref, small_ref,
    own_ref, x_ref, y_ref, d_ref,
):
    me, odd = position(), lax.axis_index("dp") & 1
    count = small_ref[5:6, 0:128]
    width = narrow_ref.shape[1]
    chans = 2 * width
    shard = narrow_ref.shape[0] // 6
    prows = width // 8
    cap = broad_ref.shape[0] - 2 * prows
    half = 3 * shard // 2
    cut = half - 16
    flat = narrow_ref.at[3 * shard : 6 * shard]
    cot = broad_ref[2 * prows :]
    pick = (iota((chans, shard), 0) == iota((chans, shard), 1) + me * shard).astype(BF16)
    taps = [narrow_ref[k * shard : (k + 1) * shard] for k in range(3)]
    first, second = base_tables(small_ref[0:4], pick, taps)
    f_high, f_low = split(first)
    info = jnp.concatenate(
        [
            small_ref[4:5, 0:cap],
            count,
            jnp.zeros((1, chans - cap - 128), F32),
        ],
        axis=1,
    )
    tail = jnp.concatenate([f_high.astype(F32), f_low.astype(F32)], axis=1)
    tail = jnp.where(iota((16, 1), 0) == 12, info, tail)
    wide = jnp.concatenate([second[0:24], second[24:48]], axis=1)
    extra = jnp.concatenate([info, jnp.zeros((7, chans), F32)], axis=0)
    own_ref[0:cut, 0:width] = flat[0:cut]
    own_ref[0:cut, width:chans] = flat[half : half + cut]
    own_ref[cut:half] = tail.astype(BF16)
    own_ref[half : half + 16, 0:width] = flat[cut:half]
    own_ref[half : half + 16, width:chans] = flat[half + cut : 2 * half]
    own_ref[half + 16 : half + 16 + 2 * prows] = broad_ref[0 : 2 * prows]
    own_ref[2 * half - 32 : 2 * half] = jnp.concatenate([wide, extra], axis=0).astype(BF16)
    part = own_ref[pl.ds(pl.multiple_of(odd * half, 16), half), :]
    for out in (x_ref, y_ref, d_ref):
        out[0:half] = part
    ahead = (iota((HALO, cap), 1) - iota((HALO, cap), 0) + HALO).astype(F32)
    take = (ahead == count).astype(BF16)
    last = mm(take, cot).astype(BF16)
    chip = me >> 1
    own_ref[2 * half :] = jnp.where((me & 1) == 0, last, cot[0:HALO])
    x_ref[half:] = jnp.where((chip ^ 1) > chip, last, cot[0:HALO])
    d_ref[half:] = jnp.where((chip ^ 3) > chip, last, cot[0:HALO])


def context_body(info_at, cot, r1, r2, l1, l2, hot_f_ref, hot_r_ref, cx_ref):
    cap = cot.shape[0]
    outer = HALO + SECOND_DILATION + FIRST_DILATION
    span = cap + 2 * outer
    counts = [info_at(o)[0:1, cap : cap + 128] for o in range(-REACH, REACH + 1)]
    begin = [None] * (2 * REACH + 1)
    begin[REACH] = jnp.zeros((1, 128), F32)
    for o in range(1, REACH + 1):
        begin[REACH + o] = begin[REACH + o - 1] + counts[REACH + o - 1]
        begin[REACH - o] = begin[REACH - o + 1] - counts[REACH - o]
    lane = iota((1, 128), 1).astype(F32)
    rowpos = (iota((span, 128), 0) - outer).astype(F32)
    total = jnp.zeros((span, 128), F32)
    for o in range(-REACH, REACH + 1):
        code = info_at(o)[0:1, 0:cap] + 1.0
        pos = jnp.where(lane < counts[REACH + o], begin[REACH + o] + lane, FAR)
        total = total + jnp.where(rowpos == pos, code, 0.0)
    codes = jnp.sum(total, axis=1, keepdims=True)
    d = FIRST_DILATION
    left, mid, right = codes[0 : span - 2 * d], codes[d : span - d], codes[2 * d : span]
    rows = span - 2 * d
    lanes = iota((rows, TABLE), 1).astype(F32)
    flip = lambda c: jnp.where(c == 0.0, 0.0, 5.0 - c)
    idx = jnp.where(mid == 0.0, -1.0, (mid - 1.0) * 25.0 + left * 5.0 + right)
    hot_f_ref[...] = (lanes == idx).astype(BF16)
    idx = jnp.where(mid == 0.0, -1.0, (4.0 - mid) * 25.0 + flip(right) * 5.0 + flip(left))
    hot_r_ref[...] = (lanes == idx).astype(BF16)

    own_n = counts[REACH]
    before_n, after_n = counts[REACH - 1], counts[REACH + 1]
    grow = cap + 2 * HALO
    lane_h = iota((1, HALO), 1).astype(F32)
    lane_s = iota((1, SPILL), 1).astype(F32)
    row_h = (iota((grow, HALO), 0) - HALO).astype(F32)
    row_s = (iota((grow, SPILL), 0) - HALO).astype(F32)
    row_o = (iota((grow, cap), 0) - HALO).astype(F32)
    own_pos = jnp.where(lane < own_n, lane, FAR)
    acc = mm((row_o == own_pos).astype(BF16), cot)
    pos = jnp.where(lane_h >= HALO - before_n[:, 0:HALO], lane_h - HALO, FAR)
    acc = acc + mm((row_h == pos).astype(BF16), r1)
    pos = jnp.where(
        counts[REACH - 2][:, 0:SPILL] > 0.0, lane_s - SPILL - before_n[:, 0:SPILL], FAR
    )
    acc = acc + mm((row_s == pos).astype(BF16), r2)
    pos = jnp.where(lane_h < after_n[:, 0:HALO], lane_h + own_n[:, 0:HALO], FAR)
    acc = acc + mm((row_h == pos).astype(BF16), l1)
    pos = jnp.where(
        (counts[REACH + 2][:, 0:SPILL] > 0.0) & (after_n[:, 0:SPILL] < HALO),
        lane_s + own_n[:, 0:SPILL] + after_n[:, 0:SPILL],
        FAR,
    )
    acc = acc + mm((row_s == pos).astype(BF16), l2)
    cx_ref[...] = (0.5 * acc).astype(BF16)


def context_kernel_plain(info_ref, cot_ref, r1_ref, r2_ref, l1_ref, l2_ref, *outs):
    context_body(
        lambda o: info_ref[REACH + o], cot_ref[...], r1_ref[...], r2_ref[...], l1_ref[...],
        l2_ref[...], *outs,
    )


def context_kernel_packed(*refs):
    parts, broad_ref, outs = refs[0:8], refs[8], refs[9:12]
    info_ref, halo_ref = refs[12:]
    me, odd = position(), lax.axis_index("dp") & 1
    chip, core = me >> 1, me & 1
    chans = broad_ref.shape[1]
    prow = chans // 16
    half = 3 * chans // 16
    info_ref[0:REACH] = jnp.zeros((REACH, 8, 256), F32)
    info_ref[REACH + 8 :] = jnp.zeros((REACH, 8, 256), F32)
    for n, part in enumerate(parts):
        peer = me ^ (2 * (n % 4) + n // 4)
        low = part[half - 16 : half].astype(F32)[12:13, 0:256]
        if n % 4 > 0:
            high = part[half - 16 : half].astype(F32)[8:9, 0:256]
            low = jnp.where(odd == 0, low, high)
        info_ref[REACH + peer] = jnp.broadcast_to(low, (8, 256))
    for n in range(2):
        halo_ref[4 * n + chip] = parts[4 * n][2 * half :]
        halo_ref[4 * n + (chip ^ 1)] = parts[4 * n + 1][half:]
        halo_ref[4 * n + (chip ^ 3)] = parts[4 * n + 3][half:]
    r1 = halo_ref[4 + jnp.maximum(chip + core - 1, 0)]
    l1 = halo_ref[4 + jnp.minimum(chip + core, 3)]
    r2 = halo_ref[jnp.maximum(chip - 1, 0)]
    l2 = halo_ref[jnp.minimum(chip + 1, 3)]
    context_body(
        lambda o: info_ref[me + (REACH + o)], broad_ref[2 * prow :], r1, r2[HALO - SPILL :], l1,
        l2[0:SPILL], *outs,
    )


def tower_body(
    first, project, conv, p2, count, emb, cap, cx_ref, hot_f_ref, hot_r_ref,
    s1_ref, gb_ref, g_ref, put,
):
    entry = iota((TABLE, 1), 0)
    by25 = (entry * 1311) >> 15
    by5 = (entry * 6554) >> 15
    in_left = by5 - 5 * by25
    in_right = entry - 5 * by5
    sums = jnp.zeros((TABLE, first.shape[1]), F32)
    for q in range(4):
        sums = jnp.where(in_left == q + 1, first[q : q + 1], sums)
    sums = sums + spread(first[4:8], by25)
    after = jnp.zeros((TABLE, first.shape[1]), F32)
    for q in range(4):
        after = jnp.where(in_right == q + 1, first[8 + q : 9 + q], after)
    value, slope = gelu_pair(sums + after)
    b1 = value.astype(BF16)
    high, low = split(slope)
    s1_ref[0:TABLE] = high
    s1_ref[TABLE : 2 * TABLE] = low
    stream = spread(emb, by25) + mm(b1, project)
    value, slope = gelu_pair(stream)
    a2 = value.astype(BF16)
    s2 = jnp.concatenate(split(slope), axis=0)

    grow = cap + 2 * HALO
    inner = cap + 2 * FIRST_DILATION
    d, D = FIRST_DILATION, SECOND_DILATION
    cx = cx_ref[...]
    back_mid = mm_nt(cx, p2)
    before = jnp.zeros((2 * grow, p2.shape[0]), F32)
    for k in range(3):
        taps = jnp.concatenate(split(mm(a2, conv(k))), axis=0)
        hot = jnp.concatenate(
            [hot_f_ref[k * D : k * D + grow], hot_r_ref[(2 - k) * D : (2 - k) * D + grow]], axis=0
        )
        before = before + mm(jnp.concatenate([hot, hot], axis=1), taps)
    value, slope = gelu_pair(before)
    own_col = (iota((cap, 1), 0).astype(F32) < count).astype(F32)
    own_gb = (cx[HALO : HALO + cap].astype(F32) * own_col).astype(BF16)
    mids = jnp.concatenate(
        [value[HALO : HALO + cap], value[grow + HALO : grow + HALO + cap]], axis=0
    ).astype(BF16)
    put(1, mm_tn(mids, jnp.concatenate([own_gb, own_gb], axis=0)))
    grad_f = (back_mid * slope[0:grow]).astype(BF16)
    grad_r = (back_mid * slope[grow:]).astype(BF16)
    ga = jnp.zeros((2 * inner, cx.shape[1]), F32)
    for k in range(3):
        rows = jnp.concatenate(
            [grad_f[(2 - k) * D : (2 - k) * D + inner], grad_r[k * D : k * D + inner]], axis=0
        )
        ga = ga + mm_nt(rows, conv(k))
    hot = jnp.concatenate(
        [hot_f_ref[2 * D : 2 * D + inner], hot_r_ref[2 * D : 2 * D + inner]], axis=0
    )
    base_g = cx[D : D + inner].astype(F32)
    g = jnp.concatenate([base_g, base_g], axis=0) + ga * mm(
        jnp.concatenate([hot, hot], axis=1), s2
    )
    gb = g.astype(BF16)
    gb_ref[...] = gb
    g_ref[0:cap] = g[d : d + cap]
    g_ref[cap : 2 * cap] = g[inner + d : inner + d + cap]
    col = jnp.concatenate([own_col, own_col], axis=0)
    own_hot = jnp.concatenate([hot[d : d + cap], hot[inner + d : inner + d + cap]], axis=0)
    own_b1 = mm((own_hot.astype(F32) * col).astype(BF16), b1).astype(BF16)
    own_g = jnp.concatenate([gb[d : d + cap], gb[inner + d : inner + d + cap]], axis=0)
    put(0, mm_tn(own_b1, own_g))


def saliency_kernel(
    small_ref, hot_f_ref, hot_r_ref, s1_ref, gb_ref, g_ref, second_ref, p1_ref, sal_ref
):
    cap = g_ref.shape[0] // 2
    inner = cap + 2 * FIRST_DILATION
    d, D = FIRST_DILATION, SECOND_DILATION
    hot = jnp.concatenate(
        [hot_f_ref[2 * D : 2 * D + inner], hot_r_ref[2 * D : 2 * D + inner]], axis=0
    )
    slope = mm(jnp.concatenate([hot, hot], axis=1), s1_ref[...])
    gh = (mm_nt(gb_ref[...], p1_ref[...]) * slope).astype(BF16)
    emb = small_ref[0:4]
    bases = small_ref[4:5, 0:cap]
    wide = jnp.concatenate(split(second_ref[...]), axis=0)
    total = jnp.zeros((4, cap), F32)
    e_high, e_low = split(jnp.concatenate([emb, emb], axis=0))
    for turn in range(2):
        g_high, g_low = split(g_ref[turn * cap : (turn + 1) * cap])
        got = mm_nt(e_high, g_high) + mm_nt(e_high, g_low) + mm_nt(e_low, g_high)
        got = got[0:4]
        table = jnp.zeros((16, cap), F32)
        for k in range(3):
            place = 2 - k if turn == 0 else k
            at = turn * inner + place * d
            both = mm_nt(
                jnp.concatenate(
                    [wide[16 * k : 16 * k + 16], wide[48 + 16 * k : 64 + 16 * k]], axis=0
                ),
                gh[at : at + cap],
            )
            table = table + both[0:16] + both[16:32]
        for q in range(4):
            code = float(q if turn == 0 else 3 - q)
            got = got + jnp.where(bases == code, table[4 * q : 4 * q + 4], 0.0)
        if turn == 1:
            got = jnp.concatenate([got[3 - c : 4 - c] for c in range(4)], axis=0)
        total = total + got
    live = iota((1, cap), 1).astype(F32) < small_ref[5:6, 0:cap]
    sal_ref[...] = jnp.where(live, total * (1.0 / math.sqrt(emb.shape[1])), 0.0)


def tower_kernel_packed(*refs):
    own_parts, plane_parts, dp_parts = refs[0:2], refs[2:8], refs[8:14]
    small_ref, cx_ref, hf_ref, hr_ref = refs[14:18]
    keep_ref, send_ref, s1_ref, gb_ref, g_ref, wide_ref, p1_ref = refs[18:25]
    conv_ref, p2_ref, first_ref, second_ref = refs[25:]
    me = position()
    core, odd = me & 1, lax.axis_index("dp") & 1
    count = small_ref[5:6, 0:1]
    width, chans = p1_ref.shape
    shard = chans // 8
    prow = width // 8
    half = 3 * shard // 2
    cut = half - 16

    def place(side, rows, peer):
        at = peer * shard

        def lay(k, start, size, source, lane):
            conv_ref[k, pl.ds(pl.multiple_of(at + start, 16), size), :] = rows(
                source, size
            )[:, lane : lane + width]

        if side == 0:
            lay(0, 0, shard, 0, 0)
            lay(1, 0, cut - shard, shard, 0)
            lay(1, shard // 2, shard // 2, 0, width)
            lay(2, 0, cut - shard // 2, shard // 2, width)
            tail = rows(cut, 16).astype(F32)
            first_ref[peer] = tail[:, 0:width] + tail[:, width:]
        else:
            lay(1, cut - shard, 16, 0, 0)
            lay(2, shard - 16, 16, 0, width)
            to = pl.ds(pl.multiple_of(peer * prow, 16), prow)
            p2_ref[to, :] = rows(16, prow)
            p1_ref[to, :] = rows(16 + prow, prow)
            second_ref[peer] = rows(half - 32, 32).astype(F32)[0:24]

    for n in range(2):
        for side in range(2):
            rows = lambda a, size, n=n, side=side: own_parts[n][
                side * half + a : side * half + a + size
            ]
            place(side, rows, me ^ n)
    for parity in range(2):

        @pl.when(odd == parity)
        def _():
            for n in range(6):
                peer = me ^ (2 * (n % 3 + 1) + n // 3)
                for side, part in ((parity, plane_parts[n]), (1 - parity, dp_parts[n])):
                    rows = lambda a, size, part=part: part[a : a + size]
                    place(side, rows, peer)

    first = first_ref[0]
    wide = second_ref[0]
    for peer in range(1, 8):
        first = first + first_ref[peer]
        wide = wide + second_ref[peer]
    wide_ref[...] = jnp.concatenate([wide[:, 0:width], wide[:, width : 2 * width]], axis=0)

    def put(block, value):
        rows = value.shape[0] // 4
        for c in range(2):
            even = value[2 * c * rows : (2 * c + 1) * rows]
            uneven = value[(2 * c + 1) * rows : (2 * c + 2) * rows]
            keep_ref[2 * block + c] = jnp.where(core == 0, even, uneven)
            send_ref[2 * block + c] = jnp.where(core == 0, uneven, even).astype(BF16)

    tower_body(
        first, p1_ref[...], lambda k: conv_ref[k], p2_ref[...], count, small_ref[0:4],
        g_ref.shape[0] // 2, cx_ref, hf_ref, hr_ref, s1_ref, gb_ref, g_ref, put,
    )


def tower_kernel_plain(
    first_ref, p1_ref, conv_ref, p2_ref, small_ref, cx_ref, hf_ref, hr_ref,
    grad_ref, s1_ref, gb_ref, g_ref,
):
    def put(block, value):
        rows = value.shape[0]
        grad_ref[block * rows : (block + 1) * rows] = value

    tower_body(
        first_ref[...], p1_ref[...], lambda k: conv_ref[k], p2_ref[...], small_ref[5:6, 0:1],
        small_ref[0:4], g_ref.shape[0] // 2, cx_ref, hf_ref, hr_ref, s1_ref, gb_ref, g_ref, put,
    )


def fold(value):
    width = value.shape[1] // 2
    return jnp.concatenate([value[:, 0:width], value[:, width:]], axis=0)


def core_sum_kernel(keep_ref, recv_ref, own_ref, *outs):
    chip = 2 * lax.axis_index("y") + lax.axis_index("x")
    own_ref[...] = keep_ref[chip] + recv_ref[chip].astype(F32)
    for n, out in enumerate(outs):
        at = chip ^ (n + 1)
        out[...] = (keep_ref[at] + recv_ref[at].astype(F32)).astype(BF16)


def plane_sum_kernel(own_ref, d_ref, y_ref, x_ref, mine_ref, *refs):
    outs, sum_ref = refs[:-1], refs[-1]
    sum_ref[...] = (
        own_ref[...] + x_ref[...].astype(F32) + y_ref[...].astype(F32) + d_ref[...].astype(F32)
    )
    z = lax.axis_index("dp")
    rows = mine_ref.shape[0] // 2
    mine_ref[...] = fold(sum_ref[pl.ds(pl.multiple_of(z * rows, 8), rows), :])
    for n, out in enumerate(outs):
        at = pl.multiple_of((z ^ (n + 1)) * rows, 8)
        out[...] = fold(sum_ref[pl.ds(at, rows), :]).astype(BF16)


def last_sum_kernel(scale, mine_ref, *refs):
    out_ref = refs[-1]
    total = mine_ref[...]
    for ref in refs[:-1]:
        total = total + ref[...].astype(F32)
    total = total * scale
    rows, half = total.shape[0] // 2, total.shape[1] // 128
    for n in range(2 * half):
        at = rows * (n // half)
        lane = 128 * (n % half)
        out_ref[pl.ds(n, rows, stride=2 * half), :] = total[at : at + rows, lane : lane + 128]


def flip_move(array, *axes):
    sizes = [lax.axis_size(a) for a in axes]
    size = math.prod(sizes)
    return lax.ppermute(array, axes, [(i, size - 1 - i) for i in range(size)])


def xor_move(array, axis, bits):
    return lax.ppermute(array, axis, [(i, i ^ bits) for i in range(lax.axis_size(axis))])


def shift_move(array, by, axes):
    size = math.prod(lax.axis_size(a) for a in axes)
    return lax.ppermute(array, axes, [(i, i + by) for i in range(size) if 0 <= i + by < size])


def context_shapes(cap, chans):
    rows = cap + 2 * (HALO + SECOND_DILATION)
    return [((rows, TABLE), BF16), ((rows, TABLE), BF16), ((cap + 2 * HALO, chans), BF16)]


def pass_shapes(cap, chans, width):
    inner = cap + 2 * FIRST_DILATION
    return [((2 * TABLE, width), BF16), ((2 * inner, chans), BF16), ((2 * cap, chans), F32)]


def lines(embed, bases, lengths):
    cap, chans = bases.shape[1], embed.shape[1]
    row = lax.broadcasted_iota(jnp.int32, (8, chans), 0)
    line = jnp.pad(bases, ((0, 0), (0, chans - cap)))
    extra = jnp.where(row == 4, line, jnp.where(row == 5, lengths, 0)).astype(F32)
    return jnp.where(row < 4, jnp.pad(embed, ((0, 4), (0, 0))), extra)


def weight(flops):
    return pl.CostEstimate(flops=flops, bytes_accessed=10**6, transcendentals=0)


def fast_shards(
    bases, lengths, cotangent, c1, p1, c2, p2, embed
):
    cot = cotangent[0]
    cap, chans = cot.shape
    width = c1.shape[2]
    n_dp = lax.axis_size("dp")
    half = 3 * c2.shape[1] // 2
    narrow = jnp.concatenate([c1.reshape(-1, width), c2.reshape(-1, width)], axis=0)
    broad = jnp.concatenate([p2, p1, cot], axis=0)
    small = lines(embed, bases, lengths)
    own, to_x, to_y, to_d = call(
        prep_kernel,
        [
            ((2 * half + HALO, chans), BF16),
            ((half + HALO, chans), BF16),
            ((half, chans), BF16),
            ((half + HALO, chans), BF16),
        ],
        [narrow, broad, small],
    )
    plane = [flip_move(to_x, "x"), flip_move(to_y, "y"), flip_move(to_d, "y", "x")]
    other = [xor_move(a[:half], "dp", 1) for a in plane]
    across = lambda arrays: [flip_move(a, "core") for a in arrays]
    rows = chans // 8
    swapped = across([own, *plane])
    hf, hr, cx = call(
        context_kernel_packed,
        context_shapes(cap, chans),
        [own, *plane, *swapped, broad],
        scratch=[
            pltpu.VMEM((8 + 2 * REACH, 8, 256), F32),
            pltpu.VMEM((8, HALO, chans), BF16),
        ],
        cost=weight(10**9),
    )
    keep, send, s1, gb, g, second, p1_full = call(
        tower_kernel_packed,
        [((4, rows, chans), F32), ((4, rows, chans), BF16), *pass_shapes(cap, chans, width)]
        + [((48, width), F32), ((width, chans), BF16)],
        [
            own, swapped[0], *plane, *swapped[1:], *other, *across(other),
            small, cx, hf, hr,
        ],
        scratch=[
            pltpu.VMEM((3, chans, width), BF16),
            pltpu.VMEM((width, chans), BF16),
            pltpu.VMEM((8, 16, width), F32),
            pltpu.VMEM((8, 24, chans), F32),
        ],
        limit=40,
        cost=weight(4 * 10**9),
    )
    recv = flip_move(send, "core")
    (sal,) = call(
        saliency_kernel,
        [((4, cap), F32)],
        [small, hf, hr, s1, gb, g, second, p1_full],
        cost=weight(10**9),
    )
    own, *outs = call(
        core_sum_kernel,
        [((rows, chans), F32)] + [((rows, chans), BF16)] * 3,
        [keep, recv],
    )
    ways = (("x",), ("y",), ("y", "x"))
    got = [flip_move(outs[n], *ways[n]) for n in (2, 1, 0)]
    part = rows // n_dp
    mine, *outs = call(
        plane_sum_kernel,
        [((2 * part, width), F32)] + [((2 * part, width), BF16)] * (n_dp - 1),
        [own, *got],
        scratch=[pltpu.VMEM((rows, chans), F32)],
    )
    got = [xor_move(outs[n], "dp", n + 1) for n in reversed(range(n_dp - 1))]
    scale = 1.0 / math.sqrt(8 * n_dp * cap)
    (grad,) = call(
        functools.partial(last_sum_kernel, scale),
        [((part * chans // 128, 128), F32)],
        [mine, *got],
    )
    return sal[None], grad.reshape(-1)


def plain_shards(bases, lengths, cotangent, c1, p1, c2, p2, embed):
    cot = cotangent[0]
    cap, chans = cot.shape
    width = c1.shape[2]
    me, count = lax.axis_index("seq"), lengths[0, 0]
    shard = c1.shape[1]
    own = lax.dynamic_slice_in_dim(embed, me * shard, shard, 1)
    act, slope = gelu_pair(own)
    taps = c1.astype(F32)
    high = lax.Precision.HIGHEST
    first = jnp.einsum("qc,kcb->kqb", act.astype(BF16).astype(F32), taps, precision=high)
    second = jnp.einsum("qc,dc,kcb->kqdb", slope, own, taps, precision=high)
    first = lax.psum(first.reshape(12, width), "seq")
    second = lax.psum(second.reshape(48, width), "seq")
    first = jnp.concatenate([first, jnp.zeros((4, width), F32)], axis=0)
    p1_full = lax.all_gather(p1, "seq", axis=0, tiled=True)
    p2_full = lax.all_gather(p2, "seq", axis=0, tiled=True)
    conv = lax.all_gather(c2, "seq", axis=1, tiled=True)
    info = jnp.concatenate(
        [bases.astype(F32), jnp.broadcast_to(count.astype(F32), (1, 128))], axis=1
    )
    info = lax.all_gather(info, "seq", axis=0, tiled=True)
    info = jnp.pad(info, ((REACH, REACH), (0, 0)))
    info = lax.dynamic_slice_in_dim(info, me, 2 * REACH + 1, 0)
    info = jnp.broadcast_to(info[:, None, :], (2 * REACH + 1, 8, cap + 128))
    padded = jnp.pad(cot, ((HALO, 0), (0, 0)))
    last = lax.dynamic_slice_in_dim(padded, count, HALO, 0)
    halos = [
        shift_move(last, 1, ("seq",)),
        shift_move(last[HALO - SPILL :], 2, ("seq",)),
        shift_move(cot[:HALO], -1, ("seq",)),
        shift_move(cot[:SPILL], -2, ("seq",)),
    ]
    small = lines(embed, bases, lengths)
    hf, hr, cx = call(
        context_kernel_plain, context_shapes(cap, chans), [info, cot, *halos]
    )
    grad, s1, gb, g = call(
        tower_kernel_plain,
        [((2 * width, chans), F32), *pass_shapes(cap, chans, width)],
        [first, p1_full, conv, p2_full, small, cx, hf, hr],
        limit=40,
    )
    (sal,) = call(
        saliency_kernel,
        [((4, cap), F32)],
        [small, hf, hr, s1, gb, g, second, p1_full],
    )
    scale = 1.0 / math.sqrt(lax.axis_size("seq") * lax.axis_size("dp") * cap)
    grad = lax.psum_scatter(
        grad.reshape(-1) * scale, ("seq", "dp"), scatter_dimension=0, tiled=True
    )
    return sal[None], grad


def solution(mesh):
    run, seq = plain_shards, "seq"
    if mesh.shape["seq"] == 8 and mesh.shape["dp"] == 4:
        run, seq = fast_shards, ("y", "x", "core")
        count = mesh.shape["dp"]
        mesh = jax.sharding.Mesh(mesh.devices.reshape(2, 2, 2, count), (*seq, "dp"))
    every = seq if isinstance(seq, tuple) else (seq,)
    in_specs = (
        P("dp", seq),
        P("dp", seq),
        P("dp", seq, None),
        P(None, seq, None),
        P(seq, None),
        P(None, seq, None),
        P(seq, None),
        P(),
    )
    out_specs = (P("dp", None, seq), P((*every, "dp")))
    return jax.shard_map(run, mesh=mesh, in_specs=in_specs, out_specs=out_specs, check_vma=False)
```

```python
import functools
import math

import jax
import jax.numpy as jnp
from jax import lax
from jax.experimental import pallas as pl
from jax.experimental.pallas import tpu as pltpu
from jax.sharding import PartitionSpec as P

FIRST_DILATION = 16
SECOND_DILATION = 64
HALO = FIRST_DILATION + SECOND_DILATION
SPILL = 16
REACH = 3
TABLE = 128
SQRT_HALF = 0.7071067811865476
INV_SQRT_TWO_PI = 0.3989422804014327
F32 = jnp.float32
BF16 = jnp.bfloat16
FAR = -100000.0


def gelu_pair(v):
    half = 0.5 * (1.0 + lax.erf(v * SQRT_HALF))
    return v * half, half + v * jnp.exp(-0.5 * v * v) * INV_SQRT_TWO_PI


def split(v):
    high = v.astype(BF16)
    return high, (v - high.astype(F32)).astype(BF16)


def mm(a, b):
    return lax.dot_general(a, b, (((1,), (0,)), ((), ())), preferred_element_type=F32)


def mm_nt(a, b):
    return lax.dot_general(a, b, (((1,), (1,)), ((), ())), preferred_element_type=F32)


def mm_tn(a, b):
    return lax.dot_general(a, b, (((0,), (0,)), ((), ())), preferred_element_type=F32)


def iota(shape, dim):
    return lax.broadcasted_iota(jnp.int32, shape, dim)


def spread(rows, index):
    out = jnp.broadcast_to(rows[0:1], (index.shape[0], rows.shape[1]))
    for q in range(1, 4):
        out = jnp.where(index == q, rows[q : q + 1], out)
    return out


def call(body, out_shapes, args, scratch=(), limit=24, cost=None):
    in_specs = [
        pl.BlockSpec(memory_space=pltpu.VMEM) for _ in args
    ]
    return pl.pallas_call(
        body,
        out_shape=[jax.ShapeDtypeStruct(s, d) for s, d in out_shapes],
        in_specs=in_specs,
        out_specs=[pl.BlockSpec(memory_space=pltpu.VMEM)] * len(out_shapes),
        scratch_shapes=list(scratch),
        compiler_params=pltpu.CompilerParams(vmem_limit_bytes=limit * 1024 * 1024),
        cost_estimate=cost,
    )(*args)


def base_tables(emb, pick, conv):
    row = iota((16, 1), 0)
    low, high = row & 3, row >> 2
    by_low = spread(emb, low)
    by_high = spread(emb, high)
    act = gelu_pair(by_low)[0].astype(BF16)
    prod_high, prod_low = split(gelu_pair(by_high)[1] * by_low)
    own = mm(jnp.concatenate([act, prod_high, prod_low], axis=0), pick).astype(BF16)
    first = jnp.zeros((16, conv[0].shape[1]), F32)
    second = []
    for k in range(3):
        res = mm(own, conv[k])
        first = jnp.where(high == k, res[0:16], first)
        second.append(res[16:32] + res[32:48])
    return first, jnp.concatenate(second, axis=0)


def position():
    return (2 * lax.axis_index("y") + lax.axis_index("x")) * 2 + lax.axis_index("core")


def prep_kernel(
    narrow_ref, broad_ref, embed_ref, bases_ref, lengths_ref,
    own_ref, x_ref, y_ref, d_ref, small_ref,
):
    me, odd = position(), lax.axis_index("dp") & 1
    cap = bases_ref.shape[1]
    count = jnp.broadcast_to(lengths_ref[...], (1, 128)).astype(F32)
    small_ref[0:4] = embed_ref[...]
    small_ref[4:5, 0:cap] = bases_ref[...].astype(F32)
    small_ref[5:6, 0:128] = count
    width = narrow_ref.shape[1]
    chans = 2 * width
    shard = narrow_ref.shape[0] // 6
    prows = width // 8
    half = 3 * shard // 2
    cut = half - 16
    flat = narrow_ref.at[3 * shard : 6 * shard]
    cot = broad_ref[2 * prows :]
    pick = (iota((chans, shard), 0) == iota((chans, shard), 1) + me * shard).astype(BF16)
    taps = [narrow_ref[k * shard : (k + 1) * shard] for k in range(3)]
    first, second = base_tables(embed_ref[...], pick, taps)
    f_high, f_low = split(first)
    info = jnp.concatenate(
        [
            bases_ref[...].astype(F32),
            count,
            jnp.zeros((1, chans - cap - 128), F32),
        ],
        axis=1,
    )
    tail = jnp.concatenate([f_high.astype(F32), f_low.astype(F32)], axis=1)
    tail = jnp.where(iota((16, 1), 0) == 12, info, tail)
    wide = jnp.concatenate([second[0:24], second[24:48]], axis=1)
    extra = jnp.concatenate([info, jnp.zeros((7, chans), F32)], axis=0)
    own_ref[0:cut, 0:width] = flat[0:cut]
    own_ref[0:cut, width:chans] = flat[half : half + cut]
    own_ref[cut:half] = tail.astype(BF16)
    own_ref[half : half + 16, 0:width] = flat[cut:half]
    own_ref[half : half + 16, width:chans] = flat[half + cut : 2 * half]
    own_ref[half + 16 : half + 16 + 2 * prows] = broad_ref[0 : 2 * prows]
    own_ref[2 * half - 32 : 2 * half] = jnp.concatenate([wide, extra], axis=0).astype(BF16)
    part = own_ref[pl.ds(pl.multiple_of(odd * half, 16), half), :]
    for out in (x_ref, y_ref, d_ref):
        out[0:half] = part
    ahead = (iota((HALO, cap), 1) - iota((HALO, cap), 0) + HALO).astype(F32)
    take = (ahead == count).astype(BF16)
    last = mm(take, cot).astype(BF16)
    chip = me >> 1
    own_ref[2 * half :] = jnp.where((me & 1) == 0, last, cot[0:HALO])
    x_ref[half:] = jnp.where((chip ^ 1) > chip, last, cot[0:HALO])
    d_ref[half:] = jnp.where((chip ^ 3) > chip, last, cot[0:HALO])


def context_body(info_at, cot, r1, r2, l1, l2, hot_f_ref, hot_r_ref, cx_ref):
    cap = cot.shape[0]
    outer = HALO + SECOND_DILATION + FIRST_DILATION
    span = cap + 2 * outer
    counts = [info_at(o)[0:1, cap : cap + 128] for o in range(-REACH, REACH + 1)]
    begin = [None] * (2 * REACH + 1)
    begin[REACH] = jnp.zeros((1, 128), F32)
    for o in range(1, REACH + 1):
        begin[REACH + o] = begin[REACH + o - 1] + counts[REACH + o - 1]
        begin[REACH - o] = begin[REACH - o + 1] - counts[REACH - o]
    lane = iota((1, 128), 1).astype(F32)
    rowpos = (iota((span, 128), 0) - outer).astype(F32)
    total = jnp.zeros((span, 128), F32)
    for o in range(-REACH, REACH + 1):
        code = info_at(o)[0:1, 0:cap] + 1.0
        pos = jnp.where(lane < counts[REACH + o], begin[REACH + o] + lane, FAR)
        total = total + jnp.where(rowpos == pos, code, 0.0)
    codes = jnp.sum(total, axis=1, keepdims=True)
    d = FIRST_DILATION
    left, mid, right = codes[0 : span - 2 * d], codes[d : span - d], codes[2 * d : span]
    rows = span - 2 * d
    lanes = iota((rows, TABLE), 1).astype(F32)
    flip = lambda c: jnp.where(c == 0.0, 0.0, 5.0 - c)
    idx = jnp.where(mid == 0.0, -1.0, (mid - 1.0) * 25.0 + left * 5.0 + right)
    hot_f_ref[...] = (lanes == idx).astype(BF16)
    idx = jnp.where(mid == 0.0, -1.0, (4.0 - mid) * 25.0 + flip(right) * 5.0 + flip(left))
    hot_r_ref[...] = (lanes == idx).astype(BF16)

    own_n = counts[REACH]
    before_n, after_n = counts[REACH - 1], counts[REACH + 1]
    grow = cap + 2 * HALO
    lane_h = iota((1, HALO), 1).astype(F32)
    lane_s = iota((1, SPILL), 1).astype(F32)
    row_h = (iota((grow, HALO), 0) - HALO).astype(F32)
    row_s = (iota((grow, SPILL), 0) - HALO).astype(F32)
    row_o = (iota((grow, cap), 0) - HALO).astype(F32)
    own_pos = jnp.where(lane < own_n, lane, FAR)
    acc = mm((row_o == own_pos).astype(BF16), cot)
    pos = jnp.where(lane_h >= HALO - before_n[:, 0:HALO], lane_h - HALO, FAR)
    acc = acc + mm((row_h == pos).astype(BF16), r1)
    pos = jnp.where(
        counts[REACH - 2][:, 0:SPILL] > 0.0, lane_s - SPILL - before_n[:, 0:SPILL], FAR
    )
    acc = acc + mm((row_s == pos).astype(BF16), r2)
    pos = jnp.where(lane_h < after_n[:, 0:HALO], lane_h + own_n[:, 0:HALO], FAR)
    acc = acc + mm((row_h == pos).astype(BF16), l1)
    pos = jnp.where(
        (counts[REACH + 2][:, 0:SPILL] > 0.0) & (after_n[:, 0:SPILL] < HALO),
        lane_s + own_n[:, 0:SPILL] + after_n[:, 0:SPILL],
        FAR,
    )
    acc = acc + mm((row_s == pos).astype(BF16), l2)
    cx_ref[...] = (0.5 * acc).astype(BF16)


def context_kernel_plain(info_ref, cot_ref, r1_ref, r2_ref, l1_ref, l2_ref, *outs):
    context_body(
        lambda o: info_ref[REACH + o], cot_ref[...], r1_ref[...], r2_ref[...], l1_ref[...],
        l2_ref[...], *outs,
    )


def context_kernel_packed(*refs):
    parts, broad_ref, outs = refs[0:8], refs[8], refs[9:12]
    info_ref, halo_ref = refs[12:]
    me, odd = position(), lax.axis_index("dp") & 1
    chip, core = me >> 1, me & 1
    chans = broad_ref.shape[1]
    prow = chans // 16
    half = 3 * chans // 16
    info_ref[0:REACH] = jnp.zeros((REACH, 8, 256), F32)
    info_ref[REACH + 8 :] = jnp.zeros((REACH, 8, 256), F32)
    for n, part in enumerate(parts):
        peer = me ^ (2 * (n % 4) + n // 4)
        low = part[half - 16 : half].astype(F32)[12:13, 0:256]
        if n % 4 > 0:
            high = part[half - 16 : half].astype(F32)[8:9, 0:256]
            low = jnp.where(odd == 0, low, high)
        info_ref[REACH + peer] = jnp.broadcast_to(low, (8, 256))
    for n in range(2):
        halo_ref[4 * n + chip] = parts[4 * n][2 * half :]
        halo_ref[4 * n + (chip ^ 1)] = parts[4 * n + 1][half:]
        halo_ref[4 * n + (chip ^ 3)] = parts[4 * n + 3][half:]
    r1 = halo_ref[4 + jnp.maximum(chip + core - 1, 0)]
    l1 = halo_ref[4 + jnp.minimum(chip + core, 3)]
    r2 = halo_ref[jnp.maximum(chip - 1, 0)]
    l2 = halo_ref[jnp.minimum(chip + 1, 3)]
    context_body(
        lambda o: info_ref[me + (REACH + o)], broad_ref[2 * prow :], r1, r2[HALO - SPILL :], l1,
        l2[0:SPILL], *outs,
    )


def tower_body(
    first, project, conv, p2, count, emb, cap, cx_ref, hot_f_ref, hot_r_ref,
    s1_ref, gb_ref, g_ref, put,
):
    entry = iota((TABLE, 1), 0)
    by25 = (entry * 1311) >> 15
    by5 = (entry * 6554) >> 15
    in_left = by5 - 5 * by25
    in_right = entry - 5 * by5
    sums = jnp.zeros((TABLE, first.shape[1]), F32)
    for q in range(4):
        sums = jnp.where(in_left == q + 1, first[q : q + 1], sums)
    sums = sums + spread(first[4:8], by25)
    after = jnp.zeros((TABLE, first.shape[1]), F32)
    for q in range(4):
        after = jnp.where(in_right == q + 1, first[8 + q : 9 + q], after)
    value, slope = gelu_pair(sums + after)
    b1 = value.astype(BF16)
    high, low = split(slope)
    s1_ref[0:TABLE] = high
    s1_ref[TABLE : 2 * TABLE] = low
    stream = spread(emb, by25) + mm(b1, project)
    value, slope = gelu_pair(stream)
    a2 = value.astype(BF16)
    s2 = jnp.concatenate(split(slope), axis=0)

    grow = cap + 2 * HALO
    inner = cap + 2 * FIRST_DILATION
    d, D = FIRST_DILATION, SECOND_DILATION
    cx = cx_ref[...]
    back_mid = mm_nt(cx, p2)
    before = jnp.zeros((2 * grow, p2.shape[0]), F32)
    for k in range(3):
        taps = jnp.concatenate(split(mm(a2, conv(k))), axis=0)
        hot = jnp.concatenate(
            [hot_f_ref[k * D : k * D + grow], hot_r_ref[(2 - k) * D : (2 - k) * D + grow]], axis=0
        )
        before = before + mm(jnp.concatenate([hot, hot], axis=1), taps)
    value, slope = gelu_pair(before)
    own_col = (iota((cap, 1), 0).astype(F32) < count).astype(F32)
    own_gb = (cx[HALO : HALO + cap].astype(F32) * own_col).astype(BF16)
    mids = jnp.concatenate(
        [value[HALO : HALO + cap], value[grow + HALO : grow + HALO + cap]], axis=0
    ).astype(BF16)
    put(1, mm_tn(mids, jnp.concatenate([own_gb, own_gb], axis=0)))
    grad_f = (back_mid * slope[0:grow]).astype(BF16)
    grad_r = (back_mid * slope[grow:]).astype(BF16)
    ga = jnp.zeros((2 * inner, cx.shape[1]), F32)
    for k in range(3):
        rows = jnp.concatenate(
            [grad_f[(2 - k) * D : (2 - k) * D + inner], grad_r[k * D : k * D + inner]], axis=0
        )
        ga = ga + mm_nt(rows, conv(k))
    hot = jnp.concatenate(
        [hot_f_ref[2 * D : 2 * D + inner], hot_r_ref[2 * D : 2 * D + inner]], axis=0
    )
    base_g = cx[D : D + inner].astype(F32)
    g = jnp.concatenate([base_g, base_g], axis=0) + ga * mm(
        jnp.concatenate([hot, hot], axis=1), s2
    )
    gb = g.astype(BF16)
    gb_ref[...] = gb
    g_ref[0:cap] = g[d : d + cap]
    g_ref[cap : 2 * cap] = g[inner + d : inner + d + cap]
    col = jnp.concatenate([own_col, own_col], axis=0)
    own_hot = jnp.concatenate([hot[d : d + cap], hot[inner + d : inner + d + cap]], axis=0)
    own_b1 = mm((own_hot.astype(F32) * col).astype(BF16), b1).astype(BF16)
    own_g = jnp.concatenate([gb[d : d + cap], gb[inner + d : inner + d + cap]], axis=0)
    put(0, mm_tn(own_b1, own_g))


def saliency_kernel(
    small_ref, hot_f_ref, hot_r_ref, s1_ref, gb_ref, g_ref, second_ref, p1_ref, sal_ref
):
    cap = g_ref.shape[0] // 2
    inner = cap + 2 * FIRST_DILATION
    d, D = FIRST_DILATION, SECOND_DILATION
    hot = jnp.concatenate(
        [hot_f_ref[2 * D : 2 * D + inner], hot_r_ref[2 * D : 2 * D + inner]], axis=0
    )
    slope = mm(jnp.concatenate([hot, hot], axis=1), s1_ref[...])
    gh = (mm_nt(gb_ref[...], p1_ref[...]) * slope).astype(BF16)
    emb = small_ref[0:4]
    bases = small_ref[4:5, 0:cap]
    wide = jnp.concatenate(split(second_ref[...]), axis=0)
    total = jnp.zeros((4, cap), F32)
    e_high, e_low = split(jnp.concatenate([emb, emb], axis=0))
    for turn in range(2):
        g_high, g_low = split(g_ref[turn * cap : (turn + 1) * cap])
        got = mm_nt(e_high, g_high) + mm_nt(e_high, g_low) + mm_nt(e_low, g_high)
        got = got[0:4]
        table = jnp.zeros((16, cap), F32)
        for k in range(3):
            place = 2 - k if turn == 0 else k
            at = turn * inner + place * d
            both = mm_nt(
                jnp.concatenate(
                    [wide[16 * k : 16 * k + 16], wide[48 + 16 * k : 64 + 16 * k]], axis=0
                ),
                gh[at : at + cap],
            )
            table = table + both[0:16] + both[16:32]
        for q in range(4):
            code = float(q if turn == 0 else 3 - q)
            got = got + jnp.where(bases == code, table[4 * q : 4 * q + 4], 0.0)
        if turn == 1:
            got = jnp.concatenate([got[3 - c : 4 - c] for c in range(4)], axis=0)
        total = total + got
    live = iota((1, cap), 1).astype(F32) < small_ref[5:6, 0:cap]
    sal_ref[...] = jnp.where(live, total * (1.0 / math.sqrt(emb.shape[1])), 0.0)


def tower_kernel_packed(*refs):
    own_parts, plane_parts, dp_parts = refs[0:2], refs[2:8], refs[8:14]
    small_ref, cx_ref, hf_ref, hr_ref = refs[14:18]
    keep_ref, send_ref, s1_ref, gb_ref, g_ref, wide_ref, p1_ref = refs[18:25]
    conv_ref, p2_ref, first_ref, second_ref = refs[25:]
    me = position()
    core, odd = me & 1, lax.axis_index("dp") & 1
    count = small_ref[5:6, 0:1]
    width, chans = p1_ref.shape
    shard = chans // 8
    prow = width // 8
    half = 3 * shard // 2
    cut = half - 16

    def place(side, rows, peer):
        at = peer * shard

        def lay(k, start, size, source, lane):
            conv_ref[k, pl.ds(pl.multiple_of(at + start, 16), size), :] = rows(
                source, size
            )[:, lane : lane + width]

        if side == 0:
            lay(0, 0, shard, 0, 0)
            lay(1, 0, cut - shard, shard, 0)
            lay(1, shard // 2, shard // 2, 0, width)
            lay(2, 0, cut - shard // 2, shard // 2, width)
            tail = rows(cut, 16).astype(F32)
            first_ref[peer] = tail[:, 0:width] + tail[:, width:]
        else:
            lay(1, cut - shard, 16, 0, 0)
            lay(2, shard - 16, 16, 0, width)
            to = pl.ds(pl.multiple_of(peer * prow, 16), prow)
            p2_ref[to, :] = rows(16, prow)
            p1_ref[to, :] = rows(16 + prow, prow)
            second_ref[peer] = rows(half - 32, 32).astype(F32)[0:24]

    for n in range(2):
        for side in range(2):
            rows = lambda a, size, n=n, side=side: own_parts[n][
                side * half + a : side * half + a + size
            ]
            place(side, rows, me ^ n)
    for parity in range(2):

        @pl.when(odd == parity)
        def _():
            for n in range(6):
                peer = me ^ (2 * (n % 3 + 1) + n // 3)
                for side, part in ((parity, plane_parts[n]), (1 - parity, dp_parts[n])):
                    rows = lambda a, size, part=part: part[a : a + size]
                    place(side, rows, peer)

    first = first_ref[0]
    wide = second_ref[0]
    for peer in range(1, 8):
        first = first + first_ref[peer]
        wide = wide + second_ref[peer]
    wide_ref[...] = jnp.concatenate([wide[:, 0:width], wide[:, width : 2 * width]], axis=0)

    def put(block, value):
        rows = value.shape[0] // 4
        for c in range(2):
            even = value[2 * c * rows : (2 * c + 1) * rows]
            uneven = value[(2 * c + 1) * rows : (2 * c + 2) * rows]
            keep_ref[2 * block + c] = jnp.where(core == 0, even, uneven)
            send_ref[2 * block + c] = jnp.where(core == 0, uneven, even).astype(BF16)

    tower_body(
        first, p1_ref[...], lambda k: conv_ref[k], p2_ref[...], count, small_ref[0:4],
        g_ref.shape[0] // 2, cx_ref, hf_ref, hr_ref, s1_ref, gb_ref, g_ref, put,
    )


def tower_kernel_plain(
    first_ref, p1_ref, conv_ref, p2_ref, small_ref, cx_ref, hf_ref, hr_ref,
    grad_ref, s1_ref, gb_ref, g_ref,
):
    def put(block, value):
        rows = value.shape[0]
        grad_ref[block * rows : (block + 1) * rows] = value

    tower_body(
        first_ref[...], p1_ref[...], lambda k: conv_ref[k], p2_ref[...], small_ref[5:6, 0:1],
        small_ref[0:4], g_ref.shape[0] // 2, cx_ref, hf_ref, hr_ref, s1_ref, gb_ref, g_ref, put,
    )


def fold(value):
    width = value.shape[1] // 2
    return jnp.concatenate([value[:, 0:width], value[:, width:]], axis=0)


def core_sum_kernel(keep_ref, recv_ref, own_ref, *outs):
    chip = 2 * lax.axis_index("y") + lax.axis_index("x")
    own_ref[...] = keep_ref[chip] + recv_ref[chip].astype(F32)
    for n, out in enumerate(outs):
        at = chip ^ (n + 1)
        out[...] = (keep_ref[at] + recv_ref[at].astype(F32)).astype(BF16)


def plane_sum_kernel(own_ref, d_ref, y_ref, x_ref, mine_ref, *refs):
    outs, sum_ref = refs[:-1], refs[-1]
    sum_ref[...] = (
        own_ref[...] + x_ref[...].astype(F32) + y_ref[...].astype(F32) + d_ref[...].astype(F32)
    )
    z = lax.axis_index("dp")
    rows = mine_ref.shape[0] // 2
    mine_ref[...] = fold(sum_ref[pl.ds(pl.multiple_of(z * rows, 8), rows), :])
    for n, out in enumerate(outs):
        at = pl.multiple_of((z ^ (n + 1)) * rows, 8)
        out[...] = fold(sum_ref[pl.ds(at, rows), :]).astype(BF16)


def last_sum_kernel(scale, mine_ref, *refs):
    out_ref = refs[-1]
    total = mine_ref[...]
    for ref in refs[:-1]:
        total = total + ref[...].astype(F32)
    total = total * scale
    rows, half = total.shape[0] // 2, total.shape[1] // 128
    for n in range(2 * half):
        at = rows * (n // half)
        lane = 128 * (n % half)
        out_ref[pl.ds(n, rows, stride=2 * half), :] = total[at : at + rows, lane : lane + 128]


def flip_move(array, *axes):
    sizes = [lax.axis_size(a) for a in axes]
    size = math.prod(sizes)
    return lax.ppermute(array, axes, [(i, size - 1 - i) for i in range(size)])


def xor_move(array, axis, bits):
    return lax.ppermute(array, axis, [(i, i ^ bits) for i in range(lax.axis_size(axis))])


def shift_move(array, by, axes):
    size = math.prod(lax.axis_size(a) for a in axes)
    return lax.ppermute(array, axes, [(i, i + by) for i in range(size) if 0 <= i + by < size])


def context_shapes(cap, chans):
    rows = cap + 2 * (HALO + SECOND_DILATION)
    return [((rows, TABLE), BF16), ((rows, TABLE), BF16), ((cap + 2 * HALO, chans), BF16)]


def pass_shapes(cap, chans, width):
    inner = cap + 2 * FIRST_DILATION
    return [((2 * TABLE, width), BF16), ((2 * inner, chans), BF16), ((2 * cap, chans), F32)]


def lines(embed, bases, lengths):
    cap, chans = bases.shape[1], embed.shape[1]
    row = lax.broadcasted_iota(jnp.int32, (8, chans), 0)
    line = jnp.pad(bases, ((0, 0), (0, chans - cap)))
    extra = jnp.where(row == 4, line, jnp.where(row == 5, lengths, 0)).astype(F32)
    return jnp.where(row < 4, jnp.pad(embed, ((0, 4), (0, 0))), extra)


def weight(flops):
    return pl.CostEstimate(flops=flops, bytes_accessed=10**6, transcendentals=0)


def fast_shards(
    bases, lengths, cotangent, c1, p1, c2, p2, embed
):
    cot = cotangent[0]
    cap, chans = cot.shape
    width = c1.shape[2]
    n_dp = lax.axis_size("dp")
    half = 3 * c2.shape[1] // 2
    narrow = jnp.concatenate([c1.reshape(-1, width), c2.reshape(-1, width)], axis=0)
    broad = jnp.concatenate([p2, p1, cot], axis=0)
    own, to_x, to_y, to_d, small = call(
        prep_kernel,
        [
            ((2 * half + HALO, chans), BF16),
            ((half + HALO, chans), BF16),
            ((half, chans), BF16),
            ((half + HALO, chans), BF16),
            ((8, chans), F32),
        ],
        [narrow, broad, embed, bases, lengths],
    )
    plane = [flip_move(to_x, "x"), flip_move(to_y, "y"), flip_move(to_d, "y", "x")]
    other = [xor_move(a[:half], "dp", 1) for a in plane]
    across = lambda arrays: [flip_move(a, "core") for a in arrays]
    rows = chans // 8
    swapped = across([own, *plane])
    hf, hr, cx = call(
        context_kernel_packed,
        context_shapes(cap, chans),
        [own, *plane, *swapped, broad],
        scratch=[
            pltpu.VMEM((8 + 2 * REACH, 8, 256), F32),
            pltpu.VMEM((8, HALO, chans), BF16),
        ],
        cost=weight(10**9),
    )
    keep, send, s1, gb, g, second, p1_full = call(
        tower_kernel_packed,
        [((4, rows, chans), F32), ((4, rows, chans), BF16), *pass_shapes(cap, chans, width)]
        + [((48, width), F32), ((width, chans), BF16)],
        [
            own, swapped[0], *plane, *swapped[1:], *other, *across(other),
            small, cx, hf, hr,
        ],
        scratch=[
            pltpu.VMEM((3, chans, width), BF16),
            pltpu.VMEM((width, chans), BF16),
            pltpu.VMEM((8, 16, width), F32),
            pltpu.VMEM((8, 24, chans), F32),
        ],
        limit=40,
        cost=weight(4 * 10**9),
    )
    recv = flip_move(send, "core")
    (sal,) = call(
        saliency_kernel,
        [((4, cap), F32)],
        [small, hf, hr, s1, gb, g, second, p1_full],
        cost=weight(10**9),
    )
    own, *outs = call(
        core_sum_kernel,
        [((rows, chans), F32)] + [((rows, chans), BF16)] * 3,
        [keep, recv],
    )
    ways = (("x",), ("y",), ("y", "x"))
    got = [flip_move(outs[n], *ways[n]) for n in (2, 1, 0)]
    part = rows // n_dp
    mine, *outs = call(
        plane_sum_kernel,
        [((2 * part, width), F32)] + [((2 * part, width), BF16)] * (n_dp - 1),
        [own, *got],
        scratch=[pltpu.VMEM((rows, chans), F32)],
    )
    got = [xor_move(outs[n], "dp", n + 1) for n in reversed(range(n_dp - 1))]
    scale = 1.0 / math.sqrt(8 * n_dp * cap)
    (grad,) = call(
        functools.partial(last_sum_kernel, scale),
        [((part * chans // 128, 128), F32)],
        [mine, *got],
    )
    return sal[None], grad.reshape(-1)


def plain_shards(bases, lengths, cotangent, c1, p1, c2, p2, embed):
    cot = cotangent[0]
    cap, chans = cot.shape
    width = c1.shape[2]
    me, count = lax.axis_index("seq"), lengths[0, 0]
    shard = c1.shape[1]
    own = lax.dynamic_slice_in_dim(embed, me * shard, shard, 1)
    act, slope = gelu_pair(own)
    taps = c1.astype(F32)
    high = lax.Precision.HIGHEST
    first = jnp.einsum("qc,kcb->kqb", act.astype(BF16).astype(F32), taps, precision=high)
    second = jnp.einsum("qc,dc,kcb->kqdb", slope, own, taps, precision=high)
    first = lax.psum(first.reshape(12, width), "seq")
    second = lax.psum(second.reshape(48, width), "seq")
    first = jnp.concatenate([first, jnp.zeros((4, width), F32)], axis=0)
    p1_full = lax.all_gather(p1, "seq", axis=0, tiled=True)
    p2_full = lax.all_gather(p2, "seq", axis=0, tiled=True)
    conv = lax.all_gather(c2, "seq", axis=1, tiled=True)
    info = jnp.concatenate(
        [bases.astype(F32), jnp.broadcast_to(count.astype(F32), (1, 128))], axis=1
    )
    info = lax.all_gather(info, "seq", axis=0, tiled=True)
    info = jnp.pad(info, ((REACH, REACH), (0, 0)))
    info = lax.dynamic_slice_in_dim(info, me, 2 * REACH + 1, 0)
    info = jnp.broadcast_to(info[:, None, :], (2 * REACH + 1, 8, cap + 128))
    padded = jnp.pad(cot, ((HALO, 0), (0, 0)))
    last = lax.dynamic_slice_in_dim(padded, count, HALO, 0)
    halos = [
        shift_move(last, 1, ("seq",)),
        shift_move(last[HALO - SPILL :], 2, ("seq",)),
        shift_move(cot[:HALO], -1, ("seq",)),
        shift_move(cot[:SPILL], -2, ("seq",)),
    ]
    small = lines(embed, bases, lengths)
    hf, hr, cx = call(
        context_kernel_plain, context_shapes(cap, chans), [info, cot, *halos]
    )
    grad, s1, gb, g = call(
        tower_kernel_plain,
        [((2 * width, chans), F32), *pass_shapes(cap, chans, width)],
        [first, p1_full, conv, p2_full, small, cx, hf, hr],
        limit=40,
    )
    (sal,) = call(
        saliency_kernel,
        [((4, cap), F32)],
        [small, hf, hr, s1, gb, g, second, p1_full],
    )
    scale = 1.0 / math.sqrt(lax.axis_size("seq") * lax.axis_size("dp") * cap)
    grad = lax.psum_scatter(
        grad.reshape(-1) * scale, ("seq", "dp"), scatter_dimension=0, tiled=True
    )
    return sal[None], grad


def solution(mesh):
    run, seq = plain_shards, "seq"
    if mesh.shape["seq"] == 8 and mesh.shape["dp"] == 4:
        run, seq = fast_shards, ("y", "x", "core")
        count = mesh.shape["dp"]
        mesh = jax.sharding.Mesh(mesh.devices.reshape(2, 2, 2, count), (*seq, "dp"))
    every = seq if isinstance(seq, tuple) else (seq,)
    in_specs = (
        P("dp", seq),
        P("dp", seq),
        P("dp", seq, None),
        P(None, seq, None),
        P(seq, None),
        P(None, seq, None),
        P(seq, None),
        P(),
    )
    out_specs = (P("dp", None, seq), P((*every, "dp")))
    return jax.shard_map(run, mesh=mesh, in_specs=in_specs, out_specs=out_specs, check_vma=False)
```

```python
import functools
import math

import jax
import jax.numpy as jnp
from jax import lax
from jax.experimental import pallas as pl
from jax.experimental.pallas import tpu as pltpu
from jax.sharding import PartitionSpec as P

FIRST_DILATION = 16
SECOND_DILATION = 64
HALO = FIRST_DILATION + SECOND_DILATION
SPILL = 16
REACH = 3
TABLE = 128
SQRT_HALF = 0.7071067811865476
INV_SQRT_TWO_PI = 0.3989422804014327
F32 = jnp.float32
BF16 = jnp.bfloat16
FAR = -100000.0


def gelu_pair(v):
    half = 0.5 * (1.0 + lax.erf(v * SQRT_HALF))
    return v * half, half + v * jnp.exp(-0.5 * v * v) * INV_SQRT_TWO_PI


def split(v):
    high = v.astype(BF16)
    return high, (v - high.astype(F32)).astype(BF16)


def mm(a, b):
    return lax.dot_general(a, b, (((1,), (0,)), ((), ())), preferred_element_type=F32)


def mm_nt(a, b):
    return lax.dot_general(a, b, (((1,), (1,)), ((), ())), preferred_element_type=F32)


def mm_tn(a, b):
    return lax.dot_general(a, b, (((0,), (0,)), ((), ())), preferred_element_type=F32)


def iota(shape, dim):
    return lax.broadcasted_iota(jnp.int32, shape, dim)


def spread(rows, index):
    out = jnp.broadcast_to(rows[0:1], (index.shape[0], rows.shape[1]))
    for q in range(1, 4):
        out = jnp.where(index == q, rows[q : q + 1], out)
    return out


def call(body, out_shapes, args, scratch=(), limit=24, cost=None):
    in_specs = [
        pl.BlockSpec(memory_space=pltpu.VMEM) for _ in args
    ]
    return pl.pallas_call(
        body,
        out_shape=[jax.ShapeDtypeStruct(s, d) for s, d in out_shapes],
        in_specs=in_specs,
        out_specs=[pl.BlockSpec(memory_space=pltpu.VMEM)] * len(out_shapes),
        scratch_shapes=list(scratch),
        compiler_params=pltpu.CompilerParams(vmem_limit_bytes=limit * 1024 * 1024),
        cost_estimate=cost,
    )(*args)


def base_tables(emb, pick, conv):
    row = iota((16, 1), 0)
    low, high = row & 3, row >> 2
    by_low = spread(emb, low)
    by_high = spread(emb, high)
    act = gelu_pair(by_low)[0].astype(BF16)
    prod_high, prod_low = split(gelu_pair(by_high)[1] * by_low)
    own = mm(jnp.concatenate([act, prod_high, prod_low], axis=0), pick).astype(BF16)
    first = jnp.zeros((16, conv[0].shape[1]), F32)
    second = []
    for k in range(3):
        res = mm(own, conv[k])
        first = jnp.where(high == k, res[0:16], first)
        second.append(res[16:32] + res[32:48])
    return first, jnp.concatenate(second, axis=0)


def position():
    return (2 * lax.axis_index("y") + lax.axis_index("x")) * 2 + lax.axis_index("core")


def prep_kernel(
    narrow_ref, broad_ref, embed_ref, bases_ref, lengths_ref,
    own_ref, x_ref, y_ref, d_ref, edge_ref, small_ref,
):
    me, odd = position(), lax.axis_index("dp") & 1
    cap = bases_ref.shape[1]
    count = jnp.broadcast_to(lengths_ref[...], (1, 128)).astype(F32)
    small_ref[0:4] = embed_ref[...]
    small_ref[4:5, 0:cap] = bases_ref[...].astype(F32)
    small_ref[5:6, 0:128] = count
    width = narrow_ref.shape[1]
    chans = 2 * width
    shard = narrow_ref.shape[0] // 6
    prows = width // 8
    half = 3 * shard // 2
    cut = half - 16
    flat = narrow_ref.at[3 * shard : 6 * shard]
    cot = broad_ref[2 * prows :]
    pick = (iota((chans, shard), 0) == iota((chans, shard), 1) + me * shard).astype(BF16)
    taps = [narrow_ref[k * shard : (k + 1) * shard] for k in range(3)]
    first, second = base_tables(embed_ref[...], pick, taps)
    f_high, f_low = split(first)
    info = jnp.concatenate(
        [
            bases_ref[...].astype(F32),
            count,
            jnp.zeros((1, chans - cap - 128), F32),
        ],
        axis=1,
    )
    tail = jnp.concatenate([f_high.astype(F32), f_low.astype(F32)], axis=1)
    tail = jnp.where(iota((16, 1), 0) == 12, info, tail)
    wide = jnp.concatenate([second[0:24], second[24:48]], axis=1)
    extra = jnp.concatenate([info, jnp.zeros((7, chans), F32)], axis=0)
    own_ref[0:cut, 0:width] = flat[0:cut]
    own_ref[0:cut, width:chans] = flat[half : half + cut]
    own_ref[cut:half] = tail.astype(BF16)
    own_ref[half : half + 16, 0:width] = flat[cut:half]
    own_ref[half : half + 16, width:chans] = flat[half + cut : 2 * half]
    own_ref[half + 16 : half + 16 + 2 * prows] = broad_ref[0 : 2 * prows]
    own_ref[2 * half - 32 : 2 * half] = jnp.concatenate([wide, extra], axis=0).astype(BF16)
    part = own_ref[pl.ds(pl.multiple_of(odd * half, 16), half), :]
    for out in (x_ref, y_ref, d_ref):
        out[0:half] = part
    ahead = (iota((HALO, cap), 1) - iota((HALO, cap), 0) + HALO).astype(F32)
    last = mm((ahead == count).astype(BF16), cot).astype(BF16)
    chip, lower = me >> 1, (me & 1) == 0
    own_ref[2 * half :] = jnp.where(lower, last, cot[0:HALO])
    edge_ref[...] = jnp.where(lower, cot[0:HALO], last)
    for out, bits in ((x_ref, 1), (d_ref, 3)):
        upward = (chip ^ bits) > chip
        out[half:] = jnp.where(upward, last[HALO - SPILL :], cot[0:SPILL])


def context_body(info_at, cot, r1, r2, l1, l2, hot_f_ref, hot_r_ref, cx_ref):
    cap = cot.shape[0]
    outer = HALO + SECOND_DILATION + FIRST_DILATION
    span = cap + 2 * outer
    counts = [info_at(o)[0:1, cap : cap + 128] for o in range(-REACH, REACH + 1)]
    begin = [None] * (2 * REACH + 1)
    begin[REACH] = jnp.zeros((1, 128), F32)
    for o in range(1, REACH + 1):
        begin[REACH + o] = begin[REACH + o - 1] + counts[REACH + o - 1]
        begin[REACH - o] = begin[REACH - o + 1] - counts[REACH - o]
    lane = iota((1, 128), 1).astype(F32)
    rowpos = (iota((span, 128), 0) - outer).astype(F32)
    total = jnp.zeros((span, 128), F32)
    for o in range(-REACH, REACH + 1):
        code = info_at(o)[0:1, 0:cap] + 1.0
        pos = jnp.where(lane < counts[REACH + o], begin[REACH + o] + lane, FAR)
        total = total + jnp.where(rowpos == pos, code, 0.0)
    codes = jnp.sum(total, axis=1, keepdims=True)
    d = FIRST_DILATION
    left, mid, right = codes[0 : span - 2 * d], codes[d : span - d], codes[2 * d : span]
    rows = span - 2 * d
    lanes = iota((rows, TABLE), 1).astype(F32)
    flip = lambda c: jnp.where(c == 0.0, 0.0, 5.0 - c)
    idx = jnp.where(mid == 0.0, -1.0, (mid - 1.0) * 25.0 + left * 5.0 + right)
    hot_f_ref[...] = (lanes == idx).astype(BF16)
    idx = jnp.where(mid == 0.0, -1.0, (4.0 - mid) * 25.0 + flip(right) * 5.0 + flip(left))
    hot_r_ref[...] = (lanes == idx).astype(BF16)

    own_n = counts[REACH]
    before_n, after_n = counts[REACH - 1], counts[REACH + 1]
    grow = cap + 2 * HALO
    lane_h = iota((1, HALO), 1).astype(F32)
    lane_s = iota((1, SPILL), 1).astype(F32)
    row_h = (iota((grow, HALO), 0) - HALO).astype(F32)
    row_s = (iota((grow, SPILL), 0) - HALO).astype(F32)
    row_o = (iota((grow, cap), 0) - HALO).astype(F32)
    own_pos = jnp.where(lane < own_n, lane, FAR)
    acc = mm((row_o == own_pos).astype(BF16), cot)
    pos = jnp.where(lane_h >= HALO - before_n[:, 0:HALO], lane_h - HALO, FAR)
    acc = acc + mm((row_h == pos).astype(BF16), r1)
    pos = jnp.where(
        counts[REACH - 2][:, 0:SPILL] > 0.0, lane_s - SPILL - before_n[:, 0:SPILL], FAR
    )
    acc = acc + mm((row_s == pos).astype(BF16), r2)
    pos = jnp.where(lane_h < after_n[:, 0:HALO], lane_h + own_n[:, 0:HALO], FAR)
    acc = acc + mm((row_h == pos).astype(BF16), l1)
    pos = jnp.where(
        (counts[REACH + 2][:, 0:SPILL] > 0.0) & (after_n[:, 0:SPILL] < HALO),
        lane_s + own_n[:, 0:SPILL] + after_n[:, 0:SPILL],
        FAR,
    )
    acc = acc + mm((row_s == pos).astype(BF16), l2)
    cx_ref[...] = (0.5 * acc).astype(BF16)


def context_kernel_plain(info_ref, cot_ref, r1_ref, r2_ref, l1_ref, l2_ref, *outs):
    context_body(
        lambda o: info_ref[REACH + o], cot_ref[...], r1_ref[...], r2_ref[...], l1_ref[...],
        l2_ref[...], *outs,
    )


def context_kernel_packed(*refs):
    parts, edge_ref, broad_ref, outs = refs[0:8], refs[8], refs[9], refs[10:13]
    info_ref = refs[13]
    me, odd = position(), lax.axis_index("dp") & 1
    chip, core = me >> 1, me & 1
    chans = broad_ref.shape[1]
    prow = chans // 16
    half = 3 * chans // 16
    info_ref[0:REACH] = jnp.zeros((REACH, 8, 256), F32)
    info_ref[REACH + 8 :] = jnp.zeros((REACH, 8, 256), F32)
    for n, part in enumerate(parts):
        peer = me ^ (2 * (n % 4) + n // 4)
        low = part[half - 16 : half].astype(F32)[12:13, 0:256]
        if n % 4 > 0:
            high = part[half - 16 : half].astype(F32)[8:9, 0:256]
            low = jnp.where(odd == 0, low, high)
        info_ref[REACH + peer] = jnp.broadcast_to(low, (8, 256))
    odd_edge, even_edge = edge_ref[...], parts[4][2 * half :]
    x_spill, d_spill = parts[1][half:], parts[3][half:]
    r1 = jnp.where(core == 0, odd_edge, even_edge)
    l1 = jnp.where(core == 0, even_edge, odd_edge)
    r2 = jnp.where(chip == 2, d_spill, x_spill)
    l2 = jnp.where(chip == 1, d_spill, x_spill)
    context_body(
        lambda o: info_ref[me + (REACH + o)], broad_ref[2 * prow :], r1, r2, l1, l2, *outs,
    )


def tower_body(
    first, project, conv, p2, count, emb, cap, cx_ref, hot_f_ref, hot_r_ref,
    s1_ref, gb_ref, g_ref, put,
):
    entry = iota((TABLE, 1), 0)
    by25 = (entry * 1311) >> 15
    by5 = (entry * 6554) >> 15
    in_left = by5 - 5 * by25
    in_right = entry - 5 * by5
    sums = jnp.zeros((TABLE, first.shape[1]), F32)
    for q in range(4):
        sums = jnp.where(in_left == q + 1, first[q : q + 1], sums)
    sums = sums + spread(first[4:8], by25)
    after = jnp.zeros((TABLE, first.shape[1]), F32)
    for q in range(4):
        after = jnp.where(in_right == q + 1, first[8 + q : 9 + q], after)
    value, slope = gelu_pair(sums + after)
    b1 = value.astype(BF16)
    high, low = split(slope)
    s1_ref[0:TABLE] = high
    s1_ref[TABLE : 2 * TABLE] = low
    stream = spread(emb, by25) + mm(b1, project)
    value, slope = gelu_pair(stream)
    a2 = value.astype(BF16)
    s2 = jnp.concatenate(split(slope), axis=0)

    grow = cap + 2 * HALO
    inner = cap + 2 * FIRST_DILATION
    d, D = FIRST_DILATION, SECOND_DILATION
    cx = cx_ref[...]
    back_mid = mm_nt(cx, p2)
    before = jnp.zeros((2 * grow, p2.shape[0]), F32)
    for k in range(3):
        taps = jnp.concatenate(split(mm(a2, conv(k))), axis=0)
        hot = jnp.concatenate(
            [hot_f_ref[k * D : k * D + grow], hot_r_ref[(2 - k) * D : (2 - k) * D + grow]], axis=0
        )
        before = before + mm(jnp.concatenate([hot, hot], axis=1), taps)
    value, slope = gelu_pair(before)
    own_col = (iota((cap, 1), 0).astype(F32) < count).astype(F32)
    own_gb = (cx[HALO : HALO + cap].astype(F32) * own_col).astype(BF16)
    mids = jnp.concatenate(
        [value[HALO : HALO + cap], value[grow + HALO : grow + HALO + cap]], axis=0
    ).astype(BF16)
    put(1, mm_tn(mids, jnp.concatenate([own_gb, own_gb], axis=0)))
    grad_f = (back_mid * slope[0:grow]).astype(BF16)
    grad_r = (back_mid * slope[grow:]).astype(BF16)
    ga = jnp.zeros((2 * inner, cx.shape[1]), F32)
    for k in range(3):
        rows = jnp.concatenate(
            [grad_f[(2 - k) * D : (2 - k) * D + inner], grad_r[k * D : k * D + inner]], axis=0
        )
        ga = ga + mm_nt(rows, conv(k))
    hot = jnp.concatenate(
        [hot_f_ref[2 * D : 2 * D + inner], hot_r_ref[2 * D : 2 * D + inner]], axis=0
    )
    base_g = cx[D : D + inner].astype(F32)
    g = jnp.concatenate([base_g, base_g], axis=0) + ga * mm(
        jnp.concatenate([hot, hot], axis=1), s2
    )
    gb = g.astype(BF16)
    gb_ref[...] = gb
    g_ref[0:cap] = g[d : d + cap]
    g_ref[cap : 2 * cap] = g[inner + d : inner + d + cap]
    col = jnp.concatenate([own_col, own_col], axis=0)
    own_hot = jnp.concatenate([hot[d : d + cap], hot[inner + d : inner + d + cap]], axis=0)
    own_b1 = mm((own_hot.astype(F32) * col).astype(BF16), b1).astype(BF16)
    own_g = jnp.concatenate([gb[d : d + cap], gb[inner + d : inner + d + cap]], axis=0)
    put(0, mm_tn(own_b1, own_g))


def saliency_kernel(
    small_ref, hot_f_ref, hot_r_ref, s1_ref, gb_ref, g_ref, second_ref, p1_ref, sal_ref
):
    cap = g_ref.shape[0] // 2
    inner = cap + 2 * FIRST_DILATION
    d, D = FIRST_DILATION, SECOND_DILATION
    hot = jnp.concatenate(
        [hot_f_ref[2 * D : 2 * D + inner], hot_r_ref[2 * D : 2 * D + inner]], axis=0
    )
    slope = mm(jnp.concatenate([hot, hot], axis=1), s1_ref[...])
    gh = (mm_nt(gb_ref[...], p1_ref[...]) * slope).astype(BF16)
    emb = small_ref[0:4]
    bases = small_ref[4:5, 0:cap]
    wide = jnp.concatenate(split(second_ref[...]), axis=0)
    total = jnp.zeros((4, cap), F32)
    e_high, e_low = split(jnp.concatenate([emb, emb], axis=0))
    for turn in range(2):
        g_high, g_low = split(g_ref[turn * cap : (turn + 1) * cap])
        got = mm_nt(e_high, g_high) + mm_nt(e_high, g_low) + mm_nt(e_low, g_high)
        got = got[0:4]
        table = jnp.zeros((16, cap), F32)
        for k in range(3):
            place = 2 - k if turn == 0 else k
            at = turn * inner + place * d
            both = mm_nt(
                jnp.concatenate(
                    [wide[16 * k : 16 * k + 16], wide[48 + 16 * k : 64 + 16 * k]], axis=0
                ),
                gh[at : at + cap],
            )
            table = table + both[0:16] + both[16:32]
        for q in range(4):
            code = float(q if turn == 0 else 3 - q)
            got = got + jnp.where(bases == code, table[4 * q : 4 * q + 4], 0.0)
        if turn == 1:
            got = jnp.concatenate([got[3 - c : 4 - c] for c in range(4)], axis=0)
        total = total + got
    live = iota((1, cap), 1).astype(F32) < small_ref[5:6, 0:cap]
    sal_ref[...] = jnp.where(live, total * (1.0 / math.sqrt(emb.shape[1])), 0.0)


def tower_kernel_packed(*refs):
    own_parts, plane_parts, dp_parts = refs[0:2], refs[2:8], refs[8:14]
    small_ref, cx_ref, hf_ref, hr_ref = refs[14:18]
    keep_ref, send_ref, s1_ref, gb_ref, g_ref, wide_ref, p1_ref = refs[18:25]
    conv_ref, p2_ref, first_ref, second_ref = refs[25:]
    me = position()
    core, odd = me & 1, lax.axis_index("dp") & 1
    count = small_ref[5:6, 0:1]
    width, chans = p1_ref.shape
    shard = chans // 8
    prow = width // 8
    half = 3 * shard // 2
    cut = half - 16

    def place(side, rows, peer):
        at = peer * shard

        def lay(k, start, size, source, lane):
            conv_ref[k, pl.ds(pl.multiple_of(at + start, 16), size), :] = rows(
                source, size
            )[:, lane : lane + width]

        if side == 0:
            lay(0, 0, shard, 0, 0)
            lay(1, 0, cut - shard, shard, 0)
            lay(1, shard // 2, shard // 2, 0, width)
            lay(2, 0, cut - shard // 2, shard // 2, width)
            tail = rows(cut, 16).astype(F32)
            first_ref[peer] = tail[:, 0:width] + tail[:, width:]
        else:
            lay(1, cut - shard, 16, 0, 0)
            lay(2, shard - 16, 16, 0, width)
            to = pl.ds(pl.multiple_of(peer * prow, 16), prow)
            p2_ref[to, :] = rows(16, prow)
            p1_ref[to, :] = rows(16 + prow, prow)
            second_ref[peer] = rows(half - 32, 32).astype(F32)[0:24]

    for n in range(2):
        for side in range(2):
            rows = lambda a, size, n=n, side=side: own_parts[n][
                side * half + a : side * half + a + size
            ]
            place(side, rows, me ^ n)
    for parity in range(2):

        @pl.when(odd == parity)
        def _():
            for n in range(6):
                peer = me ^ (2 * (n % 3 + 1) + n // 3)
                for side, part in ((parity, plane_parts[n]), (1 - parity, dp_parts[n])):
                    rows = lambda a, size, part=part: part[a : a + size]
                    place(side, rows, peer)

    first = first_ref[0]
    wide = second_ref[0]
    for peer in range(1, 8):
        first = first + first_ref[peer]
        wide = wide + second_ref[peer]
    wide_ref[...] = jnp.concatenate([wide[:, 0:width], wide[:, width : 2 * width]], axis=0)

    def put(block, value):
        rows = value.shape[0] // 4
        for c in range(2):
            even = value[2 * c * rows : (2 * c + 1) * rows]
            uneven = value[(2 * c + 1) * rows : (2 * c + 2) * rows]
            keep_ref[2 * block + c] = jnp.where(core == 0, even, uneven)
            send_ref[2 * block + c] = jnp.where(core == 0, uneven, even).astype(BF16)

    tower_body(
        first, p1_ref[...], lambda k: conv_ref[k], p2_ref[...], count, small_ref[0:4],
        g_ref.shape[0] // 2, cx_ref, hf_ref, hr_ref, s1_ref, gb_ref, g_ref, put,
    )


def tower_kernel_plain(
    first_ref, p1_ref, conv_ref, p2_ref, small_ref, cx_ref, hf_ref, hr_ref,
    grad_ref, s1_ref, gb_ref, g_ref,
):
    def put(block, value):
        rows = value.shape[0]
        grad_ref[block * rows : (block + 1) * rows] = value

    tower_body(
        first_ref[...], p1_ref[...], lambda k: conv_ref[k], p2_ref[...], small_ref[5:6, 0:1],
        small_ref[0:4], g_ref.shape[0] // 2, cx_ref, hf_ref, hr_ref, s1_ref, gb_ref, g_ref, put,
    )


def fold(value):
    width = value.shape[1] // 2
    return jnp.concatenate([value[:, 0:width], value[:, width:]], axis=0)


def core_sum_kernel(keep_ref, recv_ref, own_ref, *outs):
    chip = 2 * lax.axis_index("y") + lax.axis_index("x")
    own_ref[...] = keep_ref[chip] + recv_ref[chip].astype(F32)
    for n, out in enumerate(outs):
        at = chip ^ (n + 1)
        out[...] = (keep_ref[at] + recv_ref[at].astype(F32)).astype(BF16)


def plane_sum_kernel(own_ref, d_ref, y_ref, x_ref, mine_ref, *refs):
    outs, sum_ref = refs[:-1], refs[-1]
    sum_ref[...] = (
        own_ref[...] + x_ref[...].astype(F32) + y_ref[...].astype(F32) + d_ref[...].astype(F32)
    )
    z = lax.axis_index("dp")
    rows = mine_ref.shape[0] // 2
    mine_ref[...] = fold(sum_ref[pl.ds(pl.multiple_of(z * rows, 8), rows), :])
    for n, out in enumerate(outs):
        at = pl.multiple_of((z ^ (n + 1)) * rows, 8)
        out[...] = fold(sum_ref[pl.ds(at, rows), :]).astype(BF16)


def last_sum_kernel(scale, mine_ref, *refs):
    out_ref = refs[-1]
    total = mine_ref[...]
    for ref in refs[:-1]:
        total = total + ref[...].astype(F32)
    total = total * scale
    rows, half = total.shape[0] // 2, total.shape[1] // 128
    for n in range(2 * half):
        at = rows * (n // half)
        lane = 128 * (n % half)
        out_ref[pl.ds(n, rows, stride=2 * half), :] = total[at : at + rows, lane : lane + 128]


def flip_move(array, *axes):
    sizes = [lax.axis_size(a) for a in axes]
    size = math.prod(sizes)
    return lax.ppermute(array, axes, [(i, size - 1 - i) for i in range(size)])


def xor_move(array, axis, bits):
    return lax.ppermute(array, axis, [(i, i ^ bits) for i in range(lax.axis_size(axis))])


def shift_move(array, by, axes):
    size = math.prod(lax.axis_size(a) for a in axes)
    return lax.ppermute(array, axes, [(i, i + by) for i in range(size) if 0 <= i + by < size])


def context_shapes(cap, chans):
    rows = cap + 2 * (HALO + SECOND_DILATION)
    return [((rows, TABLE), BF16), ((rows, TABLE), BF16), ((cap + 2 * HALO, chans), BF16)]


def pass_shapes(cap, chans, width):
    inner = cap + 2 * FIRST_DILATION
    return [((2 * TABLE, width), BF16), ((2 * inner, chans), BF16), ((2 * cap, chans), F32)]


def lines(embed, bases, lengths):
    cap, chans = bases.shape[1], embed.shape[1]
    row = lax.broadcasted_iota(jnp.int32, (8, chans), 0)
    line = jnp.pad(bases, ((0, 0), (0, chans - cap)))
    extra = jnp.where(row == 4, line, jnp.where(row == 5, lengths, 0)).astype(F32)
    return jnp.where(row < 4, jnp.pad(embed, ((0, 4), (0, 0))), extra)


def weight(flops):
    return pl.CostEstimate(flops=flops, bytes_accessed=10**6, transcendentals=0)


def fast_shards(
    bases, lengths, cotangent, c1, p1, c2, p2, embed
):
    cot = cotangent[0]
    cap, chans = cot.shape
    width = c1.shape[2]
    n_dp = lax.axis_size("dp")
    half = 3 * c2.shape[1] // 2
    narrow = jnp.concatenate([c1.reshape(-1, width), c2.reshape(-1, width)], axis=0)
    broad = jnp.concatenate([p2, p1, cot], axis=0)
    own, to_x, to_y, to_d, edge, small = call(
        prep_kernel,
        [
            ((2 * half + HALO, chans), BF16),
            ((half + SPILL, chans), BF16),
            ((half, chans), BF16),
            ((half + SPILL, chans), BF16),
            ((HALO, chans), BF16),
            ((8, chans), F32),
        ],
        [narrow, broad, embed, bases, lengths],
    )
    plane = [flip_move(to_x, "x"), flip_move(to_y, "y"), flip_move(to_d, "y", "x")]
    other = [xor_move(a, "dp", 1) for a in plane]
    edge, _, _ = lax.optimization_barrier((edge, plane[0], plane[2]))
    edge = lax.ppermute(
        edge, ("y", "x", "core"), [(i, i + 2 * (i & 1) - 1) for i in range(1, 7)]
    )
    across = lambda arrays: [flip_move(a, "core") for a in arrays]
    rows = chans // 8
    late, late_y, _ = lax.optimization_barrier((own, plane[1], other[1]))
    late_x, late_d, _ = lax.optimization_barrier((plane[0], plane[2], other[0]))
    swapped = across([late, late_x, late_y, late_d])
    hf, hr, cx = call(
        context_kernel_packed,
        context_shapes(cap, chans),
        [own, *plane, *swapped, edge, broad],
        scratch=[pltpu.VMEM((8 + 2 * REACH, 8, 256), F32)],
        cost=weight(10**9),
    )
    keep, send, s1, gb, g, second, p1_full = call(
        tower_kernel_packed,
        [((4, rows, chans), F32), ((4, rows, chans), BF16), *pass_shapes(cap, chans, width)]
        + [((48, width), F32), ((width, chans), BF16)],
        [
            own, swapped[0], *plane, *swapped[1:], *other, *across(other),
            small, cx, hf, hr,
        ],
        scratch=[
            pltpu.VMEM((3, chans, width), BF16),
            pltpu.VMEM((width, chans), BF16),
            pltpu.VMEM((8, 16, width), F32),
            pltpu.VMEM((8, 24, chans), F32),
        ],
        limit=40,
        cost=weight(4 * 10**9),
    )
    recv = flip_move(send, "core")
    (sal,) = call(
        saliency_kernel,
        [((4, cap), F32)],
        [small, hf, hr, s1, gb, g, second, p1_full],
        cost=weight(10**9),
    )
    own, *outs = call(
        core_sum_kernel,
        [((rows, chans), F32)] + [((rows, chans), BF16)] * 3,
        [keep, recv],
    )
    ways = (("x",), ("y",), ("y", "x"))
    got = [flip_move(outs[n], *ways[n]) for n in (2, 1, 0)]
    part = rows // n_dp
    mine, *outs = call(
        plane_sum_kernel,
        [((2 * part, width), F32)] + [((2 * part, width), BF16)] * (n_dp - 1),
        [own, *got],
        scratch=[pltpu.VMEM((rows, chans), F32)],
    )
    got = [xor_move(outs[n], "dp", n + 1) for n in reversed(range(n_dp - 1))]
    scale = 1.0 / math.sqrt(8 * n_dp * cap)
    (grad,) = call(
        functools.partial(last_sum_kernel, scale),
        [((part * chans // 128, 128), F32)],
        [mine, *got],
    )
    return sal[None], grad.reshape(-1)


def plain_shards(bases, lengths, cotangent, c1, p1, c2, p2, embed):
    cot = cotangent[0]
    cap, chans = cot.shape
    width = c1.shape[2]
    me, count = lax.axis_index("seq"), lengths[0, 0]
    shard = c1.shape[1]
    own = lax.dynamic_slice_in_dim(embed, me * shard, shard, 1)
    act, slope = gelu_pair(own)
    taps = c1.astype(F32)
    high = lax.Precision.HIGHEST
    first = jnp.einsum("qc,kcb->kqb", act.astype(BF16).astype(F32), taps, precision=high)
    second = jnp.einsum("qc,dc,kcb->kqdb", slope, own, taps, precision=high)
    first = lax.psum(first.reshape(12, width), "seq")
    second = lax.psum(second.reshape(48, width), "seq")
    first = jnp.concatenate([first, jnp.zeros((4, width), F32)], axis=0)
    p1_full = lax.all_gather(p1, "seq", axis=0, tiled=True)
    p2_full = lax.all_gather(p2, "seq", axis=0, tiled=True)
    conv = lax.all_gather(c2, "seq", axis=1, tiled=True)
    info = jnp.concatenate(
        [bases.astype(F32), jnp.broadcast_to(count.astype(F32), (1, 128))], axis=1
    )
    info = lax.all_gather(info, "seq", axis=0, tiled=True)
    info = jnp.pad(info, ((REACH, REACH), (0, 0)))
    info = lax.dynamic_slice_in_dim(info, me, 2 * REACH + 1, 0)
    info = jnp.broadcast_to(info[:, None, :], (2 * REACH + 1, 8, cap + 128))
    padded = jnp.pad(cot, ((HALO, 0), (0, 0)))
    last = lax.dynamic_slice_in_dim(padded, count, HALO, 0)
    halos = [
        shift_move(last, 1, ("seq",)),
        shift_move(last[HALO - SPILL :], 2, ("seq",)),
        shift_move(cot[:HALO], -1, ("seq",)),
        shift_move(cot[:SPILL], -2, ("seq",)),
    ]
    small = lines(embed, bases, lengths)
    hf, hr, cx = call(
        context_kernel_plain, context_shapes(cap, chans), [info, cot, *halos]
    )
    grad, s1, gb, g = call(
        tower_kernel_plain,
        [((2 * width, chans), F32), *pass_shapes(cap, chans, width)],
        [first, p1_full, conv, p2_full, small, cx, hf, hr],
        limit=40,
    )
    (sal,) = call(
        saliency_kernel,
        [((4, cap), F32)],
        [small, hf, hr, s1, gb, g, second, p1_full],
    )
    scale = 1.0 / math.sqrt(lax.axis_size("seq") * lax.axis_size("dp") * cap)
    grad = lax.psum_scatter(
        grad.reshape(-1) * scale, ("seq", "dp"), scatter_dimension=0, tiled=True
    )
    return sal[None], grad


def solution(mesh):
    run, seq = plain_shards, "seq"
    if mesh.shape["seq"] == 8 and mesh.shape["dp"] == 4:
        run, seq = fast_shards, ("y", "x", "core")
        count = mesh.shape["dp"]
        mesh = jax.sharding.Mesh(mesh.devices.reshape(2, 2, 2, count), (*seq, "dp"))
    every = seq if isinstance(seq, tuple) else (seq,)
    in_specs = (
        P("dp", seq),
        P("dp", seq),
        P("dp", seq, None),
        P(None, seq, None),
        P(seq, None),
        P(None, seq, None),
        P(seq, None),
        P(),
    )
    out_specs = (P("dp", None, seq), P((*every, "dp")))
    return jax.shard_map(run, mesh=mesh, in_specs=in_specs, out_specs=out_specs, check_vma=False)
```

```python
import functools
import math

import jax
import jax.numpy as jnp
from jax import lax
from jax.experimental import pallas as pl
from jax.experimental.pallas import tpu as pltpu
from jax.sharding import PartitionSpec as P

FIRST_DILATION = 16
SECOND_DILATION = 64
HALO = FIRST_DILATION + SECOND_DILATION
SPILL = 16
REACH = 3
TABLE = 128
SQRT_HALF = 0.7071067811865476
INV_SQRT_TWO_PI = 0.3989422804014327
F32 = jnp.float32
BF16 = jnp.bfloat16
FAR = -100000.0


def gelu_pair(v):
    half = 0.5 * (1.0 + lax.erf(v * SQRT_HALF))
    return v * half, half + v * jnp.exp(-0.5 * v * v) * INV_SQRT_TWO_PI


def split(v):
    high = v.astype(BF16)
    return high, (v - high.astype(F32)).astype(BF16)


def mm(a, b):
    return lax.dot_general(a, b, (((1,), (0,)), ((), ())), preferred_element_type=F32)


def mm_nt(a, b):
    return lax.dot_general(a, b, (((1,), (1,)), ((), ())), preferred_element_type=F32)


def mm_tn(a, b):
    return lax.dot_general(a, b, (((0,), (0,)), ((), ())), preferred_element_type=F32)


def iota(shape, dim):
    return lax.broadcasted_iota(jnp.int32, shape, dim)


def spread(rows, index):
    out = jnp.broadcast_to(rows[0:1], (index.shape[0], rows.shape[1]))
    for q in range(1, 4):
        out = jnp.where(index == q, rows[q : q + 1], out)
    return out


def call(body, out_shapes, args, scratch=(), limit=24, cost=None):
    in_specs = [
        pl.BlockSpec(memory_space=pltpu.VMEM) for _ in args
    ]
    return pl.pallas_call(
        body,
        out_shape=[jax.ShapeDtypeStruct(s, d) for s, d in out_shapes],
        in_specs=in_specs,
        out_specs=[pl.BlockSpec(memory_space=pltpu.VMEM)] * len(out_shapes),
        scratch_shapes=list(scratch),
        compiler_params=pltpu.CompilerParams(vmem_limit_bytes=limit * 1024 * 1024),
        cost_estimate=cost,
    )(*args)


def base_tables(emb, pick, conv):
    row = iota((16, 1), 0)
    low, high = row & 3, row >> 2
    by_low = spread(emb, low)
    by_high = spread(emb, high)
    act = gelu_pair(by_low)[0].astype(BF16)
    prod_high, prod_low = split(gelu_pair(by_high)[1] * by_low)
    own = mm(jnp.concatenate([act, prod_high, prod_low], axis=0), pick).astype(BF16)
    first = jnp.zeros((16, conv[0].shape[1]), F32)
    second = []
    for k in range(3):
        res = mm(own, conv[k])
        first = jnp.where(high == k, res[0:16], first)
        second.append(res[16:32] + res[32:48])
    return first, jnp.concatenate(second, axis=0)


def position():
    return (2 * lax.axis_index("y") + lax.axis_index("x")) * 2 + lax.axis_index("core")


def prep_kernel(
    narrow_ref, broad_ref, cot_ref, embed_ref, bases_ref, lengths_ref,
    own_ref, x_ref, y_ref, d_ref, small_ref, cot_out,
):
    me, odd = position(), lax.axis_index("dp") & 1
    cap = bases_ref.shape[1]
    count = jnp.broadcast_to(lengths_ref[...], (1, 128)).astype(F32)
    small_ref[0:4] = embed_ref[...]
    small_ref[4:5, 0:cap] = bases_ref[...].astype(F32)
    small_ref[5:6, 0:128] = count
    width = narrow_ref.shape[1]
    chans = 2 * width
    shard = narrow_ref.shape[0] // 6
    prows = width // 8
    half = 3 * shard // 2
    cut = half - 16
    flat = narrow_ref.at[3 * shard : 6 * shard]
    cot = cot_ref[...]
    cot_out[...] = cot
    pick = (iota((chans, shard), 0) == iota((chans, shard), 1) + me * shard).astype(BF16)
    taps = [narrow_ref[k * shard : (k + 1) * shard] for k in range(3)]
    first, second = base_tables(embed_ref[...], pick, taps)
    f_high, f_low = split(first)
    info = jnp.concatenate(
        [
            bases_ref[...].astype(F32),
            count,
            jnp.zeros((1, chans - cap - 128), F32),
        ],
        axis=1,
    )
    tail = jnp.concatenate([f_high.astype(F32), f_low.astype(F32)], axis=1)
    tail = jnp.where(iota((16, 1), 0) == 12, info, tail)
    wide = jnp.concatenate([second[0:24], second[24:48]], axis=1)
    extra = jnp.concatenate([info, jnp.zeros((7, chans), F32)], axis=0)
    own_ref[0:cut, 0:width] = flat[0:cut]
    own_ref[0:cut, width:chans] = flat[half : half + cut]
    own_ref[cut:half] = tail.astype(BF16)
    own_ref[half : half + 16, 0:width] = flat[cut:half]
    own_ref[half : half + 16, width:chans] = flat[half + cut : 2 * half]
    own_ref[half + 16 : half + 16 + 2 * prows] = broad_ref[0 : 2 * prows]
    own_ref[2 * half - 32 : 2 * half] = jnp.concatenate([wide, extra], axis=0).astype(BF16)
    part = own_ref[pl.ds(pl.multiple_of(odd * half, 16), half), :]
    for out in (x_ref, y_ref, d_ref):
        out[0:half] = part
    ahead = (iota((HALO, cap), 1) - iota((HALO, cap), 0) + HALO).astype(F32)
    take = (ahead == count).astype(BF16)
    last = mm(take, cot).astype(BF16)
    chip = me >> 1
    own_ref[2 * half :] = jnp.where((me & 1) == 0, last, cot[0:HALO])
    x_ref[half:] = jnp.where((chip ^ 1) > chip, last, cot[0:HALO])
    d_ref[half:] = jnp.where((chip ^ 3) > chip, last, cot[0:HALO])


def context_body(info_at, cot, r1, r2, l1, l2, hot_f_ref, hot_r_ref, cx_ref):
    cap = cot.shape[0]
    outer = HALO + SECOND_DILATION + FIRST_DILATION
    span = cap + 2 * outer
    counts = [info_at(o)[0:1, cap : cap + 128] for o in range(-REACH, REACH + 1)]
    begin = [None] * (2 * REACH + 1)
    begin[REACH] = jnp.zeros((1, 128), F32)
    for o in range(1, REACH + 1):
        begin[REACH + o] = begin[REACH + o - 1] + counts[REACH + o - 1]
        begin[REACH - o] = begin[REACH - o + 1] - counts[REACH - o]
    lane = iota((1, 128), 1).astype(F32)
    rowpos = (iota((span, 128), 0) - outer).astype(F32)
    total = jnp.zeros((span, 128), F32)
    for o in range(-REACH, REACH + 1):
        code = info_at(o)[0:1, 0:cap] + 1.0
        pos = jnp.where(lane < counts[REACH + o], begin[REACH + o] + lane, FAR)
        total = total + jnp.where(rowpos == pos, code, 0.0)
    codes = jnp.sum(total, axis=1, keepdims=True)
    d = FIRST_DILATION
    left, mid, right = codes[0 : span - 2 * d], codes[d : span - d], codes[2 * d : span]
    rows = span - 2 * d
    lanes = iota((rows, TABLE), 1).astype(F32)
    flip = lambda c: jnp.where(c == 0.0, 0.0, 5.0 - c)
    idx = jnp.where(mid == 0.0, -1.0, (mid - 1.0) * 25.0 + left * 5.0 + right)
    hot_f_ref[...] = (lanes == idx).astype(BF16)
    idx = jnp.where(mid == 0.0, -1.0, (4.0 - mid) * 25.0 + flip(right) * 5.0 + flip(left))
    hot_r_ref[...] = (lanes == idx).astype(BF16)

    own_n = counts[REACH]
    before_n, after_n = counts[REACH - 1], counts[REACH + 1]
    grow = cap + 2 * HALO
    lane_h = iota((1, HALO), 1).astype(F32)
    lane_s = iota((1, SPILL), 1).astype(F32)
    row_h = (iota((grow, HALO), 0) - HALO).astype(F32)
    row_s = (iota((grow, SPILL), 0) - HALO).astype(F32)
    row_o = (iota((grow, cap), 0) - HALO).astype(F32)
    own_pos = jnp.where(lane < own_n, lane, FAR)
    acc = mm((row_o == own_pos).astype(BF16), cot)
    pos = jnp.where(lane_h >= HALO - before_n[:, 0:HALO], lane_h - HALO, FAR)
    acc = acc + mm((row_h == pos).astype(BF16), r1)
    pos = jnp.where(
        counts[REACH - 2][:, 0:SPILL] > 0.0, lane_s - SPILL - before_n[:, 0:SPILL], FAR
    )
    acc = acc + mm((row_s == pos).astype(BF16), r2)
    pos = jnp.where(lane_h < after_n[:, 0:HALO], lane_h + own_n[:, 0:HALO], FAR)
    acc = acc + mm((row_h == pos).astype(BF16), l1)
    pos = jnp.where(
        (counts[REACH + 2][:, 0:SPILL] > 0.0) & (after_n[:, 0:SPILL] < HALO),
        lane_s + own_n[:, 0:SPILL] + after_n[:, 0:SPILL],
        FAR,
    )
    acc = acc + mm((row_s == pos).astype(BF16), l2)
    cx_ref[...] = (0.5 * acc).astype(BF16)


def context_kernel_plain(info_ref, cot_ref, r1_ref, r2_ref, l1_ref, l2_ref, *outs):
    context_body(
        lambda o: info_ref[REACH + o], cot_ref[...], r1_ref[...], r2_ref[...], l1_ref[...],
        l2_ref[...], *outs,
    )


def context_kernel_packed(*refs):
    parts, cot_ref, outs = refs[0:8], refs[8], refs[9:12]
    info_ref, halo_ref = refs[12:]
    me, odd = position(), lax.axis_index("dp") & 1
    chip, core = me >> 1, me & 1
    half = 3 * cot_ref.shape[1] // 16
    info_ref[0:REACH] = jnp.zeros((REACH, 8, 256), F32)
    info_ref[REACH + 8 :] = jnp.zeros((REACH, 8, 256), F32)
    for n, part in enumerate(parts):
        peer = me ^ (2 * (n % 4) + n // 4)
        low = part[half - 16 : half].astype(F32)[12:13, 0:256]
        if n % 4 > 0:
            high = part[half - 16 : half].astype(F32)[8:9, 0:256]
            low = jnp.where(odd == 0, low, high)
        info_ref[REACH + peer] = jnp.broadcast_to(low, (8, 256))
    for n in range(2):
        halo_ref[4 * n + chip] = parts[4 * n][2 * half :]
        halo_ref[4 * n + (chip ^ 1)] = parts[4 * n + 1][half:]
        halo_ref[4 * n + (chip ^ 3)] = parts[4 * n + 3][half:]
    r1 = halo_ref[4 + jnp.maximum(chip + core - 1, 0)]
    l1 = halo_ref[4 + jnp.minimum(chip + core, 3)]
    r2 = halo_ref[jnp.maximum(chip - 1, 0)]
    l2 = halo_ref[jnp.minimum(chip + 1, 3)]
    context_body(
        lambda o: info_ref[me + (REACH + o)], cot_ref[...], r1, r2[HALO - SPILL :], l1,
        l2[0:SPILL], *outs,
    )


def tower_body(
    first, project, conv, p2, count, emb, cap, cx_ref, hot_f_ref, hot_r_ref,
    s1_ref, gb_ref, g_ref, put,
):
    entry = iota((TABLE, 1), 0)
    by25 = (entry * 1311) >> 15
    by5 = (entry * 6554) >> 15
    in_left = by5 - 5 * by25
    in_right = entry - 5 * by5
    sums = jnp.zeros((TABLE, first.shape[1]), F32)
    for q in range(4):
        sums = jnp.where(in_left == q + 1, first[q : q + 1], sums)
    sums = sums + spread(first[4:8], by25)
    after = jnp.zeros((TABLE, first.shape[1]), F32)
    for q in range(4):
        after = jnp.where(in_right == q + 1, first[8 + q : 9 + q], after)
    value, slope = gelu_pair(sums + after)
    b1 = value.astype(BF16)
    high, low = split(slope)
    s1_ref[0:TABLE] = high
    s1_ref[TABLE : 2 * TABLE] = low
    stream = spread(emb, by25) + mm(b1, project)
    value, slope = gelu_pair(stream)
    a2 = value.astype(BF16)
    s2 = jnp.concatenate(split(slope), axis=0)

    grow = cap + 2 * HALO
    inner = cap + 2 * FIRST_DILATION
    d, D = FIRST_DILATION, SECOND_DILATION
    cx = cx_ref[...]
    back_mid = mm_nt(cx, p2)
    before = jnp.zeros((2 * grow, p2.shape[0]), F32)
    for k in range(3):
        taps = jnp.concatenate(split(mm(a2, conv(k))), axis=0)
        hot = jnp.concatenate(
            [hot_f_ref[k * D : k * D + grow], hot_r_ref[(2 - k) * D : (2 - k) * D + grow]], axis=0
        )
        before = before + mm(jnp.concatenate([hot, hot], axis=1), taps)
    value, slope = gelu_pair(before)
    own_col = (iota((cap, 1), 0).astype(F32) < count).astype(F32)
    own_gb = (cx[HALO : HALO + cap].astype(F32) * own_col).astype(BF16)
    mids = jnp.concatenate(
        [value[HALO : HALO + cap], value[grow + HALO : grow + HALO + cap]], axis=0
    ).astype(BF16)
    put(1, mm_tn(mids, jnp.concatenate([own_gb, own_gb], axis=0)))
    grad_f = (back_mid * slope[0:grow]).astype(BF16)
    grad_r = (back_mid * slope[grow:]).astype(BF16)
    ga = jnp.zeros((2 * inner, cx.shape[1]), F32)
    for k in range(3):
        rows = jnp.concatenate(
            [grad_f[(2 - k) * D : (2 - k) * D + inner], grad_r[k * D : k * D + inner]], axis=0
        )
        ga = ga + mm_nt(rows, conv(k))
    hot = jnp.concatenate(
        [hot_f_ref[2 * D : 2 * D + inner], hot_r_ref[2 * D : 2 * D + inner]], axis=0
    )
    base_g = cx[D : D + inner].astype(F32)
    g = jnp.concatenate([base_g, base_g], axis=0) + ga * mm(
        jnp.concatenate([hot, hot], axis=1), s2
    )
    gb = g.astype(BF16)
    gb_ref[...] = gb
    g_ref[0:cap] = g[d : d + cap]
    g_ref[cap : 2 * cap] = g[inner + d : inner + d + cap]
    col = jnp.concatenate([own_col, own_col], axis=0)
    own_hot = jnp.concatenate([hot[d : d + cap], hot[inner + d : inner + d + cap]], axis=0)
    own_b1 = mm((own_hot.astype(F32) * col).astype(BF16), b1).astype(BF16)
    own_g = jnp.concatenate([gb[d : d + cap], gb[inner + d : inner + d + cap]], axis=0)
    put(0, mm_tn(own_b1, own_g))


def saliency_kernel(
    small_ref, hot_f_ref, hot_r_ref, s1_ref, gb_ref, g_ref, second_ref, p1_ref, sal_ref
):
    cap = g_ref.shape[0] // 2
    inner = cap + 2 * FIRST_DILATION
    d, D = FIRST_DILATION, SECOND_DILATION
    hot = jnp.concatenate(
        [hot_f_ref[2 * D : 2 * D + inner], hot_r_ref[2 * D : 2 * D + inner]], axis=0
    )
    slope = mm(jnp.concatenate([hot, hot], axis=1), s1_ref[...])
    gh = (mm_nt(gb_ref[...], p1_ref[...]) * slope).astype(BF16)
    emb = small_ref[0:4]
    bases = small_ref[4:5, 0:cap]
    wide = jnp.concatenate(split(second_ref[...]), axis=0)
    total = jnp.zeros((4, cap), F32)
    e_high, e_low = split(jnp.concatenate([emb, emb], axis=0))
    for turn in range(2):
        g_high, g_low = split(g_ref[turn * cap : (turn + 1) * cap])
        got = mm_nt(e_high, g_high) + mm_nt(e_high, g_low) + mm_nt(e_low, g_high)
        got = got[0:4]
        table = jnp.zeros((16, cap), F32)
        for k in range(3):
            place = 2 - k if turn == 0 else k
            at = turn * inner + place * d
            both = mm_nt(
                jnp.concatenate(
                    [wide[16 * k : 16 * k + 16], wide[48 + 16 * k : 64 + 16 * k]], axis=0
                ),
                gh[at : at + cap],
            )
            table = table + both[0:16] + both[16:32]
        for q in range(4):
            code = float(q if turn == 0 else 3 - q)
            got = got + jnp.where(bases == code, table[4 * q : 4 * q + 4], 0.0)
        if turn == 1:
            got = jnp.concatenate([got[3 - c : 4 - c] for c in range(4)], axis=0)
        total = total + got
    live = iota((1, cap), 1).astype(F32) < small_ref[5:6, 0:cap]
    sal_ref[...] = jnp.where(live, total * (1.0 / math.sqrt(emb.shape[1])), 0.0)


def tower_kernel_packed(*refs):
    own_parts, plane_parts, dp_parts = refs[0:2], refs[2:8], refs[8:14]
    small_ref, cx_ref, hf_ref, hr_ref = refs[14:18]
    keep_ref, send_ref, s1_ref, gb_ref, g_ref, wide_ref, p1_ref = refs[18:25]
    conv_ref, p2_ref, first_ref, second_ref = refs[25:]
    me = position()
    core, odd = me & 1, lax.axis_index("dp") & 1
    count = small_ref[5:6, 0:1]
    width, chans = p1_ref.shape
    shard = chans // 8
    prow = width // 8
    half = 3 * shard // 2
    cut = half - 16

    def place(side, rows, peer):
        at = peer * shard

        def lay(k, start, size, source, lane):
            conv_ref[k, pl.ds(pl.multiple_of(at + start, 16), size), :] = rows(
                source, size
            )[:, lane : lane + width]

        if side == 0:
            lay(0, 0, shard, 0, 0)
            lay(1, 0, cut - shard, shard, 0)
            lay(1, shard // 2, shard // 2, 0, width)
            lay(2, 0, cut - shard // 2, shard // 2, width)
            tail = rows(cut, 16).astype(F32)
            first_ref[peer] = tail[:, 0:width] + tail[:, width:]
        else:
            lay(1, cut - shard, 16, 0, 0)
            lay(2, shard - 16, 16, 0, width)
            to = pl.ds(pl.multiple_of(peer * prow, 16), prow)
            p2_ref[to, :] = rows(16, prow)
            p1_ref[to, :] = rows(16 + prow, prow)
            second_ref[peer] = rows(half - 32, 32).astype(F32)[0:24]

    for n in range(2):
        for side in range(2):
            rows = lambda a, size, n=n, side=side: own_parts[n][
                side * half + a : side * half + a + size
            ]
            place(side, rows, me ^ n)
    for parity in range(2):

        @pl.when(odd == parity)
        def _():
            for n in range(6):
                peer = me ^ (2 * (n % 3 + 1) + n // 3)
                for side, part in ((parity, plane_parts[n]), (1 - parity, dp_parts[n])):
                    rows = lambda a, size, part=part: part[a : a + size]
                    place(side, rows, peer)

    first = first_ref[0]
    wide = second_ref[0]
    for peer in range(1, 8):
        first = first + first_ref[peer]
        wide = wide + second_ref[peer]
    wide_ref[...] = jnp.concatenate([wide[:, 0:width], wide[:, width : 2 * width]], axis=0)

    def put(block, value):
        rows = value.shape[0] // 4
        for c in range(2):
            even = value[2 * c * rows : (2 * c + 1) * rows]
            uneven = value[(2 * c + 1) * rows : (2 * c + 2) * rows]
            keep_ref[2 * block + c] = jnp.where(core == 0, even, uneven)
            send_ref[2 * block + c] = jnp.where(core == 0, uneven, even).astype(BF16)

    tower_body(
        first, p1_ref[...], lambda k: conv_ref[k], p2_ref[...], count, small_ref[0:4],
        g_ref.shape[0] // 2, cx_ref, hf_ref, hr_ref, s1_ref, gb_ref, g_ref, put,
    )


def tower_kernel_plain(
    first_ref, p1_ref, conv_ref, p2_ref, small_ref, cx_ref, hf_ref, hr_ref,
    grad_ref, s1_ref, gb_ref, g_ref,
):
    def put(block, value):
        rows = value.shape[0]
        grad_ref[block * rows : (block + 1) * rows] = value

    tower_body(
        first_ref[...], p1_ref[...], lambda k: conv_ref[k], p2_ref[...], small_ref[5:6, 0:1],
        small_ref[0:4], g_ref.shape[0] // 2, cx_ref, hf_ref, hr_ref, s1_ref, gb_ref, g_ref, put,
    )


def fold(value):
    width = value.shape[1] // 2
    return jnp.concatenate([value[:, 0:width], value[:, width:]], axis=0)


def core_sum_kernel(keep_ref, recv_ref, own_ref, *outs):
    chip = 2 * lax.axis_index("y") + lax.axis_index("x")
    own_ref[...] = keep_ref[chip] + recv_ref[chip].astype(F32)
    for n, out in enumerate(outs):
        at = chip ^ (n + 1)
        out[...] = (keep_ref[at] + recv_ref[at].astype(F32)).astype(BF16)


def plane_sum_kernel(own_ref, d_ref, y_ref, x_ref, mine_ref, *refs):
    outs, sum_ref = refs[:-1], refs[-1]
    sum_ref[...] = (
        own_ref[...] + x_ref[...].astype(F32) + y_ref[...].astype(F32) + d_ref[...].astype(F32)
    )
    z = lax.axis_index("dp")
    rows = mine_ref.shape[0] // 2
    mine_ref[...] = fold(sum_ref[pl.ds(pl.multiple_of(z * rows, 8), rows), :])
    for n, out in enumerate(outs):
        at = pl.multiple_of((z ^ (n + 1)) * rows, 8)
        out[...] = fold(sum_ref[pl.ds(at, rows), :]).astype(BF16)


def last_sum_kernel(scale, mine_ref, *refs):
    out_ref = refs[-1]
    total = mine_ref[...]
    for ref in refs[:-1]:
        total = total + ref[...].astype(F32)
    total = total * scale
    rows, half = total.shape[0] // 2, total.shape[1] // 128
    for n in range(2 * half):
        at = rows * (n // half)
        lane = 128 * (n % half)
        out_ref[pl.ds(n, rows, stride=2 * half), :] = total[at : at + rows, lane : lane + 128]


def flip_move(array, *axes):
    sizes = [lax.axis_size(a) for a in axes]
    size = math.prod(sizes)
    return lax.ppermute(array, axes, [(i, size - 1 - i) for i in range(size)])


def xor_move(array, axis, bits):
    return lax.ppermute(array, axis, [(i, i ^ bits) for i in range(lax.axis_size(axis))])


def shift_move(array, by, axes):
    size = math.prod(lax.axis_size(a) for a in axes)
    return lax.ppermute(array, axes, [(i, i + by) for i in range(size) if 0 <= i + by < size])


def context_shapes(cap, chans):
    rows = cap + 2 * (HALO + SECOND_DILATION)
    return [((rows, TABLE), BF16), ((rows, TABLE), BF16), ((cap + 2 * HALO, chans), BF16)]


def pass_shapes(cap, chans, width):
    inner = cap + 2 * FIRST_DILATION
    return [((2 * TABLE, width), BF16), ((2 * inner, chans), BF16), ((2 * cap, chans), F32)]


def lines(embed, bases, lengths):
    cap, chans = bases.shape[1], embed.shape[1]
    row = lax.broadcasted_iota(jnp.int32, (8, chans), 0)
    line = jnp.pad(bases, ((0, 0), (0, chans - cap)))
    extra = jnp.where(row == 4, line, jnp.where(row == 5, lengths, 0)).astype(F32)
    return jnp.where(row < 4, jnp.pad(embed, ((0, 4), (0, 0))), extra)


def weight(flops):
    return pl.CostEstimate(flops=flops, bytes_accessed=10**6, transcendentals=0)


def fast_shards(
    bases, lengths, cotangent, c1, p1, c2, p2, embed
):
    cot = cotangent[0]
    cap, chans = cot.shape
    width = c1.shape[2]
    n_dp = lax.axis_size("dp")
    half = 3 * c2.shape[1] // 2
    narrow = jnp.concatenate([c1.reshape(-1, width), c2.reshape(-1, width)], axis=0)
    broad = jnp.concatenate([p2, p1], axis=0)
    own, to_x, to_y, to_d, small, cot = call(
        prep_kernel,
        [
            ((2 * half + HALO, chans), BF16),
            ((half + HALO, chans), BF16),
            ((half, chans), BF16),
            ((half + HALO, chans), BF16),
            ((8, chans), F32),
            ((cap, chans), BF16),
        ],
        [narrow, broad, cot, embed, bases, lengths],
    )
    plane = [flip_move(to_x, "x"), flip_move(to_y, "y"), flip_move(to_d, "y", "x")]
    other = [xor_move(a[:half], "dp", 1) for a in plane]
    across = lambda arrays: [flip_move(a, "core") for a in arrays]
    rows = chans // 8
    swapped = across([own, *plane])
    hf, hr, cx = call(
        context_kernel_packed,
        context_shapes(cap, chans),
        [own, *plane, *swapped, cot],
        scratch=[
            pltpu.VMEM((8 + 2 * REACH, 8, 256), F32),
            pltpu.VMEM((8, HALO, chans), BF16),
        ],
        cost=weight(10**9),
    )
    keep, send, s1, gb, g, second, p1_full = call(
        tower_kernel_packed,
        [((4, rows, chans), F32), ((4, rows, chans), BF16), *pass_shapes(cap, chans, width)]
        + [((48, width), F32), ((width, chans), BF16)],
        [
            own, swapped[0], *plane, *swapped[1:], *other, *across(other),
            small, cx, hf, hr,
        ],
        scratch=[
            pltpu.VMEM((3, chans, width), BF16),
            pltpu.VMEM((width, chans), BF16),
            pltpu.VMEM((8, 16, width), F32),
            pltpu.VMEM((8, 24, chans), F32),
        ],
        limit=40,
        cost=weight(4 * 10**9),
    )
    recv = flip_move(send, "core")
    (sal,) = call(
        saliency_kernel,
        [((4, cap), F32)],
        [small, hf, hr, s1, gb, g, second, p1_full],
        cost=weight(10**9),
    )
    own, *outs = call(
        core_sum_kernel,
        [((rows, chans), F32)] + [((rows, chans), BF16)] * 3,
        [keep, recv],
    )
    ways = (("x",), ("y",), ("y", "x"))
    got = [flip_move(outs[n], *ways[n]) for n in (2, 1, 0)]
    part = rows // n_dp
    mine, *outs = call(
        plane_sum_kernel,
        [((2 * part, width), F32)] + [((2 * part, width), BF16)] * (n_dp - 1),
        [own, *got],
        scratch=[pltpu.VMEM((rows, chans), F32)],
    )
    got = [xor_move(outs[n], "dp", n + 1) for n in reversed(range(n_dp - 1))]
    scale = 1.0 / math.sqrt(8 * n_dp * cap)
    (grad,) = call(
        functools.partial(last_sum_kernel, scale),
        [((part * chans // 128, 128), F32)],
        [mine, *got],
    )
    return sal[None], grad.reshape(-1)


def plain_shards(bases, lengths, cotangent, c1, p1, c2, p2, embed):
    cot = cotangent[0]
    cap, chans = cot.shape
    width = c1.shape[2]
    me, count = lax.axis_index("seq"), lengths[0, 0]
    shard = c1.shape[1]
    own = lax.dynamic_slice_in_dim(embed, me * shard, shard, 1)
    act, slope = gelu_pair(own)
    taps = c1.astype(F32)
    high = lax.Precision.HIGHEST
    first = jnp.einsum("qc,kcb->kqb", act.astype(BF16).astype(F32), taps, precision=high)
    second = jnp.einsum("qc,dc,kcb->kqdb", slope, own, taps, precision=high)
    first = lax.psum(first.reshape(12, width), "seq")
    second = lax.psum(second.reshape(48, width), "seq")
    first = jnp.concatenate([first, jnp.zeros((4, width), F32)], axis=0)
    p1_full = lax.all_gather(p1, "seq", axis=0, tiled=True)
    p2_full = lax.all_gather(p2, "seq", axis=0, tiled=True)
    conv = lax.all_gather(c2, "seq", axis=1, tiled=True)
    info = jnp.concatenate(
        [bases.astype(F32), jnp.broadcast_to(count.astype(F32), (1, 128))], axis=1
    )
    info = lax.all_gather(info, "seq", axis=0, tiled=True)
    info = jnp.pad(info, ((REACH, REACH), (0, 0)))
    info = lax.dynamic_slice_in_dim(info, me, 2 * REACH + 1, 0)
    info = jnp.broadcast_to(info[:, None, :], (2 * REACH + 1, 8, cap + 128))
    padded = jnp.pad(cot, ((HALO, 0), (0, 0)))
    last = lax.dynamic_slice_in_dim(padded, count, HALO, 0)
    halos = [
        shift_move(last, 1, ("seq",)),
        shift_move(last[HALO - SPILL :], 2, ("seq",)),
        shift_move(cot[:HALO], -1, ("seq",)),
        shift_move(cot[:SPILL], -2, ("seq",)),
    ]
    small = lines(embed, bases, lengths)
    hf, hr, cx = call(
        context_kernel_plain, context_shapes(cap, chans), [info, cot, *halos]
    )
    grad, s1, gb, g = call(
        tower_kernel_plain,
        [((2 * width, chans), F32), *pass_shapes(cap, chans, width)],
        [first, p1_full, conv, p2_full, small, cx, hf, hr],
        limit=40,
    )
    (sal,) = call(
        saliency_kernel,
        [((4, cap), F32)],
        [small, hf, hr, s1, gb, g, second, p1_full],
    )
    scale = 1.0 / math.sqrt(lax.axis_size("seq") * lax.axis_size("dp") * cap)
    grad = lax.psum_scatter(
        grad.reshape(-1) * scale, ("seq", "dp"), scatter_dimension=0, tiled=True
    )
    return sal[None], grad


def solution(mesh):
    run, seq = plain_shards, "seq"
    if mesh.shape["seq"] == 8 and mesh.shape["dp"] == 4:
        run, seq = fast_shards, ("y", "x", "core")
        count = mesh.shape["dp"]
        mesh = jax.sharding.Mesh(mesh.devices.reshape(2, 2, 2, count), (*seq, "dp"))
    every = seq if isinstance(seq, tuple) else (seq,)
    in_specs = (
        P("dp", seq),
        P("dp", seq),
        P("dp", seq, None),
        P(None, seq, None),
        P(seq, None),
        P(None, seq, None),
        P(seq, None),
        P(),
    )
    out_specs = (P("dp", None, seq), P((*every, "dp")))
    return jax.shard_map(run, mesh=mesh, in_specs=in_specs, out_specs=out_specs, check_vma=False)
```

```python
import functools
import math

import jax
import jax.numpy as jnp
from jax import lax
from jax.experimental import pallas as pl
from jax.experimental.pallas import tpu as pltpu
from jax.sharding import PartitionSpec as P

FIRST_DILATION = 16
SECOND_DILATION = 64
HALO = FIRST_DILATION + SECOND_DILATION
SPILL = 16
REACH = 3
TABLE = 128
SQRT_HALF = 0.7071067811865476
INV_SQRT_TWO_PI = 0.3989422804014327
F32 = jnp.float32
BF16 = jnp.bfloat16
FAR = -100000.0


def gelu_pair(v):
    half = 0.5 * (1.0 + lax.erf(v * SQRT_HALF))
    return v * half, half + v * jnp.exp(-0.5 * v * v) * INV_SQRT_TWO_PI


def split(v):
    high = v.astype(BF16)
    return high, (v - high.astype(F32)).astype(BF16)


def mm(a, b):
    return lax.dot_general(a, b, (((1,), (0,)), ((), ())), preferred_element_type=F32)


def mm_nt(a, b):
    return lax.dot_general(a, b, (((1,), (1,)), ((), ())), preferred_element_type=F32)


def mm_tn(a, b):
    return lax.dot_general(a, b, (((0,), (0,)), ((), ())), preferred_element_type=F32)


def iota(shape, dim):
    return lax.broadcasted_iota(jnp.int32, shape, dim)


def spread(rows, index):
    out = jnp.broadcast_to(rows[0:1], (index.shape[0], rows.shape[1]))
    for q in range(1, 4):
        out = jnp.where(index == q, rows[q : q + 1], out)
    return out


def call(body, out_shapes, args, scratch=(), limit=24, cost=None):
    in_specs = [
        pl.BlockSpec(memory_space=pltpu.VMEM) for _ in args
    ]
    return pl.pallas_call(
        body,
        out_shape=[jax.ShapeDtypeStruct(s, d) for s, d in out_shapes],
        in_specs=in_specs,
        out_specs=[pl.BlockSpec(memory_space=pltpu.VMEM)] * len(out_shapes),
        scratch_shapes=list(scratch),
        compiler_params=pltpu.CompilerParams(vmem_limit_bytes=limit * 1024 * 1024),
        cost_estimate=cost,
    )(*args)


def base_tables(emb, pick, conv):
    row = iota((16, 1), 0)
    low, high = row & 3, row >> 2
    by_low = spread(emb, low)
    by_high = spread(emb, high)
    act = gelu_pair(by_low)[0].astype(BF16)
    prod_high, prod_low = split(gelu_pair(by_high)[1] * by_low)
    own = mm(jnp.concatenate([act, prod_high, prod_low], axis=0), pick).astype(BF16)
    first = jnp.zeros((16, conv[0].shape[1]), F32)
    second = []
    for k in range(3):
        res = mm(own, conv[k])
        first = jnp.where(high == k, res[0:16], first)
        second.append(res[16:32] + res[32:48])
    return first, jnp.concatenate(second, axis=0)


def position():
    return (2 * lax.axis_index("y") + lax.axis_index("x")) * 2 + lax.axis_index("core")


def prep_kernel(
    narrow_ref, broad_ref, cot_ref, embed_ref, bases_ref, lengths_ref,
    own_ref, x_ref, y_ref, d_ref, small_ref, cot_out,
):
    me, odd = position(), lax.axis_index("dp") & 1
    cap = bases_ref.shape[1]
    count = jnp.broadcast_to(lengths_ref[...], (1, 128)).astype(F32)
    small_ref[0:4] = embed_ref[...]
    small_ref[4:5, 0:cap] = bases_ref[...].astype(F32)
    small_ref[5:6, 0:128] = count
    width = narrow_ref.shape[1]
    chans = 2 * width
    shard = narrow_ref.shape[0] // 6
    prows = width // 8
    half = 3 * shard // 2
    cut = half - 16
    flat = narrow_ref.at[3 * shard : 6 * shard]
    cot = cot_ref[...]
    cot_out[...] = cot
    pick = (iota((chans, shard), 0) == iota((chans, shard), 1) + me * shard).astype(BF16)
    taps = [narrow_ref[k * shard : (k + 1) * shard] for k in range(3)]
    first, second = base_tables(embed_ref[...], pick, taps)
    f_high, f_low = split(first)
    info = jnp.concatenate(
        [
            bases_ref[...].astype(F32),
            count,
            jnp.zeros((1, chans - cap - 128), F32),
        ],
        axis=1,
    )
    tail = jnp.concatenate([f_high.astype(F32), f_low.astype(F32)], axis=1)
    tail = jnp.where(iota((16, 1), 0) == 12, info, tail)
    wide = jnp.concatenate([second[0:24], second[24:48]], axis=1)
    extra = jnp.concatenate([info, jnp.zeros((7, chans), F32)], axis=0)
    own_ref[0:cut, 0:width] = flat[0:cut]
    own_ref[0:cut, width:chans] = flat[half : half + cut]
    own_ref[cut:half] = tail.astype(BF16)
    own_ref[half : half + 16, 0:width] = flat[cut:half]
    own_ref[half : half + 16, width:chans] = flat[half + cut : 2 * half]
    own_ref[half + 16 : half + 16 + 2 * prows] = broad_ref[0 : 2 * prows]
    own_ref[2 * half - 32 : 2 * half] = jnp.concatenate([wide, extra], axis=0).astype(BF16)
    part = own_ref[pl.ds(pl.multiple_of(odd * half, 16), half), :]
    for out in (x_ref, y_ref, d_ref):
        out[0:half] = part
    ahead = (iota((HALO, cap), 1) - iota((HALO, cap), 0) + HALO).astype(F32)
    take = (ahead == count).astype(BF16)
    last = mm(take, cot).astype(BF16)
    chip = me >> 1
    own_ref[2 * half :] = jnp.where((me & 1) == 0, last, cot[0:HALO])
    x_ref[half:] = jnp.where((chip ^ 1) > chip, last, cot[0:HALO])
    d_ref[half:] = jnp.where((chip ^ 3) > chip, last, cot[0:HALO])


def context_body(info_at, cot, r1, r2, l1, l2, hot_f_ref, hot_r_ref, cx_ref):
    cap = cot.shape[0]
    outer = HALO + SECOND_DILATION + FIRST_DILATION
    span = cap + 2 * outer
    counts = [info_at(o)[0:1, cap : cap + 128] for o in range(-REACH, REACH + 1)]
    begin = [None] * (2 * REACH + 1)
    begin[REACH] = jnp.zeros((1, 128), F32)
    for o in range(1, REACH + 1):
        begin[REACH + o] = begin[REACH + o - 1] + counts[REACH + o - 1]
        begin[REACH - o] = begin[REACH - o + 1] - counts[REACH - o]
    lane = iota((1, 128), 1).astype(F32)
    rowpos = (iota((span, 128), 0) - outer).astype(F32)
    total = jnp.zeros((span, 128), F32)
    for o in range(-REACH, REACH + 1):
        code = info_at(o)[0:1, 0:cap] + 1.0
        pos = jnp.where(lane < counts[REACH + o], begin[REACH + o] + lane, FAR)
        total = total + jnp.where(rowpos == pos, code, 0.0)
    codes = jnp.sum(total, axis=1, keepdims=True)
    d = FIRST_DILATION
    left, mid, right = codes[0 : span - 2 * d], codes[d : span - d], codes[2 * d : span]
    rows = span - 2 * d
    lanes = iota((rows, TABLE), 1).astype(F32)
    flip = lambda c: jnp.where(c == 0.0, 0.0, 5.0 - c)
    idx = jnp.where(mid == 0.0, -1.0, (mid - 1.0) * 25.0 + left * 5.0 + right)
    hot_f_ref[...] = (lanes == idx).astype(BF16)
    idx = jnp.where(mid == 0.0, -1.0, (4.0 - mid) * 25.0 + flip(right) * 5.0 + flip(left))
    hot_r_ref[...] = (lanes == idx).astype(BF16)

    own_n = counts[REACH]
    before_n, after_n = counts[REACH - 1], counts[REACH + 1]
    grow = cap + 2 * HALO
    lane_h = iota((1, HALO), 1).astype(F32)
    lane_s = iota((1, SPILL), 1).astype(F32)
    row_h = (iota((grow, HALO), 0) - HALO).astype(F32)
    row_s = (iota((grow, SPILL), 0) - HALO).astype(F32)
    row_o = (iota((grow, cap), 0) - HALO).astype(F32)
    own_pos = jnp.where(lane < own_n, lane, FAR)
    acc = mm((row_o == own_pos).astype(BF16), cot)
    pos = jnp.where(lane_h >= HALO - before_n[:, 0:HALO], lane_h - HALO, FAR)
    acc = acc + mm((row_h == pos).astype(BF16), r1)
    pos = jnp.where(
        counts[REACH - 2][:, 0:SPILL] > 0.0, lane_s - SPILL - before_n[:, 0:SPILL], FAR
    )
    acc = acc + mm((row_s == pos).astype(BF16), r2)
    pos = jnp.where(lane_h < after_n[:, 0:HALO], lane_h + own_n[:, 0:HALO], FAR)
    acc = acc + mm((row_h == pos).astype(BF16), l1)
    pos = jnp.where(
        (counts[REACH + 2][:, 0:SPILL] > 0.0) & (after_n[:, 0:SPILL] < HALO),
        lane_s + own_n[:, 0:SPILL] + after_n[:, 0:SPILL],
        FAR,
    )
    acc = acc + mm((row_s == pos).astype(BF16), l2)
    cx_ref[...] = (0.5 * acc).astype(BF16)


def context_kernel_plain(info_ref, cot_ref, r1_ref, r2_ref, l1_ref, l2_ref, *outs):
    context_body(
        lambda o: info_ref[REACH + o], cot_ref[...], r1_ref[...], r2_ref[...], l1_ref[...],
        l2_ref[...], *outs,
    )


def context_kernel_packed(*refs):
    parts, cot_ref, outs = refs[0:8], refs[8], refs[9:12]
    info_ref, halo_ref = refs[12:]
    me, odd = position(), lax.axis_index("dp") & 1
    chip, core = me >> 1, me & 1
    half = 3 * cot_ref.shape[1] // 16
    info_ref[0:REACH] = jnp.zeros((REACH, 8, 256), F32)
    info_ref[REACH + 8 :] = jnp.zeros((REACH, 8, 256), F32)
    for n, part in enumerate(parts):
        peer = me ^ (2 * (n % 4) + n // 4)
        low = part[half - 16 : half].astype(F32)[12:13, 0:256]
        if n % 4 > 0:
            high = part[half - 16 : half].astype(F32)[8:9, 0:256]
            low = jnp.where(odd == 0, low, high)
        info_ref[REACH + peer] = jnp.broadcast_to(low, (8, 256))
    for n in range(2):
        halo_ref[4 * n + chip] = parts[4 * n][2 * half :]
        halo_ref[4 * n + (chip ^ 1)] = parts[4 * n + 1][half:]
        halo_ref[4 * n + (chip ^ 3)] = parts[4 * n + 3][half:]
    r1 = halo_ref[4 + jnp.maximum(chip + core - 1, 0)]
    l1 = halo_ref[4 + jnp.minimum(chip + core, 3)]
    r2 = halo_ref[jnp.maximum(chip - 1, 0)]
    l2 = halo_ref[jnp.minimum(chip + 1, 3)]
    context_body(
        lambda o: info_ref[me + (REACH + o)], cot_ref[...], r1, r2[HALO - SPILL :], l1,
        l2[0:SPILL], *outs,
    )


def tower_front(
    first, project, conv, p2, count, emb, cap, cx_ref, hot_f_ref, hot_r_ref, s1_ref, put
):
    entry = iota((TABLE, 1), 0)
    by25 = (entry * 1311) >> 15
    by5 = (entry * 6554) >> 15
    in_left = by5 - 5 * by25
    in_right = entry - 5 * by5
    sums = jnp.zeros((TABLE, first.shape[1]), F32)
    for q in range(4):
        sums = jnp.where(in_left == q + 1, first[q : q + 1], sums)
    sums = sums + spread(first[4:8], by25)
    after = jnp.zeros((TABLE, first.shape[1]), F32)
    for q in range(4):
        after = jnp.where(in_right == q + 1, first[8 + q : 9 + q], after)
    value, slope = gelu_pair(sums + after)
    b1 = value.astype(BF16)
    high, low = split(slope)
    s1_ref[0:TABLE] = high
    s1_ref[TABLE : 2 * TABLE] = low
    stream = spread(emb, by25) + mm(b1, project)
    value, slope = gelu_pair(stream)
    a2 = value.astype(BF16)
    s2 = jnp.concatenate(split(slope), axis=0)

    grow = cap + 2 * HALO
    D = SECOND_DILATION
    cx = cx_ref[...]
    back_mid = mm_nt(cx, p2)
    before = jnp.zeros((2 * grow, p2.shape[0]), F32)
    for k in range(3):
        taps = jnp.concatenate(split(mm(a2, conv(k))), axis=0)
        hot = jnp.concatenate(
            [hot_f_ref[k * D : k * D + grow], hot_r_ref[(2 - k) * D : (2 - k) * D + grow]], axis=0
        )
        before = before + mm(jnp.concatenate([hot, hot], axis=1), taps)
    value, slope = gelu_pair(before)
    own_col = (iota((cap, 1), 0).astype(F32) < count).astype(F32)
    own_gb = (cx[HALO : HALO + cap].astype(F32) * own_col).astype(BF16)
    mids = jnp.concatenate(
        [value[HALO : HALO + cap], value[grow + HALO : grow + HALO + cap]], axis=0
    ).astype(BF16)
    put(1, mm_tn(mids, jnp.concatenate([own_gb, own_gb], axis=0)))
    grad_f = (back_mid * slope[0:grow]).astype(BF16)
    grad_r = (back_mid * slope[grow:]).astype(BF16)
    return b1, s2, grad_f, grad_r


def tower_back(
    conv, b1, s2, grad_f, grad_r, count, cap, cx_ref, hot_f_ref, hot_r_ref, gb_ref, g_ref, put
):
    inner = cap + 2 * FIRST_DILATION
    d, D = FIRST_DILATION, SECOND_DILATION
    cx = cx_ref[...]
    own_col = (iota((cap, 1), 0).astype(F32) < count).astype(F32)
    ga = jnp.zeros((2 * inner, cx.shape[1]), F32)
    for k in range(3):
        rows = jnp.concatenate(
            [grad_f[(2 - k) * D : (2 - k) * D + inner], grad_r[k * D : k * D + inner]], axis=0
        )
        ga = ga + mm_nt(rows, conv(k))
    hot = jnp.concatenate(
        [hot_f_ref[2 * D : 2 * D + inner], hot_r_ref[2 * D : 2 * D + inner]], axis=0
    )
    base_g = cx[D : D + inner].astype(F32)
    g = jnp.concatenate([base_g, base_g], axis=0) + ga * mm(
        jnp.concatenate([hot, hot], axis=1), s2
    )
    gb = g.astype(BF16)
    gb_ref[...] = gb
    g_ref[0:cap] = g[d : d + cap]
    g_ref[cap : 2 * cap] = g[inner + d : inner + d + cap]
    col = jnp.concatenate([own_col, own_col], axis=0)
    own_hot = jnp.concatenate([hot[d : d + cap], hot[inner + d : inner + d + cap]], axis=0)
    own_b1 = mm((own_hot.astype(F32) * col).astype(BF16), b1).astype(BF16)
    own_g = jnp.concatenate([gb[d : d + cap], gb[inner + d : inner + d + cap]], axis=0)
    put(0, mm_tn(own_b1, own_g))


def saliency_kernel(
    small_ref, hot_f_ref, hot_r_ref, s1_ref, gb_ref, g_ref, second_ref, p1_ref, sal_ref
):
    cap = g_ref.shape[0] // 2
    inner = cap + 2 * FIRST_DILATION
    d, D = FIRST_DILATION, SECOND_DILATION
    hot = jnp.concatenate(
        [hot_f_ref[2 * D : 2 * D + inner], hot_r_ref[2 * D : 2 * D + inner]], axis=0
    )
    slope = mm(jnp.concatenate([hot, hot], axis=1), s1_ref[...])
    gh = (mm_nt(gb_ref[...], p1_ref[...]) * slope).astype(BF16)
    emb = small_ref[0:4]
    bases = small_ref[4:5, 0:cap]
    wide = jnp.concatenate(split(second_ref[...]), axis=0)
    total = jnp.zeros((4, cap), F32)
    e_high, e_low = split(jnp.concatenate([emb, emb], axis=0))
    for turn in range(2):
        g_high, g_low = split(g_ref[turn * cap : (turn + 1) * cap])
        got = mm_nt(e_high, g_high) + mm_nt(e_high, g_low) + mm_nt(e_low, g_high)
        got = got[0:4]
        table = jnp.zeros((16, cap), F32)
        for k in range(3):
            place = 2 - k if turn == 0 else k
            at = turn * inner + place * d
            both = mm_nt(
                jnp.concatenate(
                    [wide[16 * k : 16 * k + 16], wide[48 + 16 * k : 64 + 16 * k]], axis=0
                ),
                gh[at : at + cap],
            )
            table = table + both[0:16] + both[16:32]
        for q in range(4):
            code = float(q if turn == 0 else 3 - q)
            got = got + jnp.where(bases == code, table[4 * q : 4 * q + 4], 0.0)
        if turn == 1:
            got = jnp.concatenate([got[3 - c : 4 - c] for c in range(4)], axis=0)
        total = total + got
    live = iota((1, cap), 1).astype(F32) < small_ref[5:6, 0:cap]
    sal_ref[...] = jnp.where(live, total * (1.0 / math.sqrt(emb.shape[1])), 0.0)


def tower_kernel_packed(*refs):
    own_parts, plane_parts, dp_parts = refs[0:2], refs[2:8], refs[8:14]
    small_ref, cx_ref, hf_ref, hr_ref = refs[14:18]
    keep_ref, send_ref, s1_ref, wide_ref, p1_ref, conv_ref, *outs = refs[18:28]
    p2_ref, first_ref, second_ref = refs[28:]
    me = position()
    core, odd = me & 1, lax.axis_index("dp") & 1
    count = small_ref[5:6, 0:1]
    width, chans = p1_ref.shape
    shard = chans // 8
    prow = width // 8
    half = 3 * shard // 2
    cut = half - 16

    def place(side, rows, peer):
        at = peer * shard

        def lay(k, start, size, source, lane):
            conv_ref[k, pl.ds(pl.multiple_of(at + start, 16), size), :] = rows(
                source, size
            )[:, lane : lane + width]

        if side == 0:
            lay(0, 0, shard, 0, 0)
            lay(1, 0, cut - shard, shard, 0)
            lay(1, shard // 2, shard // 2, 0, width)
            lay(2, 0, cut - shard // 2, shard // 2, width)
            tail = rows(cut, 16).astype(F32)
            first_ref[peer] = tail[:, 0:width] + tail[:, width:]
        else:
            lay(1, cut - shard, 16, 0, 0)
            lay(2, shard - 16, 16, 0, width)
            to = pl.ds(pl.multiple_of(peer * prow, 16), prow)
            p2_ref[to, :] = rows(16, prow)
            p1_ref[to, :] = rows(16 + prow, prow)
            second_ref[peer] = rows(half - 32, 32).astype(F32)[0:24]

    for n in range(2):
        for side in range(2):
            rows = lambda a, size, n=n, side=side: own_parts[n][
                side * half + a : side * half + a + size
            ]
            place(side, rows, me ^ n)
    for parity in range(2):

        @pl.when(odd == parity)
        def _():
            for n in range(6):
                peer = me ^ (2 * (n % 3 + 1) + n // 3)
                for side, part in ((parity, plane_parts[n]), (1 - parity, dp_parts[n])):
                    rows = lambda a, size, part=part: part[a : a + size]
                    place(side, rows, peer)

    first = first_ref[0]
    wide = second_ref[0]
    for peer in range(1, 8):
        first = first + first_ref[peer]
        wide = wide + second_ref[peer]
    wide_ref[...] = jnp.concatenate([wide[:, 0:width], wide[:, width : 2 * width]], axis=0)

    results = tower_front(
        first, p1_ref[...], lambda k: conv_ref[k], p2_ref[...], count, small_ref[0:4],
        cx_ref.shape[0] - 2 * HALO, cx_ref, hf_ref, hr_ref, s1_ref,
        functools.partial(share, core, keep_ref, send_ref),
    )
    for out, value in zip(outs, results):
        out[...] = value


def share(core, keep_ref, send_ref, block, value):
    rows = value.shape[0] // 4
    for c in range(2):
        even = value[2 * c * rows : (2 * c + 1) * rows]
        uneven = value[(2 * c + 1) * rows : (2 * c + 2) * rows]
        keep_ref[c] = jnp.where(core == 0, even, uneven)
        send_ref[c] = jnp.where(core == 0, uneven, even).astype(BF16)


def back_kernel(
    conv_ref, b1_ref, s2_ref, grad_f_ref, grad_r_ref, small_ref, cx_ref, hf_ref, hr_ref,
    keep_ref, send_ref, gb_ref, g_ref,
):
    tower_back(
        lambda k: conv_ref[k], b1_ref[...], s2_ref[...], grad_f_ref[...], grad_r_ref[...],
        small_ref[5:6, 0:1], cx_ref.shape[0] - 2 * HALO, cx_ref, hf_ref, hr_ref, gb_ref, g_ref,
        functools.partial(share, lax.axis_index("core"), keep_ref, send_ref),
    )


def tower_kernel_plain(
    first_ref, p1_ref, conv_ref, p2_ref, small_ref, cx_ref, hf_ref, hr_ref,
    grad_ref, s1_ref, gb_ref, g_ref,
):
    def put(block, value):
        rows = value.shape[0]
        grad_ref[block * rows : (block + 1) * rows] = value

    cap, count = g_ref.shape[0] // 2, small_ref[5:6, 0:1]
    conv = lambda k: conv_ref[k]
    results = tower_front(
        first_ref[...], p1_ref[...], conv, p2_ref[...], count, small_ref[0:4], cap, cx_ref,
        hf_ref, hr_ref, s1_ref, put,
    )
    tower_back(conv, *results, count, cap, cx_ref, hf_ref, hr_ref, gb_ref, g_ref, put)


def fold(value):
    width = value.shape[1] // 2
    return jnp.concatenate([value[:, 0:width], value[:, width:]], axis=0)


def core_sum_kernel(keep1_ref, recv1_ref, keep2_ref, recv2_ref, own_ref, *outs):
    chip = 2 * lax.axis_index("y") + lax.axis_index("x")
    for n, out in enumerate((own_ref, *outs)):
        at, low = (chip ^ n) & 1, (chip ^ n) < 2
        total = jnp.where(
            low,
            keep1_ref[at] + recv1_ref[at].astype(F32),
            keep2_ref[at] + recv2_ref[at].astype(F32),
        )
        out[...] = total.astype(out.dtype)


def plane_sum_kernel(own_ref, d_ref, y_ref, x_ref, mine_ref, *refs):
    outs, sum_ref = refs[:-1], refs[-1]
    sum_ref[...] = (
        own_ref[...] + x_ref[...].astype(F32) + y_ref[...].astype(F32) + d_ref[...].astype(F32)
    )
    z = lax.axis_index("dp")
    rows = mine_ref.shape[0] // 2
    mine_ref[...] = fold(sum_ref[pl.ds(pl.multiple_of(z * rows, 8), rows), :])
    for n, out in enumerate(outs):
        at = pl.multiple_of((z ^ (n + 1)) * rows, 8)
        out[...] = fold(sum_ref[pl.ds(at, rows), :]).astype(BF16)


def last_sum_kernel(scale, mine_ref, *refs):
    out_ref = refs[-1]
    total = mine_ref[...]
    for ref in refs[:-1]:
        total = total + ref[...].astype(F32)
    total = total * scale
    rows, half = total.shape[0] // 2, total.shape[1] // 128
    for n in range(2 * half):
        at = rows * (n // half)
        lane = 128 * (n % half)
        out_ref[pl.ds(n, rows, stride=2 * half), :] = total[at : at + rows, lane : lane + 128]


def flip_move(array, *axes):
    sizes = [lax.axis_size(a) for a in axes]
    size = math.prod(sizes)
    return lax.ppermute(array, axes, [(i, size - 1 - i) for i in range(size)])


def xor_move(array, axis, bits):
    return lax.ppermute(array, axis, [(i, i ^ bits) for i in range(lax.axis_size(axis))])


def shift_move(array, by, axes):
    size = math.prod(lax.axis_size(a) for a in axes)
    return lax.ppermute(array, axes, [(i, i + by) for i in range(size) if 0 <= i + by < size])


def context_shapes(cap, chans):
    rows = cap + 2 * (HALO + SECOND_DILATION)
    return [((rows, TABLE), BF16), ((rows, TABLE), BF16), ((cap + 2 * HALO, chans), BF16)]


def pass_shapes(cap, chans, width):
    inner = cap + 2 * FIRST_DILATION
    return [((2 * TABLE, width), BF16), ((2 * inner, chans), BF16), ((2 * cap, chans), F32)]


def lines(embed, bases, lengths):
    cap, chans = bases.shape[1], embed.shape[1]
    row = lax.broadcasted_iota(jnp.int32, (8, chans), 0)
    line = jnp.pad(bases, ((0, 0), (0, chans - cap)))
    extra = jnp.where(row == 4, line, jnp.where(row == 5, lengths, 0)).astype(F32)
    return jnp.where(row < 4, jnp.pad(embed, ((0, 4), (0, 0))), extra)


def weight(flops):
    return pl.CostEstimate(flops=flops, bytes_accessed=10**6, transcendentals=0)


def fast_shards(
    bases, lengths, cotangent, c1, p1, c2, p2, embed
):
    cot = cotangent[0]
    cap, chans = cot.shape
    width = c1.shape[2]
    n_dp = lax.axis_size("dp")
    half = 3 * c2.shape[1] // 2
    narrow = jnp.concatenate([c1.reshape(-1, width), c2.reshape(-1, width)], axis=0)
    broad = jnp.concatenate([p2, p1], axis=0)
    own, to_x, to_y, to_d, small, cot = call(
        prep_kernel,
        [
            ((2 * half + HALO, chans), BF16),
            ((half + HALO, chans), BF16),
            ((half, chans), BF16),
            ((half + HALO, chans), BF16),
            ((8, chans), F32),
            ((cap, chans), BF16),
        ],
        [narrow, broad, cot, embed, bases, lengths],
    )
    plane = [flip_move(to_x, "x"), flip_move(to_y, "y"), flip_move(to_d, "y", "x")]
    other = [xor_move(a[:half], "dp", 1) for a in plane]
    across = lambda arrays: [flip_move(a, "core") for a in arrays]
    rows = chans // 8
    swapped = across([own, *plane])
    hf, hr, cx = call(
        context_kernel_packed,
        context_shapes(cap, chans),
        [own, *plane, *swapped, cot],
        scratch=[
            pltpu.VMEM((8 + 2 * REACH, 8, 256), F32),
            pltpu.VMEM((8, HALO, chans), BF16),
        ],
        cost=weight(10**9),
    )
    keep2, send2, s1, second, p1_full, conv, *middle = call(
        tower_kernel_packed,
        [((2, rows, chans), F32), ((2, rows, chans), BF16), ((2 * TABLE, width), BF16)]
        + [((48, width), F32), ((width, chans), BF16), ((3, chans, width), BF16)]
        + [((TABLE, width), BF16), ((2 * TABLE, chans), BF16)]
        + [((cap + 2 * HALO, width), BF16)] * 2,
        [
            own, swapped[0], *plane, *swapped[1:], *other, *across(other),
            small, cx, hf, hr,
        ],
        scratch=[
            pltpu.VMEM((width, chans), BF16),
            pltpu.VMEM((8, 16, width), F32),
            pltpu.VMEM((8, 24, chans), F32),
        ],
        limit=40,
        cost=weight(4 * 10**9),
    )
    recv2 = flip_move(send2, "core")
    keep1, send1, gb, g = call(
        back_kernel,
        [((2, rows, chans), F32), ((2, rows, chans), BF16)] + pass_shapes(cap, chans, width)[1:],
        [conv, *middle, small, cx, hf, hr],
        cost=weight(2 * 10**9),
    )
    recv1 = flip_move(send1, "core")
    (sal,) = call(
        saliency_kernel,
        [((4, cap), F32)],
        [small, hf, hr, s1, gb, g, second, p1_full],
        cost=weight(10**9),
    )
    own, *outs = call(
        core_sum_kernel,
        [((rows, chans), F32)] + [((rows, chans), BF16)] * 3,
        [keep1, recv1, keep2, recv2],
    )
    ways = (("x",), ("y",), ("y", "x"))
    got = [flip_move(outs[n], *ways[n]) for n in (2, 1, 0)]
    part = rows // n_dp
    mine, *outs = call(
        plane_sum_kernel,
        [((2 * part, width), F32)] + [((2 * part, width), BF16)] * (n_dp - 1),
        [own, *got],
        scratch=[pltpu.VMEM((rows, chans), F32)],
    )
    got = [xor_move(outs[n], "dp", n + 1) for n in reversed(range(n_dp - 1))]
    scale = 1.0 / math.sqrt(8 * n_dp * cap)
    (grad,) = call(
        functools.partial(last_sum_kernel, scale),
        [((part * chans // 128, 128), F32)],
        [mine, *got],
    )
    return sal[None], grad.reshape(-1)


def plain_shards(bases, lengths, cotangent, c1, p1, c2, p2, embed):
    cot = cotangent[0]
    cap, chans = cot.shape
    width = c1.shape[2]
    me, count = lax.axis_index("seq"), lengths[0, 0]
    shard = c1.shape[1]
    own = lax.dynamic_slice_in_dim(embed, me * shard, shard, 1)
    act, slope = gelu_pair(own)
    taps = c1.astype(F32)
    high = lax.Precision.HIGHEST
    first = jnp.einsum("qc,kcb->kqb", act.astype(BF16).astype(F32), taps, precision=high)
    second = jnp.einsum("qc,dc,kcb->kqdb", slope, own, taps, precision=high)
    first = lax.psum(first.reshape(12, width), "seq")
    second = lax.psum(second.reshape(48, width), "seq")
    first = jnp.concatenate([first, jnp.zeros((4, width), F32)], axis=0)
    p1_full = lax.all_gather(p1, "seq", axis=0, tiled=True)
    p2_full = lax.all_gather(p2, "seq", axis=0, tiled=True)
    conv = lax.all_gather(c2, "seq", axis=1, tiled=True)
    info = jnp.concatenate(
        [bases.astype(F32), jnp.broadcast_to(count.astype(F32), (1, 128))], axis=1
    )
    info = lax.all_gather(info, "seq", axis=0, tiled=True)
    info = jnp.pad(info, ((REACH, REACH), (0, 0)))
    info = lax.dynamic_slice_in_dim(info, me, 2 * REACH + 1, 0)
    info = jnp.broadcast_to(info[:, None, :], (2 * REACH + 1, 8, cap + 128))
    padded = jnp.pad(cot, ((HALO, 0), (0, 0)))
    last = lax.dynamic_slice_in_dim(padded, count, HALO, 0)
    halos = [
        shift_move(last, 1, ("seq",)),
        shift_move(last[HALO - SPILL :], 2, ("seq",)),
        shift_move(cot[:HALO], -1, ("seq",)),
        shift_move(cot[:SPILL], -2, ("seq",)),
    ]
    small = lines(embed, bases, lengths)
    hf, hr, cx = call(
        context_kernel_plain, context_shapes(cap, chans), [info, cot, *halos]
    )
    grad, s1, gb, g = call(
        tower_kernel_plain,
        [((2 * width, chans), F32), *pass_shapes(cap, chans, width)],
        [first, p1_full, conv, p2_full, small, cx, hf, hr],
        limit=40,
    )
    (sal,) = call(
        saliency_kernel,
        [((4, cap), F32)],
        [small, hf, hr, s1, gb, g, second, p1_full],
    )
    scale = 1.0 / math.sqrt(lax.axis_size("seq") * lax.axis_size("dp") * cap)
    grad = lax.psum_scatter(
        grad.reshape(-1) * scale, ("seq", "dp"), scatter_dimension=0, tiled=True
    )
    return sal[None], grad


def solution(mesh):
    run, seq = plain_shards, "seq"
    if mesh.shape["seq"] == 8 and mesh.shape["dp"] == 4:
        run, seq = fast_shards, ("y", "x", "core")
        count = mesh.shape["dp"]
        mesh = jax.sharding.Mesh(mesh.devices.reshape(2, 2, 2, count), (*seq, "dp"))
    every = seq if isinstance(seq, tuple) else (seq,)
    in_specs = (
        P("dp", seq),
        P("dp", seq),
        P("dp", seq, None),
        P(None, seq, None),
        P(seq, None),
        P(None, seq, None),
        P(seq, None),
        P(),
    )
    out_specs = (P("dp", None, seq), P((*every, "dp")))
    return jax.shard_map(run, mesh=mesh, in_specs=in_specs, out_specs=out_specs, check_vma=False)
```

```python
import functools
import math

import jax
import jax.numpy as jnp
from jax import lax
from jax.experimental import pallas as pl
from jax.experimental.pallas import tpu as pltpu
from jax.sharding import PartitionSpec as P

FIRST_DILATION = 16
SECOND_DILATION = 64
HALO = FIRST_DILATION + SECOND_DILATION
SPILL = 16
REACH = 3
TABLE = 128
SQRT_HALF = 0.7071067811865476
INV_SQRT_TWO_PI = 0.3989422804014327
F32 = jnp.float32
BF16 = jnp.bfloat16
FAR = -100000.0


def gelu_pair(v):
    half = 0.5 * (1.0 + lax.erf(v * SQRT_HALF))
    return v * half, half + v * jnp.exp(-0.5 * v * v) * INV_SQRT_TWO_PI


def split(v):
    high = v.astype(BF16)
    return high, (v - high.astype(F32)).astype(BF16)


def mm(a, b):
    return lax.dot_general(a, b, (((1,), (0,)), ((), ())), preferred_element_type=F32)


def mm_nt(a, b):
    return lax.dot_general(a, b, (((1,), (1,)), ((), ())), preferred_element_type=F32)


def mm_tn(a, b):
    return lax.dot_general(a, b, (((0,), (0,)), ((), ())), preferred_element_type=F32)


def iota(shape, dim):
    return lax.broadcasted_iota(jnp.int32, shape, dim)


def spread(rows, index):
    out = jnp.broadcast_to(rows[0:1], (index.shape[0], rows.shape[1]))
    for q in range(1, 4):
        out = jnp.where(index == q, rows[q : q + 1], out)
    return out


def call(body, out_shapes, args, scratch=(), limit=24, cost=None):
    in_specs = [
        pl.BlockSpec(memory_space=pltpu.VMEM) for _ in args
    ]
    return pl.pallas_call(
        body,
        out_shape=[jax.ShapeDtypeStruct(s, d) for s, d in out_shapes],
        in_specs=in_specs,
        out_specs=[pl.BlockSpec(memory_space=pltpu.VMEM)] * len(out_shapes),
        scratch_shapes=list(scratch),
        compiler_params=pltpu.CompilerParams(vmem_limit_bytes=limit * 1024 * 1024),
        cost_estimate=cost,
    )(*args)


def base_tables(emb, pick, conv):
    row = iota((16, 1), 0)
    low, high = row & 3, row >> 2
    by_low = spread(emb, low)
    by_high = spread(emb, high)
    act = gelu_pair(by_low)[0].astype(BF16)
    prod_high, prod_low = split(gelu_pair(by_high)[1] * by_low)
    own = mm(jnp.concatenate([act, prod_high, prod_low], axis=0), pick).astype(BF16)
    first = jnp.zeros((16, conv[0].shape[1]), F32)
    second = []
    for k in range(3):
        res = mm(own, conv[k])
        first = jnp.where(high == k, res[0:16], first)
        second.append(res[16:32] + res[32:48])
    return first, jnp.concatenate(second, axis=0)


def position():
    return (2 * lax.axis_index("y") + lax.axis_index("x")) * 2 + lax.axis_index("core")


def prep_kernel(
    narrow_ref, broad_ref, cot_ref, embed_ref, bases_ref, lengths_ref,
    own_ref, x_ref, y_ref, d_ref, small_ref, cot_out,
):
    me, odd = position(), lax.axis_index("dp") & 1
    cap = bases_ref.shape[1]
    count = jnp.broadcast_to(lengths_ref[...], (1, 128)).astype(F32)
    small_ref[0:4] = embed_ref[...]
    small_ref[4:5, 0:cap] = bases_ref[...].astype(F32)
    small_ref[5:6, 0:128] = count
    width = narrow_ref.shape[1]
    chans = 2 * width
    shard = narrow_ref.shape[0] // 6
    prows = width // 8
    half = 3 * shard // 2
    cut = half - 16
    flat = narrow_ref.at[3 * shard : 6 * shard]
    cot = cot_ref[...]
    cot_out[...] = cot
    pick = (iota((chans, shard), 0) == iota((chans, shard), 1) + me * shard).astype(BF16)
    taps = [narrow_ref[k * shard : (k + 1) * shard] for k in range(3)]
    first, second = base_tables(embed_ref[...], pick, taps)
    f_high, f_low = split(first)
    info = jnp.concatenate(
        [
            bases_ref[...].astype(F32),
            count,
            jnp.zeros((1, chans - cap - 128), F32),
        ],
        axis=1,
    )
    tail = jnp.concatenate([f_high.astype(F32), f_low.astype(F32)], axis=1)
    tail = jnp.where(iota((16, 1), 0) == 12, info, tail)
    wide = jnp.concatenate([second[0:24], second[24:48]], axis=1)
    extra = jnp.concatenate([info, jnp.zeros((7, chans), F32)], axis=0)
    own_ref[0:cut, 0:width] = flat[0:cut]
    own_ref[0:cut, width:chans] = flat[half : half + cut]
    own_ref[cut:half] = tail.astype(BF16)
    own_ref[half : half + 16, 0:width] = flat[cut:half]
    own_ref[half : half + 16, width:chans] = flat[half + cut : 2 * half]
    own_ref[half + 16 : half + 16 + 2 * prows] = broad_ref[0 : 2 * prows]
    own_ref[2 * half - 32 : 2 * half] = jnp.concatenate([wide, extra], axis=0).astype(BF16)
    part = own_ref[pl.ds(pl.multiple_of(odd * half, 16), half), :]
    for out in (x_ref, y_ref, d_ref):
        out[0:half] = part
    ahead = (iota((HALO, cap), 1) - iota((HALO, cap), 0) + HALO).astype(F32)
    take = (ahead == count).astype(BF16)
    last = mm(take, cot).astype(BF16)
    chip = me >> 1
    own_ref[2 * half :] = jnp.where((me & 1) == 0, last, cot[0:HALO])
    x_ref[half:] = jnp.where((chip ^ 1) > chip, last, cot[0:HALO])
    d_ref[half:] = jnp.where((chip ^ 3) > chip, last, cot[0:HALO])


def context_body(info_at, cot, r1, r2, l1, l2, hot_f_ref, hot_r_ref, cx_ref):
    cap = cot.shape[0]
    outer = HALO + SECOND_DILATION + FIRST_DILATION
    span = cap + 2 * outer
    counts = [info_at(o)[0:1, cap : cap + 128] for o in range(-REACH, REACH + 1)]
    begin = [None] * (2 * REACH + 1)
    begin[REACH] = jnp.zeros((1, 128), F32)
    for o in range(1, REACH + 1):
        begin[REACH + o] = begin[REACH + o - 1] + counts[REACH + o - 1]
        begin[REACH - o] = begin[REACH - o + 1] - counts[REACH - o]
    lane = iota((1, 128), 1).astype(F32)
    rowpos = (iota((span, 128), 0) - outer).astype(F32)
    total = jnp.zeros((span, 128), F32)
    for o in range(-REACH, REACH + 1):
        code = info_at(o)[0:1, 0:cap] + 1.0
        pos = jnp.where(lane < counts[REACH + o], begin[REACH + o] + lane, FAR)
        total = total + jnp.where(rowpos == pos, code, 0.0)
    codes = jnp.sum(total, axis=1, keepdims=True)
    d = FIRST_DILATION
    left, mid, right = codes[0 : span - 2 * d], codes[d : span - d], codes[2 * d : span]
    rows = span - 2 * d
    lanes = iota((rows, TABLE), 1).astype(F32)
    flip = lambda c: jnp.where(c == 0.0, 0.0, 5.0 - c)
    idx = jnp.where(mid == 0.0, -1.0, (mid - 1.0) * 25.0 + left * 5.0 + right)
    hot_f_ref[...] = (lanes == idx).astype(BF16)
    idx = jnp.where(mid == 0.0, -1.0, (4.0 - mid) * 25.0 + flip(right) * 5.0 + flip(left))
    hot_r_ref[...] = (lanes == idx).astype(BF16)

    own_n = counts[REACH]
    before_n, after_n = counts[REACH - 1], counts[REACH + 1]
    grow = cap + 2 * HALO
    lane_h = iota((1, HALO), 1).astype(F32)
    lane_s = iota((1, SPILL), 1).astype(F32)
    row_h = (iota((grow, HALO), 0) - HALO).astype(F32)
    row_s = (iota((grow, SPILL), 0) - HALO).astype(F32)
    row_o = (iota((grow, cap), 0) - HALO).astype(F32)
    own_pos = jnp.where(lane < own_n, lane, FAR)
    acc = mm((row_o == own_pos).astype(BF16), cot)
    pos = jnp.where(lane_h >= HALO - before_n[:, 0:HALO], lane_h - HALO, FAR)
    acc = acc + mm((row_h == pos).astype(BF16), r1)
    pos = jnp.where(
        counts[REACH - 2][:, 0:SPILL] > 0.0, lane_s - SPILL - before_n[:, 0:SPILL], FAR
    )
    acc = acc + mm((row_s == pos).astype(BF16), r2)
    pos = jnp.where(lane_h < after_n[:, 0:HALO], lane_h + own_n[:, 0:HALO], FAR)
    acc = acc + mm((row_h == pos).astype(BF16), l1)
    pos = jnp.where(
        (counts[REACH + 2][:, 0:SPILL] > 0.0) & (after_n[:, 0:SPILL] < HALO),
        lane_s + own_n[:, 0:SPILL] + after_n[:, 0:SPILL],
        FAR,
    )
    acc = acc + mm((row_s == pos).astype(BF16), l2)
    cx_ref[...] = (0.5 * acc).astype(BF16)


def context_kernel_plain(info_ref, cot_ref, r1_ref, r2_ref, l1_ref, l2_ref, *outs):
    context_body(
        lambda o: info_ref[REACH + o], cot_ref[...], r1_ref[...], r2_ref[...], l1_ref[...],
        l2_ref[...], *outs,
    )


def context_kernel_packed(*refs):
    parts, cot_ref, outs = refs[0:8], refs[8], refs[9:12]
    info_ref, halo_ref = refs[12:]
    me, odd = position(), lax.axis_index("dp") & 1
    chip, core = me >> 1, me & 1
    half = 3 * cot_ref.shape[1] // 16
    info_ref[0:REACH] = jnp.zeros((REACH, 8, 256), F32)
    info_ref[REACH + 8 :] = jnp.zeros((REACH, 8, 256), F32)
    for n, part in enumerate(parts):
        peer = me ^ (2 * (-n % 4) + n // 4)
        low = part[half - 16 : half].astype(F32)[12:13, 0:256]
        if n % 4 > 0:
            high = part[half - 16 : half].astype(F32)[8:9, 0:256]
            low = jnp.where(odd == 0, low, high)
        info_ref[REACH + peer] = jnp.broadcast_to(low, (8, 256))
    for n in range(2):
        halo_ref[4 * n + chip] = parts[4 * n][2 * half :]
        halo_ref[4 * n + (chip ^ 3)] = parts[4 * n + 1][half:]
        halo_ref[4 * n + (chip ^ 1)] = parts[4 * n + 3][half:]
    r1 = halo_ref[4 + jnp.maximum(chip + core - 1, 0)]
    l1 = halo_ref[4 + jnp.minimum(chip + core, 3)]
    r2 = halo_ref[jnp.maximum(chip - 1, 0)]
    l2 = halo_ref[jnp.minimum(chip + 1, 3)]
    context_body(
        lambda o: info_ref[me + (REACH + o)], cot_ref[...], r1, r2[HALO - SPILL :], l1,
        l2[0:SPILL], *outs,
    )


def tower_body(
    first, project, conv, p2, count, emb, cap, cx_ref, hot_f_ref, hot_r_ref,
    s1_ref, gb_ref, g_ref, put,
):
    entry = iota((TABLE, 1), 0)
    by25 = (entry * 1311) >> 15
    by5 = (entry * 6554) >> 15
    in_left = by5 - 5 * by25
    in_right = entry - 5 * by5
    sums = jnp.zeros((TABLE, first.shape[1]), F32)
    for q in range(4):
        sums = jnp.where(in_left == q + 1, first[q : q + 1], sums)
    sums = sums + spread(first[4:8], by25)
    after = jnp.zeros((TABLE, first.shape[1]), F32)
    for q in range(4):
        after = jnp.where(in_right == q + 1, first[8 + q : 9 + q], after)
    value, slope = gelu_pair(sums + after)
    b1 = value.astype(BF16)
    high, low = split(slope)
    s1_ref[0:TABLE] = high
    s1_ref[TABLE : 2 * TABLE] = low
    stream = spread(emb, by25) + mm(b1, project)
    value, slope = gelu_pair(stream)
    a2 = value.astype(BF16)
    s2 = jnp.concatenate(split(slope), axis=0)

    grow = cap + 2 * HALO
    inner = cap + 2 * FIRST_DILATION
    d, D = FIRST_DILATION, SECOND_DILATION
    cx = cx_ref[...]
    back_mid = mm_nt(cx, p2)
    before = jnp.zeros((2 * grow, p2.shape[0]), F32)
    for k in range(3):
        taps = jnp.concatenate(split(mm(a2, conv(k))), axis=0)
        hot = jnp.concatenate(
            [hot_f_ref[k * D : k * D + grow], hot_r_ref[(2 - k) * D : (2 - k) * D + grow]], axis=0
        )
        before = before + mm(jnp.concatenate([hot, hot], axis=1), taps)
    value, slope = gelu_pair(before)
    own_col = (iota((cap, 1), 0).astype(F32) < count).astype(F32)
    own_gb = (cx[HALO : HALO + cap].astype(F32) * own_col).astype(BF16)
    mids = jnp.concatenate(
        [value[HALO : HALO + cap], value[grow + HALO : grow + HALO + cap]], axis=0
    ).astype(BF16)
    put(1, mm_tn(mids, jnp.concatenate([own_gb, own_gb], axis=0)))
    grad_f = (back_mid * slope[0:grow]).astype(BF16)
    grad_r = (back_mid * slope[grow:]).astype(BF16)
    ga = jnp.zeros((2 * inner, cx.shape[1]), F32)
    for k in range(3):
        rows = jnp.concatenate(
            [grad_f[(2 - k) * D : (2 - k) * D + inner], grad_r[k * D : k * D + inner]], axis=0
        )
        ga = ga + mm_nt(rows, conv(k))
    hot = jnp.concatenate(
        [hot_f_ref[2 * D : 2 * D + inner], hot_r_ref[2 * D : 2 * D + inner]], axis=0
    )
    base_g = cx[D : D + inner].astype(F32)
    g = jnp.concatenate([base_g, base_g], axis=0) + ga * mm(
        jnp.concatenate([hot, hot], axis=1), s2
    )
    gb = g.astype(BF16)
    gb_ref[...] = gb
    g_ref[0:cap] = g[d : d + cap]
    g_ref[cap : 2 * cap] = g[inner + d : inner + d + cap]
    col = jnp.concatenate([own_col, own_col], axis=0)
    own_hot = jnp.concatenate([hot[d : d + cap], hot[inner + d : inner + d + cap]], axis=0)
    own_b1 = mm((own_hot.astype(F32) * col).astype(BF16), b1).astype(BF16)
    own_g = jnp.concatenate([gb[d : d + cap], gb[inner + d : inner + d + cap]], axis=0)
    put(0, mm_tn(own_b1, own_g))


def saliency_kernel(
    small_ref, hot_f_ref, hot_r_ref, s1_ref, gb_ref, g_ref, second_ref, p1_ref, sal_ref
):
    cap = g_ref.shape[0] // 2
    inner = cap + 2 * FIRST_DILATION
    d, D = FIRST_DILATION, SECOND_DILATION
    hot = jnp.concatenate(
        [hot_f_ref[2 * D : 2 * D + inner], hot_r_ref[2 * D : 2 * D + inner]], axis=0
    )
    slope = mm(jnp.concatenate([hot, hot], axis=1), s1_ref[...])
    gh = (mm_nt(gb_ref[...], p1_ref[...]) * slope).astype(BF16)
    emb = small_ref[0:4]
    bases = small_ref[4:5, 0:cap]
    wide = jnp.concatenate(split(second_ref[...]), axis=0)
    total = jnp.zeros((4, cap), F32)
    e_high, e_low = split(jnp.concatenate([emb, emb], axis=0))
    for turn in range(2):
        g_high, g_low = split(g_ref[turn * cap : (turn + 1) * cap])
        got = mm_nt(e_high, g_high) + mm_nt(e_high, g_low) + mm_nt(e_low, g_high)
        got = got[0:4]
        table = jnp.zeros((16, cap), F32)
        for k in range(3):
            place = 2 - k if turn == 0 else k
            at = turn * inner + place * d
            both = mm_nt(
                jnp.concatenate(
                    [wide[16 * k : 16 * k + 16], wide[48 + 16 * k : 64 + 16 * k]], axis=0
                ),
                gh[at : at + cap],
            )
            table = table + both[0:16] + both[16:32]
        for q in range(4):
            code = float(q if turn == 0 else 3 - q)
            got = got + jnp.where(bases == code, table[4 * q : 4 * q + 4], 0.0)
        if turn == 1:
            got = jnp.concatenate([got[3 - c : 4 - c] for c in range(4)], axis=0)
        total = total + got
    live = iota((1, cap), 1).astype(F32) < small_ref[5:6, 0:cap]
    sal_ref[...] = jnp.where(live, total * (1.0 / math.sqrt(emb.shape[1])), 0.0)


def tower_kernel_packed(*refs):
    own_parts, plane_parts, dp_parts = refs[0:2], refs[2:8], refs[8:14]
    small_ref, cx_ref, hf_ref, hr_ref = refs[14:18]
    keep_ref, send_ref, s1_ref, gb_ref, g_ref, wide_ref, p1_ref = refs[18:25]
    conv_ref, p2_ref, first_ref, second_ref = refs[25:]
    me = position()
    core, odd = me & 1, lax.axis_index("dp") & 1
    count = small_ref[5:6, 0:1]
    width, chans = p1_ref.shape
    shard = chans // 8
    prow = width // 8
    half = 3 * shard // 2
    cut = half - 16

    def place(side, rows, peer):
        at = peer * shard

        def lay(k, start, size, source, lane):
            conv_ref[k, pl.ds(pl.multiple_of(at + start, 16), size), :] = rows(
                source, size
            )[:, lane : lane + width]

        if side == 0:
            lay(0, 0, shard, 0, 0)
            lay(1, 0, cut - shard, shard, 0)
            lay(1, shard // 2, shard // 2, 0, width)
            lay(2, 0, cut - shard // 2, shard // 2, width)
            tail = rows(cut, 16).astype(F32)
            first_ref[peer] = tail[:, 0:width] + tail[:, width:]
        else:
            lay(1, cut - shard, 16, 0, 0)
            lay(2, shard - 16, 16, 0, width)
            to = pl.ds(pl.multiple_of(peer * prow, 16), prow)
            p2_ref[to, :] = rows(16, prow)
            p1_ref[to, :] = rows(16 + prow, prow)
            second_ref[peer] = rows(half - 32, 32).astype(F32)[0:24]

    for n in range(2):
        for side in range(2):
            rows = lambda a, size, n=n, side=side: own_parts[n][
                side * half + a : side * half + a + size
            ]
            place(side, rows, me ^ n)
    for parity in range(2):

        @pl.when(odd == parity)
        def _():
            for n in range(6):
                peer = me ^ (2 * (3 - n % 3) + n // 3)
                for side, part in ((parity, plane_parts[n]), (1 - parity, dp_parts[n])):
                    rows = lambda a, size, part=part: part[a : a + size]
                    place(side, rows, peer)

    first = first_ref[0]
    wide = second_ref[0]
    for peer in range(1, 8):
        first = first + first_ref[peer]
        wide = wide + second_ref[peer]
    wide_ref[...] = jnp.concatenate([wide[:, 0:width], wide[:, width : 2 * width]], axis=0)

    def put(block, value):
        rows = value.shape[0] // 4
        for c in range(2):
            even = value[2 * c * rows : (2 * c + 1) * rows]
            uneven = value[(2 * c + 1) * rows : (2 * c + 2) * rows]
            keep_ref[2 * block + c] = jnp.where(core == 0, even, uneven)
            send_ref[2 * block + c] = jnp.where(core == 0, uneven, even).astype(BF16)

    tower_body(
        first, p1_ref[...], lambda k: conv_ref[k], p2_ref[...], count, small_ref[0:4],
        g_ref.shape[0] // 2, cx_ref, hf_ref, hr_ref, s1_ref, gb_ref, g_ref, put,
    )


def tower_kernel_plain(
    first_ref, p1_ref, conv_ref, p2_ref, small_ref, cx_ref, hf_ref, hr_ref,
    grad_ref, s1_ref, gb_ref, g_ref,
):
    def put(block, value):
        rows = value.shape[0]
        grad_ref[block * rows : (block + 1) * rows] = value

    tower_body(
        first_ref[...], p1_ref[...], lambda k: conv_ref[k], p2_ref[...], small_ref[5:6, 0:1],
        small_ref[0:4], g_ref.shape[0] // 2, cx_ref, hf_ref, hr_ref, s1_ref, gb_ref, g_ref, put,
    )


def fold(value):
    width = value.shape[1] // 2
    return jnp.concatenate([value[:, 0:width], value[:, width:]], axis=0)


def core_sum_kernel(keep_ref, recv_ref, own_ref, *outs):
    chip = 2 * lax.axis_index("y") + lax.axis_index("x")
    own_ref[...] = keep_ref[chip] + recv_ref[chip].astype(F32)
    for n, out in enumerate(outs):
        at = chip ^ (n + 1)
        out[...] = (keep_ref[at] + recv_ref[at].astype(F32)).astype(BF16)


def plane_sum_kernel(own_ref, d_ref, y_ref, x_ref, mine_ref, *refs):
    outs, sum_ref = refs[:-1], refs[-1]
    sum_ref[...] = (
        own_ref[...] + x_ref[...].astype(F32) + y_ref[...].astype(F32) + d_ref[...].astype(F32)
    )
    z = lax.axis_index("dp")
    rows = mine_ref.shape[0] // 2
    mine_ref[...] = fold(sum_ref[pl.ds(pl.multiple_of(z * rows, 8), rows), :])
    for n, out in enumerate(outs):
        at = pl.multiple_of((z ^ (n + 1)) * rows, 8)
        out[...] = fold(sum_ref[pl.ds(at, rows), :]).astype(BF16)


def last_sum_kernel(scale, mine_ref, *refs):
    out_ref = refs[-1]
    total = mine_ref[...]
    for ref in refs[:-1]:
        total = total + ref[...].astype(F32)
    total = total * scale
    rows, half = total.shape[0] // 2, total.shape[1] // 128
    for n in range(2 * half):
        at = rows * (n // half)
        lane = 128 * (n % half)
        out_ref[pl.ds(n, rows, stride=2 * half), :] = total[at : at + rows, lane : lane + 128]


def flip_move(array, *axes):
    sizes = [lax.axis_size(a) for a in axes]
    size = math.prod(sizes)
    return lax.ppermute(array, axes, [(i, size - 1 - i) for i in range(size)])


def xor_move(array, axis, bits):
    return lax.ppermute(array, axis, [(i, i ^ bits) for i in range(lax.axis_size(axis))])


def shift_move(array, by, axes):
    size = math.prod(lax.axis_size(a) for a in axes)
    return lax.ppermute(array, axes, [(i, i + by) for i in range(size) if 0 <= i + by < size])


def context_shapes(cap, chans):
    rows = cap + 2 * (HALO + SECOND_DILATION)
    return [((rows, TABLE), BF16), ((rows, TABLE), BF16), ((cap + 2 * HALO, chans), BF16)]


def pass_shapes(cap, chans, width):
    inner = cap + 2 * FIRST_DILATION
    return [((2 * TABLE, width), BF16), ((2 * inner, chans), BF16), ((2 * cap, chans), F32)]


def lines(embed, bases, lengths):
    cap, chans = bases.shape[1], embed.shape[1]
    row = lax.broadcasted_iota(jnp.int32, (8, chans), 0)
    line = jnp.pad(bases, ((0, 0), (0, chans - cap)))
    extra = jnp.where(row == 4, line, jnp.where(row == 5, lengths, 0)).astype(F32)
    return jnp.where(row < 4, jnp.pad(embed, ((0, 4), (0, 0))), extra)


def weight(flops):
    return pl.CostEstimate(flops=flops, bytes_accessed=10**6, transcendentals=0)


def fast_shards(
    bases, lengths, cotangent, c1, p1, c2, p2, embed
):
    cot = cotangent[0]
    cap, chans = cot.shape
    width = c1.shape[2]
    n_dp = lax.axis_size("dp")
    half = 3 * c2.shape[1] // 2
    narrow = jnp.concatenate([c1.reshape(-1, width), c2.reshape(-1, width)], axis=0)
    broad = jnp.concatenate([p2, p1], axis=0)
    own, to_x, to_y, to_d, small, cot = call(
        prep_kernel,
        [
            ((2 * half + HALO, chans), BF16),
            ((half + HALO, chans), BF16),
            ((half, chans), BF16),
            ((half + HALO, chans), BF16),
            ((8, chans), F32),
            ((cap, chans), BF16),
        ],
        [narrow, broad, cot, embed, bases, lengths],
    )
    plane = [flip_move(to_d, "y", "x"), flip_move(to_y, "y"), flip_move(to_x, "x")]
    other = [xor_move(a[:half], "dp", 1) for a in plane]
    across = lambda arrays: [flip_move(a, "core") for a in arrays]
    rows = chans // 8
    swapped = across([own, *plane])
    hf, hr, cx = call(
        context_kernel_packed,
        context_shapes(cap, chans),
        [own, *plane, *swapped, cot],
        scratch=[
            pltpu.VMEM((8 + 2 * REACH, 8, 256), F32),
            pltpu.VMEM((8, HALO, chans), BF16),
        ],
        cost=weight(10**9),
    )
    keep, send, s1, gb, g, second, p1_full = call(
        tower_kernel_packed,
        [((4, rows, chans), F32), ((4, rows, chans), BF16), *pass_shapes(cap, chans, width)]
        + [((48, width), F32), ((width, chans), BF16)],
        [
            own, swapped[0], *plane, *swapped[1:], *other, *across(other),
            small, cx, hf, hr,
        ],
        scratch=[
            pltpu.VMEM((3, chans, width), BF16),
            pltpu.VMEM((width, chans), BF16),
            pltpu.VMEM((8, 16, width), F32),
            pltpu.VMEM((8, 24, chans), F32),
        ],
        limit=40,
        cost=weight(4 * 10**9),
    )
    recv = flip_move(send, "core")
    (sal,) = call(
        saliency_kernel,
        [((4, cap), F32)],
        [small, hf, hr, s1, gb, g, second, p1_full],
        cost=weight(10**9),
    )
    own, *outs = call(
        core_sum_kernel,
        [((rows, chans), F32)] + [((rows, chans), BF16)] * 3,
        [keep, recv],
    )
    ways = (("x",), ("y",), ("y", "x"))
    got = [flip_move(outs[n], *ways[n]) for n in (2, 1, 0)]
    part = rows // n_dp
    mine, *outs = call(
        plane_sum_kernel,
        [((2 * part, width), F32)] + [((2 * part, width), BF16)] * (n_dp - 1),
        [own, *got],
        scratch=[pltpu.VMEM((rows, chans), F32)],
    )
    got = [xor_move(outs[n], "dp", n + 1) for n in reversed(range(n_dp - 1))]
    scale = 1.0 / math.sqrt(8 * n_dp * cap)
    (grad,) = call(
        functools.partial(last_sum_kernel, scale),
        [((part * chans // 128, 128), F32)],
        [mine, *got],
    )
    return sal[None], grad.reshape(-1)


def plain_shards(bases, lengths, cotangent, c1, p1, c2, p2, embed):
    cot = cotangent[0]
    cap, chans = cot.shape
    width = c1.shape[2]
    me, count = lax.axis_index("seq"), lengths[0, 0]
    shard = c1.shape[1]
    own = lax.dynamic_slice_in_dim(embed, me * shard, shard, 1)
    act, slope = gelu_pair(own)
    taps = c1.astype(F32)
    high = lax.Precision.HIGHEST
    first = jnp.einsum("qc,kcb->kqb", act.astype(BF16).astype(F32), taps, precision=high)
    second = jnp.einsum("qc,dc,kcb->kqdb", slope, own, taps, precision=high)
    first = lax.psum(first.reshape(12, width), "seq")
    second = lax.psum(second.reshape(48, width), "seq")
    first = jnp.concatenate([first, jnp.zeros((4, width), F32)], axis=0)
    p1_full = lax.all_gather(p1, "seq", axis=0, tiled=True)
    p2_full = lax.all_gather(p2, "seq", axis=0, tiled=True)
    conv = lax.all_gather(c2, "seq", axis=1, tiled=True)
    info = jnp.concatenate(
        [bases.astype(F32), jnp.broadcast_to(count.astype(F32), (1, 128))], axis=1
    )
    info = lax.all_gather(info, "seq", axis=0, tiled=True)
    info = jnp.pad(info, ((REACH, REACH), (0, 0)))
    info = lax.dynamic_slice_in_dim(info, me, 2 * REACH + 1, 0)
    info = jnp.broadcast_to(info[:, None, :], (2 * REACH + 1, 8, cap + 128))
    padded = jnp.pad(cot, ((HALO, 0), (0, 0)))
    last = lax.dynamic_slice_in_dim(padded, count, HALO, 0)
    halos = [
        shift_move(last, 1, ("seq",)),
        shift_move(last[HALO - SPILL :], 2, ("seq",)),
        shift_move(cot[:HALO], -1, ("seq",)),
        shift_move(cot[:SPILL], -2, ("seq",)),
    ]
    small = lines(embed, bases, lengths)
    hf, hr, cx = call(
        context_kernel_plain, context_shapes(cap, chans), [info, cot, *halos]
    )
    grad, s1, gb, g = call(
        tower_kernel_plain,
        [((2 * width, chans), F32), *pass_shapes(cap, chans, width)],
        [first, p1_full, conv, p2_full, small, cx, hf, hr],
        limit=40,
    )
    (sal,) = call(
        saliency_kernel,
        [((4, cap), F32)],
        [small, hf, hr, s1, gb, g, second, p1_full],
    )
    scale = 1.0 / math.sqrt(lax.axis_size("seq") * lax.axis_size("dp") * cap)
    grad = lax.psum_scatter(
        grad.reshape(-1) * scale, ("seq", "dp"), scatter_dimension=0, tiled=True
    )
    return sal[None], grad


def solution(mesh):
    run, seq = plain_shards, "seq"
    if mesh.shape["seq"] == 8 and mesh.shape["dp"] == 4:
        run, seq = fast_shards, ("y", "x", "core")
        count = mesh.shape["dp"]
        mesh = jax.sharding.Mesh(mesh.devices.reshape(2, 2, 2, count), (*seq, "dp"))
    every = seq if isinstance(seq, tuple) else (seq,)
    in_specs = (
        P("dp", seq),
        P("dp", seq),
        P("dp", seq, None),
        P(None, seq, None),
        P(seq, None),
        P(None, seq, None),
        P(seq, None),
        P(),
    )
    out_specs = (P("dp", None, seq), P((*every, "dp")))
    return jax.shard_map(run, mesh=mesh, in_specs=in_specs, out_specs=out_specs, check_vma=False)
```
